256 devices in a mesh: dp: 4 (over y_lo, core), space: 64 (over x, z, y_hi).
Axes of the slice: x: 4, y: 4 (y_hi: 2, y_lo: 2; y = y_hi * 2 + y_lo), z: 8, core: 2. Of those that a mesh axis runs over, the one named last changes fastest.
Arguments:
- inputs: bfloat16 [4, 128, 512, 256], P('dp', 'space'), may hold values from -4 to 4
- cotangent: bfloat16 [4, 128, 512, 256], P('dp', 'space'), may hold values from -1.2 to 1.2
- occupancy: int32 [4, 128, 512], P('dp', 'space'), may hold values 0 or 1
- neighbours: int32 [4, 128, 27], P('dp', 'space'), may hold values from -1 to 1, as said below
- weight: bfloat16 [27, 256, 256], replicated, may hold values from -0.375 to 0.375
- error_in: bfloat16 [4, 64, 6912, 256], P('dp', 'space'), may hold values from -24 to 24
- q_start: float32 [256, 32], replicated, may hold values from -0.375 to 0.375
Outputs:
- input_grad: bfloat16 [4, 128, 512, 256], P('dp', 'space')
- q_factor: float32 [256, 32], replicated
- new_error: bfloat16 [4, 64, 6912, 256], P('dp', 'space')
The draws below stay inside these ranges and needn't reach their ends.
Inputs may be any that keep to these rules, and one draw needn't show every extreme that they name: `neighbours`: an entry that is not -1 names a slot 0 to 1 of a brick in the slab whose space index differs by the direction's third component e, on the same dp index; the entry of direction 13 is the brick's own slot; two entries of a brick in different directions never name the same brick.
All inputs are finite; a program needn't handle non-finite values. No bound on the sum of `occupancy` on one device may be relied on, other than what follows from the above.
Results may differ from the reference program's by a relative error of at most 0.00045.
Values may be sent and summed in bfloat16 or wider, within the bound.
No kernel may reach another device: no remote copies, remote signals or barrier semaphores. Data moves between devices by JAX's collectives and lax.ppermute only.
A program may use at most 128 MiB of HBM per device.

```python
import jax
import jax.numpy as jnp
import numpy as np
from jax import lax

CI = 256
CO = 256
RANK = 32
EDGE = 8
BRICK_DEV = 2
VOXELS = 512
KROWS = 6912
SHAPES = 4
SLABS = 64
BRICKS = 128
N_DP = 4
N_SPACE = 64


def shared_voxels(key):
    first_key = jax.random.fold_in(key, 0)
    full_shape = (SHAPES, BRICKS, VOXELS, CI)
    normal_values = jax.random.normal(first_key, full_shape, jnp.float32)
    return normal_values


def draw_inputs(key, part):
    normal_values = shared_voxels(key)
    return jnp.clip(normal_values, -4.0, 4.0).astype(jnp.bfloat16)


def draw_cotangent(key, part):
    normal_values = shared_voxels(key)
    key = jax.random.fold_in(key, 5)
    out_shape = (SHAPES, BRICKS, VOXELS, CO)
    own_normal = jax.random.normal(key, out_shape, jnp.float32)
    return (0.25 * (0.1 * jnp.clip(normal_values, -4.0, 4.0)[..., :CO] + jnp.clip(own_normal, -4.0, 4.0))).astype(jnp.bfloat16)


def draw_neighbours(key, part):
    key = jax.random.fold_in(key, 11)
    slab_count = BRICKS // BRICK_DEV
    slab_keys = jax.random.split(key, SHAPES * slab_count)
    chosen_cells = jax.vmap(lambda slab_key: jax.random.permutation(slab_key, 2 * BRICK_DEV)[:BRICK_DEV])(slab_keys)
    chosen_cells = chosen_cells.reshape(SHAPES, slab_count, BRICK_DEV).astype(jnp.int32)
    cell_x = chosen_cells // 2
    cell_y = chosen_cells % 2
    step_table = np.array([(step_x, step_y, step_z) for step_x in (-1, 0, 1) for step_y in (-1, 0, 1) for step_z in (-1, 0, 1)], dtype=np.int32)
    step_x = jnp.asarray(step_table[:, 0])
    step_y = jnp.asarray(step_table[:, 1])
    step_z = jnp.asarray(step_table[:, 2])
    target_slab = jnp.arange(slab_count, dtype=jnp.int32)[:, None] + step_z[None, :]
    inside = (target_slab >= 0) & (target_slab < slab_count)
    clipped_slab = jnp.clip(target_slab, 0, slab_count - 1)
    target_x = cell_x[..., None] + step_x
    target_y = cell_y[..., None] + step_y
    candidate_x = jnp.take(cell_x, clipped_slab, axis=1)
    candidate_y = jnp.take(cell_y, clipped_slab, axis=1)
    matches = (candidate_x[:, :, None, :, :] == target_x[..., None]) & (candidate_y[:, :, None, :, :] == target_y[..., None])
    found = jnp.any(matches, axis=-1) & inside[None, :, None, :]
    slot_numbers = jnp.arange(BRICK_DEV, dtype=jnp.int32)
    slot_index = jnp.sum(jnp.where(matches, slot_numbers, 0), axis=-1)
    result = jnp.where(found, slot_index, -1)
    return result.reshape(SHAPES, BRICKS, 27).astype(jnp.int32)


def touch_ends(values, rng, low, top_value):
    longest = values.shape.index(max(values.shape))
    spots = []
    for shift in (0, 1):
        where = [jax.random.randint(jax.random.fold_in(rng, axis), (), 0, length) for axis, length in enumerate(values.shape)]
        where[longest] = (where[longest] + shift) % values.shape[longest]
        spots.append(tuple(where))
    return values.at[spots[0]].set(low).at[spots[1]].set(top_value)


def levels(key, dims, shards, smallest, largest):
    def one(dim, parts):
        heights = jax.random.uniform(jax.random.fold_in(jax.random.fold_in(key, 6), dim), (parts,), jnp.float32, smallest / len(shards), largest / len(shards))
        return jnp.repeat(jnp.exp(heights), dims[dim] // parts).reshape((-1,) + (1,) * (len(dims) - dim - 1))

    gain = one(*shards[0])
    for cut in shards[1:]:
        gain = gain * one(*cut)
    return gain


def centred(key, shape, deviation, bound, shards=(), kind=jnp.bfloat16):
    factor_of = levels(key, shape, shards, -0.22, 0.18) if shards else 1.0
    drawn = jax.random.normal(key, shape, jnp.float32) * deviation * factor_of
    return jnp.minimum(jnp.maximum(drawn, -bound), bound).astype(kind)


def setup_inputs(seed: int = 0) -> dict:
    key_of = jax.random.split(jax.random.key(seed), 8)
    inputs = draw_inputs(jax.random.fold_in(key_of[7], 71), 0)
    cotangent = draw_cotangent(jax.random.fold_in(key_of[7], 71), 0)
    occupancy = touch_ends((jax.random.randint(key_of[2], (SHAPES, BRICKS, VOXELS), 0, 2) < 1).astype(jnp.int32), jax.random.fold_in(key_of[2], 1), 0, 1)
    neighbours = draw_neighbours(jax.random.fold_in(key_of[7], 71), 0)
    weight = centred(key_of[4], (27, CI, CO), CO ** -0.5, 0.375)
    error_in = centred(key_of[5], (SHAPES, SLABS, KROWS, CO), 4.0, 24.0, ((0, 4), (1, 64)))
    q_start = centred(key_of[6], (CO, RANK), CO ** -0.5, 0.375, (), jnp.float32)
    return {"inputs": inputs, "cotangent": cotangent, "occupancy": occupancy, "neighbours": neighbours, "weight": weight, "error_in": error_in, "q_start": q_start}


def pick_edge(source_block, dim_index, step):
    extent = source_block.shape[dim_index]
    if step < 0:
        return lax.slice_in_dim(source_block, extent - 1, extent, axis=dim_index)
    if step > 0:
        return lax.slice_in_dim(source_block, 0, 1, axis=dim_index)
    return source_block

def neighbourhood(own_bricks, lower_bricks, upper_bricks, neighbour_slots):
    sources = (lower_bricks, own_bricks, upper_bricks)
    x_pieces = []
    for step_x in (-1, 0, 1):
        y_pieces = []
        for step_y in (-1, 0, 1):
            z_pieces = []
            for step_z in (-1, 0, 1):
                source_block = pick_edge(sources[step_z + 1], 1, step_x)
                source_block = pick_edge(source_block, 2, step_y)
                source_block = pick_edge(source_block, 3, step_z)
                slot_index = neighbour_slots[:, (step_x + 1) * 9 + (step_y + 1) * 3 + (step_z + 1)]
                gathered = jnp.take(source_block, jnp.maximum(slot_index, 0), axis=0)
                valid = (slot_index >= 0)[:, None, None, None, None]
                z_pieces.append(jnp.where(valid, gathered, jnp.zeros_like(gathered)))
            y_pieces.append(jnp.concatenate(z_pieces, axis=3))
        x_pieces.append(jnp.concatenate(y_pieces, axis=2))
    return jnp.concatenate(x_pieces, axis=1)

def tap_views(padded, direction_sign):
    views = []
    for step_x in (-1, 0, 1):
        for step_y in (-1, 0, 1):
            for step_z in (-1, 0, 1):
                start_x = 1 + direction_sign * step_x
                start_y = 1 + direction_sign * step_y
                start_z = 1 + direction_sign * step_z
                views.append(padded[:, start_x:start_x + EDGE, start_y:start_y + EDGE, start_z:start_z + EDGE, :])
    return jnp.stack(views, axis=4)

def brick_backward(padded_inputs, padded_cotangent, occupied_cotangent, occupied, weight):
    voxel_rows = occupied.shape[0] * occupied.shape[1]
    input_columns = tap_views(padded_inputs, 1).reshape(voxel_rows, -1)
    local_gradient = lax.dot_general(input_columns.astype(jnp.float32), occupied_cotangent.reshape(voxel_rows, -1).astype(jnp.float32), (((0,), (0,)), ((), ())), preferred_element_type=jnp.float32)
    grad_columns = tap_views(padded_cotangent, -1).reshape(voxel_rows, 27, -1)
    summed = lax.dot_general(grad_columns.astype(jnp.float32), weight.astype(jnp.float32), (((1, 2), (0, 2)), ((), ())), preferred_element_type=jnp.float32)
    input_grad = (summed * occupied.reshape(voxel_rows, 1)).astype(jnp.bfloat16)
    return (local_gradient, input_grad)

def orthonormal(p_matrix):
    gram_matrix = jnp.dot(p_matrix.T, p_matrix, precision=lax.Precision.HIGHEST)
    cholesky_factor = jnp.linalg.cholesky(gram_matrix)
    return lax.linalg.triangular_solve(cholesky_factor, p_matrix, left_side=False, lower=True, transpose_a=True)

def reference(inputs, cotangent, occupancy, neighbours, weight, error_in, q_start):
    occupied_all = occupancy.astype(jnp.bfloat16)[..., None]
    occupied_inputs = (inputs * occupied_all).reshape(SHAPES, BRICKS, EDGE, EDGE, EDGE, CI)
    occupied_cotangent = (cotangent * occupied_all).reshape(SHAPES, BRICKS, EDGE, EDGE, EDGE, CO)
    margin = ((0, 0), (BRICK_DEV, BRICK_DEV), (0, 0), (0, 0), (0, 0), (0, 0))
    framed_inputs = jnp.pad(occupied_inputs, margin)
    framed_cotangent = jnp.pad(occupied_cotangent, margin)
    devices = N_DP * N_SPACE

    def per_device(position):
        shape_index = (position // N_SPACE).astype(jnp.int32)
        slab_index = (position % N_SPACE).astype(jnp.int32)
        start = (slab_index * BRICK_DEV).astype(jnp.int32)
        around_inputs = lax.dynamic_slice_in_dim(lax.dynamic_index_in_dim(framed_inputs, shape_index, 0, keepdims=False), start, 3 * BRICK_DEV, 0)
        around_cotangent = lax.dynamic_slice_in_dim(lax.dynamic_index_in_dim(framed_cotangent, shape_index, 0, keepdims=False), start, 3 * BRICK_DEV, 0)
        slots = lax.dynamic_slice_in_dim(lax.dynamic_index_in_dim(neighbours, shape_index, 0, keepdims=False), start, BRICK_DEV, 0)
        occupied = lax.dynamic_slice_in_dim(lax.dynamic_index_in_dim(occupied_all, shape_index, 0, keepdims=False), start, BRICK_DEV, 0)
        error_block = lax.dynamic_index_in_dim(lax.dynamic_index_in_dim(error_in, shape_index, 0, keepdims=False), slab_index, 0, keepdims=False)
        own_cotangent = around_cotangent[BRICK_DEV:2 * BRICK_DEV]
        padded_inputs = neighbourhood(around_inputs[BRICK_DEV:2 * BRICK_DEV], around_inputs[:BRICK_DEV], around_inputs[2 * BRICK_DEV:], slots)
        padded_cotangent = neighbourhood(own_cotangent, around_cotangent[:BRICK_DEV], around_cotangent[2 * BRICK_DEV:], slots)
        local_gradient, input_grad = brick_backward(padded_inputs, padded_cotangent, own_cotangent, occupied, weight)
        return (local_gradient + error_block.astype(jnp.float32), input_grad)
    corrected, input_grads = lax.map(per_device, jnp.arange(devices, dtype=jnp.int32))
    p_mean = jnp.einsum('dkc,cr->kr', corrected, q_start, precision=lax.Precision.HIGHEST) / devices
    p_basis = orthonormal(p_mean)
    q_factor = jnp.einsum('dkc,kr->cr', corrected, p_basis, precision=lax.Precision.HIGHEST) / devices
    approximation = jnp.dot(p_basis, q_factor.T, precision=lax.Precision.HIGHEST)
    new_error = (corrected - approximation[None]).astype(jnp.bfloat16).reshape(SHAPES, N_SPACE, KROWS, CO)
    input_grad = input_grads.reshape(SHAPES, BRICKS, VOXELS, CI)
    return (input_grad, q_factor, new_error)
```

```python
import jax
import jax.numpy as jnp
from jax import lax
from jax.experimental import pallas as pl
from jax.experimental.pallas import tpu as pltpu
from jax.sharding import PartitionSpec as P

EDGE = 8
PLANE = EDGE * EDGE
F32 = jnp.float32
BF16 = jnp.bfloat16
NT = (((1,), (1,)), ((), ()))
NN = (((1,), (0,)), ((), ()))
STEPS = (-1, 0, 1)


def split(value):
    high = value.astype(BF16)
    low = (value - high.astype(F32)).astype(BF16)
    return high, low


def source_rows(slots, step_x, step_y, step_z, along):
    shape = (128, 1) if along == 0 else (1, 128)
    place = lax.broadcasted_iota(jnp.int32, shape, along)
    brick = place // PLANE
    y = (place // EDGE) % EDGE + step_y
    z = place % EDGE + step_z
    wrapped_y = y % EDGE
    wrapped_z = z % EDGE
    rows = jnp.full(shape, -1, jnp.int32)
    for side_y in sorted({0, step_y}):
        in_y = (y < 0) if side_y < 0 else (y >= EDGE) if side_y > 0 else (y >= 0) & (y < EDGE)
        for side_z in sorted({0, step_z}):
            in_z = (z < 0) if side_z < 0 else (z >= EDGE) if side_z > 0 else (z >= 0) & (z < EDGE)
            if side_z == 0:
                offset = wrapped_y * EDGE + wrapped_z
                first, stride = 0, PLANE
            else:
                offset = wrapped_y
                first, stride = (128 if side_z < 0 else 144), EDGE
            for which in (0, 1):
                slot = slots[which, (step_x + 1) * 9 + (side_y + 1) * 3 + side_z + 1]
                base = jnp.where(slot < 0, -4096, slot * stride + first)
                rows = jnp.where(in_y & in_z & (brick == which), base + offset, rows)
    return rows


def one_hot(rows, along):
    shape = (128, 256) if along == 0 else (256, 128)
    places = lax.broadcasted_iota(jnp.int32, shape, 1 - along)
    return jnp.where(places == rows, 1.0, 0.0).astype(BF16)


def own_plane(field, mask, plane):
    rows = jnp.concatenate(
        [field[0, plane * PLANE : (plane + 1) * PLANE, :], field[1, plane * PLANE : (plane + 1) * PLANE, :]],
        axis=0,
    )
    return rows * mask[:, plane : plane + 1]


def source_plane(field, mask, lower, upper, plane):
    own = own_plane(field, mask, plane)
    return jnp.concatenate(
        [own, lower[plane], upper[plane], jnp.zeros((96, own.shape[1]), BF16)], axis=0
    )


def groups():
    return [(step_y, step_z) for step_y in STEPS for step_z in STEPS]


def coordinates():
    dp, space = lax.axis_index("dp"), lax.axis_index("space")
    return dp % 2, space // 16, (space % 2) * 2 + dp // 2, (space // 2) % 8


def place_of(tap, y):
    return ((tap // 7) ^ y) * 7 + tap % 7


def put_factor(mine, other, tap, value):
    core, x, y, _ = coordinates()
    place = place_of(tap, y)
    halves = value[:, :128], value[:, 128:]
    kept = jnp.where(core == 0, halves[0], halves[1])
    sent = jnp.where(core == 0, halves[1], halves[0])
    for block in range(4):
        rows = slice(block * 8, block * 8 + 8)
        mine[block ^ x, place] = kept[rows]
        other[block ^ x, place] = sent[rows]


def get_factor(mine, other, tap):
    core, x, y, _ = coordinates()
    place = place_of(tap, y)
    own = jnp.concatenate([mine[block ^ x, place] for block in range(4)], axis=0)
    rest = jnp.concatenate([other[block ^ x, place] for block in range(4)], axis=0)
    both = jnp.concatenate(
        [jnp.where(core == 0, own, rest), jnp.where(core == 0, rest, own)], axis=1
    )
    return both * (1.0 / 256.0)


def gradient_kernel(slots, field, cotangent, occupancy, lower, upper, start, error, corrected, mine, other, views, own, start_split):
    group = pl.program_id(0)

    @pl.when(group == 0)
    def _():
        mask = occupancy[...].T.astype(BF16)
        high, low = split(start[...].T)
        start_split[0:32, :] = high
        start_split[32:64, :] = low
        sources = []
        for plane in range(EDGE):
            own[plane * 128 : (plane + 1) * 128, :] = own_plane(cotangent, mask, plane)
            sources.append(source_plane(field, mask, lower, upper, plane).T)
        inner = jnp.concatenate(sources, axis=0)
        for first in range(0, 9, 2):
            pair = groups()[first : first + 2]
            for step_x, left, where in ((-1, sources[7], 0), (0, inner, 1), (1, sources[0], 9)):
                picks = jnp.concatenate(
                    [one_hot(source_rows(slots, step_x, y, z, 1), 1) for y, z in pair], axis=1
                )
                found = lax.dot_general(left, picks, NN, preferred_element_type=F32).astype(BF16)
                for member in range(len(pair)):
                    for block in range(left.shape[0] // 256):
                        views[first + member, :, (where + block) * 128 : (where + block + 1) * 128] = found[
                            block * 256 : (block + 1) * 256, member * 128 : (member + 1) * 128
                        ]

    for tap_x in range(3):
        columns = views[group, :, tap_x * 128 : tap_x * 128 + 1024]
        total = lax.dot_general(columns, own[...], NN, preferred_element_type=F32)
        total = total + error[tap_x, 0].astype(F32)
        corrected[tap_x, 0] = total
        high, low = split(total)
        both = lax.dot_general(start_split[...], high, NT, preferred_element_type=F32)
        rest = lax.dot_general(start_split[0:32, :], low, NT, preferred_element_type=F32)
        put_factor(mine, other, tap_x * 9 + group, both[0:32] + both[32:64] + rest)

    @pl.when(group == 8)
    def _():
        put_factor(mine, other, 27, jnp.zeros((32, 256), F32))


def local_gradient(slots, field, cotangent, occupancy, lower, upper, start, error):
    whole = lambda *shape: pl.BlockSpec(shape, lambda group: (0,) * len(shape))
    taps = lambda *shape: pl.BlockSpec((3, 1) + shape, lambda group: (0, group, 0, 0))
    return pl.pallas_call(
        gradient_kernel,
        grid=(9,),
        in_specs=[
            pl.BlockSpec(memory_space=pltpu.SMEM),
            whole(2, 512, 256),
            whole(2, 512, 256),
            whole(8, 128),
            whole(8, 16, 256),
            whole(8, 16, 256),
            whole(256, 32),
            taps(256, 256),
        ],
        out_specs=[taps(256, 256), whole(4, 28, 8, 128), whole(4, 28, 8, 128)],
        out_shape=[
            jax.ShapeDtypeStruct((3, 9, 256, 256), F32),
            jax.ShapeDtypeStruct((4, 28, 8, 128), F32),
            jax.ShapeDtypeStruct((4, 28, 8, 128), F32),
        ],
        scratch_shapes=[
            pltpu.VMEM((9, 256, 1280), BF16),
            pltpu.VMEM((1024, 256), BF16),
            pltpu.VMEM((64, 256), BF16),
        ],
        compiler_params=pltpu.CompilerParams(vmem_limit_bytes=48 * 1024 * 1024),
        cost_estimate=pl.CostEstimate(flops=6 * 10**9, bytes_accessed=14 * 10**6, transcendentals=0),
        name="local_gradient",
    )(slots, field, cotangent, occupancy, lower, upper, start, error)


def input_kernel(slots, cotangent, occupancy, lower, upper, weight, grad, views, mask_rows, total):
    group = pl.program_id(0)

    @pl.when(group == 0)
    def _():
        mask_rows[...] = occupancy[...].T
        mask = mask_rows[...].astype(BF16)
        sources = [source_plane(cotangent, mask, lower, upper, plane) for plane in range(EDGE)]
        for first in range(9):
            y, z = groups()[first]
            picks = [one_hot(source_rows(slots, step_x, y, z, 0), 0) for step_x in STEPS]
            for plane in range(-1, EDGE + 1):
                side = -1 if plane < 0 else 1 if plane >= EDGE else 0
                found = lax.dot_general(
                    picks[side + 1], sources[plane % EDGE], NN, preferred_element_type=F32
                )
                views[first, (plane + 1) * 128 : (plane + 2) * 128, :] = found.astype(BF16)
        total[...] = jnp.zeros_like(total)

    columns = jnp.concatenate(
        [views[8 - group, (2 - tap_x) * 128 : (2 - tap_x) * 128 + 1024, :] for tap_x in range(3)], axis=1
    )
    weights = jnp.concatenate([weight[tap_x, 0] for tap_x in range(3)], axis=1)
    total[...] += lax.dot_general(columns, weights, NT, preferred_element_type=F32)

    @pl.when(group == 8)
    def _():
        for plane in range(EDGE):
            rows = total[plane * 128 : (plane + 1) * 128, :] * mask_rows[:, plane : plane + 1]
            for brick in (0, 1):
                grad[brick, plane * PLANE : (plane + 1) * PLANE, :] = rows[
                    brick * PLANE : (brick + 1) * PLANE
                ].astype(BF16)


def input_gradient(slots, cotangent, occupancy, lower, upper, weight):
    whole = lambda *shape: pl.BlockSpec(shape, lambda group: (0,) * len(shape))
    taps = lambda *shape: pl.BlockSpec((3, 1) + shape, lambda group: (0, group, 0, 0))
    return pl.pallas_call(
        input_kernel,
        grid=(9,),
        in_specs=[
            pl.BlockSpec(memory_space=pltpu.SMEM),
            whole(2, 512, 256),
            whole(8, 128),
            whole(8, 16, 256),
            whole(8, 16, 256),
            taps(256, 256),
        ],
        out_specs=whole(2, 512, 256),
        out_shape=jax.ShapeDtypeStruct((2, 512, 256), BF16),
        scratch_shapes=[
            pltpu.VMEM((9, 1280, 256), BF16),
            pltpu.VMEM((128, 8), F32),
            pltpu.VMEM((1024, 256), F32),
        ],
        compiler_params=pltpu.CompilerParams(vmem_limit_bytes=48 * 1024 * 1024),
        cost_estimate=pl.CostEstimate(flops=6 * 10**9, bytes_accessed=6 * 10**6, transcendentals=0),
        name="input_gradient",
    )(slots, cotangent, occupancy, lower, upper, weight)


def right_kernel(mine, other, corrected, right, gram):
    step = pl.program_id(0)

    @pl.when(step == 0)
    def _():
        right[...] = jnp.zeros_like(right)
        gram[...] = jnp.zeros_like(gram)

    left = jnp.concatenate([get_factor(mine, other, step * 3 + tap) for tap in range(3)], axis=1)
    gram[...] += lax.dot_general(left, left, NT, precision=lax.Precision.HIGHEST, preferred_element_type=F32)
    left_high, left_low = split(left)
    high, low = split(corrected[...].reshape(768, 256))
    both = lax.dot_general(
        jnp.concatenate([left_high, left_low], axis=0), high, NN, preferred_element_type=F32
    )
    rest = lax.dot_general(left_high, low, NN, preferred_element_type=F32)
    right[...] += both[0:32] + both[32:64] + rest


def right_product(mine, other, corrected):
    blocks = lambda *shape: pl.BlockSpec((3,) + shape, lambda step: (step, 0, 0))
    whole = lambda *shape: pl.BlockSpec(shape, lambda step: (0,) * len(shape))
    return pl.pallas_call(
        right_kernel,
        grid=(9,),
        in_specs=[whole(4, 28, 8, 128), whole(4, 28, 8, 128), blocks(256, 256)],
        out_specs=[whole(32, 256), whole(32, 32)],
        out_shape=[jax.ShapeDtypeStruct((32, 256), F32), jax.ShapeDtypeStruct((32, 32), F32)],
        compiler_params=pltpu.CompilerParams(vmem_limit_bytes=32 * 1024 * 1024),
        name="right_product",
    )(mine, other, corrected)


def inverse_kernel(gram, inverse):
    places = lax.broadcasted_iota(jnp.int32, (32, 32), 0)
    columns = lax.broadcasted_iota(jnp.int32, (32, 32), 1)
    work = gram[...]
    made = jnp.where(places == columns, 1.0, 0.0).astype(F32)
    row_index = lax.broadcasted_iota(jnp.int32, (32, 1), 0)
    for step in range(32):
        scale = 1.0 / jnp.sqrt(work[step : step + 1, step : step + 1])
        work_row = work[step : step + 1, :] * scale
        made_row = made[step : step + 1, :] * scale
        column = work[:, step : step + 1] * scale
        later = jnp.where(row_index > step, column, 0.0)
        here = row_index == step
        work = jnp.where(here, work_row, work - later * work_row)
        made = jnp.where(here, made_row, made - later * made_row)
    inverse[...] = made


def inverse_factor(gram):
    return pl.pallas_call(
        inverse_kernel, out_shape=jax.ShapeDtypeStruct((32, 32), F32), name="inverse_factor"
    )(gram)


def error_kernel(mine, other, corrected, right, inverse, new_error, q_factor, basis):
    step = pl.program_id(0)

    @pl.when(step == 0)
    def _():
        q_rows = lax.dot_general(
            inverse[...], right[...], NN, precision=lax.Precision.HIGHEST, preferred_element_type=F32
        ) * (1.0 / 256.0)
        q_factor[...] = q_rows.T
        back = lax.dot_general(
            inverse[...].T, q_rows, NN, precision=lax.Precision.HIGHEST, preferred_element_type=F32
        )
        high, low = split(back)
        basis[0:32, :] = high
        basis[32:64, :] = high
        basis[64:96, :] = low
        basis[96:128, :] = jnp.zeros((32, 256), BF16)

    for tap in range(3):
        high, low = split(get_factor(mine, other, step * 3 + tap))
        left = jnp.concatenate([high, low, high, jnp.zeros((32, 256), BF16)], axis=0).T
        product = lax.dot_general(left, basis[...], NN, preferred_element_type=F32)
        new_error[tap] = (corrected[tap] - product).astype(BF16)


def remaining_error(mine, other, corrected, right, inverse):
    blocks = lambda *shape: pl.BlockSpec((3,) + shape, lambda step: (step, 0, 0))
    whole = lambda *shape: pl.BlockSpec(shape, lambda step: (0,) * len(shape))
    return pl.pallas_call(
        error_kernel,
        grid=(9,),
        in_specs=[whole(4, 28, 8, 128), whole(4, 28, 8, 128), blocks(256, 256), whole(32, 256), whole(32, 32)],
        out_specs=[blocks(256, 256), whole(256, 32)],
        out_shape=[jax.ShapeDtypeStruct((27, 256, 256), BF16), jax.ShapeDtypeStruct((256, 32), F32)],
        scratch_shapes=[pltpu.VMEM((128, 256), BF16)],
        compiler_params=pltpu.CompilerParams(vmem_limit_bytes=32 * 1024 * 1024),
        name="remaining_error",
    )(mine, other, corrected, right, inverse)


def face(field, occupied, at):
    chosen = field.reshape(2, EDGE, EDGE, EDGE, -1)[:, :, :, at, :]
    kept = occupied.reshape(2, EDGE, EDGE, EDGE)[:, :, :, at].astype(BF16)
    return (chosen * kept[..., None]).transpose(1, 0, 2, 3).reshape(EDGE, 2 * EDGE, -1)


def shifted(value, by):
    devices = lax.axis_size("space")
    return lax.ppermute(value, "space", [(i, i + by) for i in range(devices) if 0 <= i + by < devices])


def partners(core=0, x=0, y=0, z=0):
    def place(at_core, at_x, at_y, at_z):
        return (at_y % 2 * 2 + at_core) * 64 + (at_x * 8 + at_z) * 2 + at_y // 2

    return [
        (place(c, i, j, l), place(c ^ core, i ^ x, j ^ y, l ^ z))
        for c in range(2)
        for i in range(4)
        for j in range(4)
        for l in range(8)
    ]


def swapped(value, **bits):
    return lax.ppermute(value, ("dp", "space"), partners(**bits))


def added(values):
    return (values[0] + values[1]) + (values[2] + values[3])


def summed_among(value, steps):
    return added([value] + [swapped(value, **bits) for bits in steps])


ALONG_X = [dict(x=1), dict(x=2), dict(x=3)]
ALONG_Y = [dict(y=1), dict(y=2), dict(y=3)]
ALONG_Z = [dict(z=2), dict(z=4), dict(z=6)]
CORE_AND_Z = [dict(core=1), dict(z=1), dict(core=1, z=1)]


def factor_sum(mine, other):
    part = mine + swapped(other, core=1)
    part = added([part[0]] + [swapped(part[k], x=k) for k in (1, 2, 3)])
    part = part.reshape(4, 7, 8, 128)
    part = added([part[0]] + [swapped(part[k], y=k) for k in (1, 2, 3)])
    part = summed_among(part, ALONG_Z)
    part = part + swapped(part, z=1)
    part = jnp.concatenate([part] + [swapped(part, **bits) for bits in ALONG_Y], axis=0)
    part = jnp.stack([part] + [swapped(part, **bits) for bits in ALONG_X], axis=0)
    return part, swapped(part, core=1)


def right_sum(value):
    for steps in (CORE_AND_Z, ALONG_X, ALONG_Y, ALONG_Z):
        value = summed_among(value, steps)
    return value


def body(inputs, cotangent, occupancy, neighbours, weight, error_in, q_start):
    field, gradient, occupied, slots = inputs[0], cotangent[0], occupancy[0], neighbours[0]
    mask = occupied.reshape(2, EDGE, PLANE).transpose(1, 0, 2).reshape(EDGE, 2 * PLANE).astype(F32)
    lower_field = shifted(face(field, occupied, EDGE - 1), 1)
    upper_field = shifted(face(field, occupied, 0), -1)
    lower_gradient = shifted(face(gradient, occupied, EDGE - 1), 1)
    upper_gradient = shifted(face(gradient, occupied, 0), -1)
    corrected, mine, other = local_gradient(
        slots, field, gradient, mask, lower_field, upper_field, q_start, error_in.reshape(3, 9, 256, 256)
    )
    corrected = corrected.reshape(27, 256, 256)
    mine, other = factor_sum(mine, other)
    input_grad = input_gradient(
        slots, gradient, mask, lower_gradient, upper_gradient, weight.reshape(3, 9, 256, 256)
    )
    right, gram = right_product(mine, other, corrected)
    right = right_sum(right)
    inverse = inverse_factor(gram)
    new_error, q_factor = remaining_error(mine, other, corrected, right, inverse)
    return (input_grad[None], q_factor, new_error.reshape(1, 1, 6912, 256))


def solution(mesh):
    in_specs = (
        P("dp", "space", None, None),
        P("dp", "space", None, None),
        P("dp", "space", None),
        P("dp", "space", None),
        P(),
        P("dp", "space", None, None),
        P(),
    )
    out_specs = (P("dp", "space", None, None), P(), P("dp", "space", None, None))
    return jax.shard_map(body, mesh=mesh, in_specs=in_specs, out_specs=out_specs, check_vma=False)
```

```python
import functools

import jax
import jax.numpy as jnp
from jax import lax
from jax.experimental import pallas as pl
from jax.experimental.pallas import tpu as pltpu
from jax.sharding import PartitionSpec as P

EDGE = 8
PLANE = EDGE * EDGE
F32 = jnp.float32
BF16 = jnp.bfloat16
NT = (((1,), (1,)), ((), ()))
NN = (((1,), (0,)), ((), ()))
TN = (((0,), (0,)), ((), ()))
STEPS = (-1, 0, 1)
MIB = 1024 * 1024


def split(value):
    high = value.astype(BF16)
    low = (value - high.astype(F32)).astype(BF16)
    return high, low


def source_rows(slots, step_x, step_y, step_z, along):
    shape = (128, 1) if along == 0 else (1, 128)
    place = lax.broadcasted_iota(jnp.int32, shape, along)
    brick = place // PLANE
    y = (place // EDGE) % EDGE + step_y
    z = place % EDGE + step_z
    wrapped_y = y % EDGE
    wrapped_z = z % EDGE
    rows = jnp.full(shape, -1, jnp.int32)
    for side_y in sorted({0, step_y}):
        in_y = (y < 0) if side_y < 0 else (y >= EDGE) if side_y > 0 else (y >= 0) & (y < EDGE)
        for side_z in sorted({0, step_z}):
            in_z = (z < 0) if side_z < 0 else (z >= EDGE) if side_z > 0 else (z >= 0) & (z < EDGE)
            if side_z == 0:
                offset = wrapped_y * EDGE + wrapped_z
                first, stride = 0, PLANE
            else:
                offset = wrapped_y
                first, stride = (128 if side_z < 0 else 144), EDGE
            for which in (0, 1):
                slot = slots[which, (step_x + 1) * 9 + (side_y + 1) * 3 + side_z + 1]
                base = jnp.where(slot < 0, -4096, slot * stride + first)
                rows = jnp.where(in_y & in_z & (brick == which), base + offset, rows)
    return rows


def one_hot(rows, along, depth):
    shape = (128, depth) if along == 0 else (depth, 128)
    places = lax.broadcasted_iota(jnp.int32, shape, 1 - along)
    return jnp.where(places == rows, 1.0, 0.0).astype(BF16)


def own_plane(field, mask, plane):
    rows = jnp.concatenate([field[b, plane * PLANE : (plane + 1) * PLANE, :] for b in (0, 1)], axis=0)
    return rows * mask[:, plane : plane + 1]


def with_faces(own, lower, upper, plane):
    rest = jnp.zeros((96, own.shape[1]), BF16)
    return jnp.concatenate([own, lower[0, plane], upper[0, plane], rest], axis=0)


def coordinates():
    dp, space = lax.axis_index("dp"), lax.axis_index("space")
    return dp % 2, space // 16, (space % 2) * 2 + dp // 2, (space // 2) % 8


def place_of(tap, y):
    return ((tap // 7) ^ y) * 7 + tap % 7


def put_factor(mine, other, tap, value):
    core, x, y, _ = coordinates()
    place = place_of(tap, y)
    halves = value[:, :128], value[:, 128:]
    kept = jnp.where(core == 0, halves[0], halves[1])
    sent = jnp.where(core == 0, halves[1], halves[0])
    for block in range(4):
        rows = slice(block * 8, block * 8 + 8)
        mine[block ^ x, place] = kept[rows]
        other[block ^ x, place] = sent[rows]


def get_factor(mine, other, tap):
    core, x, y, _ = coordinates()
    place = place_of(tap, y)
    own = jnp.concatenate([mine[block ^ x, place] for block in range(4)], axis=0)
    rest = jnp.concatenate([other[block ^ x, place] for block in range(4)], axis=0)
    both = jnp.concatenate([jnp.where(core == 0, own, rest), jnp.where(core == 0, rest, own)], axis=1)
    return both * (1.0 / 256.0)


def whole(*shape):
    return pl.BlockSpec(shape, lambda *step: (0,) * len(shape))


def faces_kernel(field, cotangent, occupancy, up, down):
    mask = occupancy[...].T.astype(BF16)
    row = lax.broadcasted_iota(jnp.int32, (32, 128), 0)
    place = lax.broadcasted_iota(jnp.int32, (32, 128), 1)
    wanted = jnp.where(row < 16, row * EDGE + EDGE - 1, (row - 16) * EDGE)
    picks = jnp.where(place == wanted, 1.0, 0.0).astype(BF16)
    for which, source in enumerate((field, cotangent)):
        for plane in range(EDGE):
            found = lax.dot_general(picks, own_plane(source, mask, plane), NN, preferred_element_type=F32)
            up[which, plane] = found[:16].astype(BF16)
            down[which, plane] = found[16:].astype(BF16)


def brick_faces(field, cotangent, occupancy):
    shape = jax.ShapeDtypeStruct((2, EDGE, 16, 256), BF16)
    return pl.pallas_call(faces_kernel, out_shape=[shape, shape], compiler_params=SMALL, name="brick_faces")(
        in_hbm(field), in_hbm(cotangent), occupancy
    )


def gradient_kernel(sides, *refs):
    count = 3 * len(sides)
    faces = sides != (0,)
    slots, field, cotangent, occupancy, start, error = refs[:6]
    refs = refs[6:]
    if faces:
        lower, upper, _, mine_before, other_before = refs[:5]
        refs = refs[5:]
    corrected, mine, other, views, own, start_split, kept_high, kept_low = refs
    step = pl.program_id(0)

    @pl.when(step == 0)
    def _():
        mask = occupancy[...].T.astype(BF16)
        high, low = split(start[...])
        start_split[0:32, :] = high
        start_split[32:64, :] = low
        depth = 256 if faces else 128
        sources = []
        for plane in range(EDGE):
            own[plane * 128 : (plane + 1) * 128, :] = own_plane(cotangent, mask, plane)
            source = own_plane(field, mask, plane)
            if faces:
                source = with_faces(source, lower, upper, plane)
            sources.append(source.T)
        inner = jnp.concatenate(sources, axis=0)
        groups = [(y, z) for y in STEPS for z in sides]
        for first in range(0, count, 2):
            pair = groups[first : first + 2]
            for step_x, left, where in ((-1, sources[7], 0), (0, inner, 1), (1, sources[0], 9)):
                picks = jnp.concatenate(
                    [one_hot(source_rows(slots, step_x, y, z, 1), 1, depth) for y, z in pair], axis=1
                )
                found = lax.dot_general(left, picks, NN, preferred_element_type=F32).astype(BF16)
                for member in range(len(pair)):
                    for block in range(left.shape[0] // 256):
                        views[first + member, :, (where + block) * 128 : (where + block + 1) * 128] = found[
                            block * 256 : (block + 1) * 256, member * 128 : (member + 1) * 128
                        ]
        if faces:
            mine[...] = mine_before[...]
            other[...] = other_before[...]

    def product():
        columns = jnp.concatenate([views[step, :, k * 128 : k * 128 + 1024] for k in range(3)], axis=0)
        total = lax.dot_general(columns, own[...], NN, preferred_element_type=F32)
        total = total + error[:, 0, 0].astype(F32).reshape(768, 256)
        corrected[:, 0, 0] = total.reshape(3, 256, 256)
        return split(total)

    def keep(parts):
        kept_high[...], kept_low[...] = parts

    def factor():
        both = lax.dot_general(start_split[...], kept_high[...], NT, preferred_element_type=F32)
        rest = lax.dot_general(start_split[0:32, :], kept_low[...], NT, preferred_element_type=F32)
        return both[0:32] + both[32:64] + rest

    def put(made):
        before = step - 1
        if faces:
            group = before // 2 * 3 + before % 2 * 2
        else:
            group = before * 3 + 1
        for tap_x in range(3):
            put_factor(mine, other, tap_x * 9 + group, made[:, tap_x * 256 : tap_x * 256 + 256])

    @pl.when(step == 0)
    def _():
        keep(product())

    @pl.when((step > 0) & (step < count))
    def _():
        made = factor()
        parts = product()
        put(made)
        keep(parts)

    @pl.when(step == count)
    def _():
        put(factor())
        if not faces:
            put_factor(mine, other, 27, jnp.zeros((32, 256), F32))


def local_gradient(sides, slots, field, cotangent, occupancy, start, error, *more):
    count = 3 * len(sides)
    faces = sides != (0,)

    def at(step):
        group = jnp.minimum(step, count - 1)
        return (0, group // 2, group % 2 * 2, 0, 0) if faces else (0, group, 1, 0, 0)

    taps = pl.BlockSpec((3, 1, 1, 256, 256), at)
    piece = whole(4, 28, 8, 128)
    face = whole(1, EDGE, 16, 256)
    in_specs = [
        pl.BlockSpec(memory_space=pltpu.SMEM),
        whole(2, 512, 256),
        whole(2, 512, 256),
        whole(8, 128),
        whole(32, 256),
        taps,
    ]
    if faces:
        in_specs += [face, face, pl.BlockSpec(memory_space=pl.ANY), piece, piece]
    return pl.pallas_call(
        functools.partial(gradient_kernel, sides),
        grid=(count + 1,),
        in_specs=in_specs,
        out_specs=[taps, piece, piece],
        out_shape=[
            CORRECTED,
            jax.ShapeDtypeStruct((4, 28, 8, 128), F32),
            jax.ShapeDtypeStruct((4, 28, 8, 128), F32),
        ],
        input_output_aliases={8: 0} if faces else {},
        scratch_shapes=[
            pltpu.VMEM((count, 256, 1280), BF16),
            pltpu.VMEM((1024, 256), BF16),
            pltpu.VMEM((64, 256), BF16),
            pltpu.VMEM((768, 256), BF16),
            pltpu.VMEM((768, 256), BF16),
        ],
        compiler_params=pltpu.CompilerParams(vmem_limit_bytes=GRAD_LIMIT),
        cost_estimate=pl.CostEstimate(
            flops=count * 6 * 10**8, bytes_accessed=count * 15 * 10**5, transcendentals=0
        ),
        name="gradient_with_faces" if faces else "gradient_own",
    )(slots, field, cotangent, occupancy, start, error, *more)


def input_kernel(side, last, *refs):
    slots, cotangent, occupancy, weight = refs[:4]
    refs = refs[4:]
    if side:
        face, total_before = refs[:2]
        refs = refs[2:]
    result, views, total = refs[-3:]
    step = pl.program_id(0)

    @pl.when(step == 0)
    def _():
        mask = occupancy[...].T.astype(BF16)
        sources = [own_plane(cotangent, mask, plane) for plane in range(EDGE)]
        if side:
            sources = [with_faces(own, face, face, plane) for plane, own in enumerate(sources)]
        for index, y in enumerate(STEPS):
            picks = [one_hot(source_rows(slots, x, y, -side, 0), 0, 256 if side else 128) for x in STEPS]
            for plane in range(-1, EDGE + 1):
                which = 0 if plane < 0 else 2 if plane >= EDGE else 1
                found = lax.dot_general(picks[which], sources[plane % EDGE], NN, preferred_element_type=F32)
                views[index, (plane + 1) * 128 : (plane + 2) * 128, :] = found.astype(BF16)
        total[...] = total_before[...] if side else jnp.zeros_like(total)

    columns = jnp.concatenate(
        [views[2 - step, (2 - tap_x) * 128 : (2 - tap_x) * 128 + 1024, :] for tap_x in range(3)], axis=1
    )
    weights = jnp.concatenate([weight[tap_x, 0, 0] for tap_x in range(3)], axis=1)
    total[...] += lax.dot_general(columns, weights, NT, preferred_element_type=F32)

    @pl.when(step == 2)
    def _():
        if not last:
            result[...] = total[...]
            return
        mask = occupancy[...].T
        for plane in range(EDGE):
            rows = total[plane * 128 : (plane + 1) * 128, :] * mask[:, plane : plane + 1]
            for brick in (0, 1):
                result[brick, plane * PLANE : (plane + 1) * PLANE, :] = rows[
                    brick * PLANE : (brick + 1) * PLANE
                ].astype(BF16)


def input_gradient(side, last, slots, cotangent, occupancy, weight, *more, tie=None):
    in_specs = [
        pl.BlockSpec(memory_space=pltpu.SMEM),
        whole(2, 512, 256),
        whole(8, 128),
        pl.BlockSpec((3, 1, 1, 256, 256), lambda step: (0, step, side + 1, 0, 0)),
    ]
    if side:
        in_specs += [pl.BlockSpec((1, EDGE, 16, 256), lambda step: (1, 0, 0, 0)), whole(1024, 256)]
    if tie is not None:
        in_specs += [pl.BlockSpec(memory_space=pl.ANY)]
        more += (tie,)
    if last:
        shape, spec = jax.ShapeDtypeStruct((2, 512, 256), BF16), whole(2, 512, 256)
    else:
        shape, spec = jax.ShapeDtypeStruct((1024, 256), F32), whole(1024, 256)
    return pl.pallas_call(
        functools.partial(input_kernel, side, last),
        grid=(3,),
        in_specs=in_specs,
        out_specs=spec,
        out_shape=shape,
        scratch_shapes=[pltpu.VMEM((3, 1280, 256), BF16), pltpu.VMEM((1024, 256), F32)],
        compiler_params=pltpu.CompilerParams(vmem_limit_bytes=INPUT_LIMIT),
        cost_estimate=pl.CostEstimate(flops=2 * 10**9, bytes_accessed=4 * 10**6, transcendentals=0),
        name=("input_own", "input_above", "input_below")[side],
    )(slots, cotangent, occupancy, weight, *more)


def right_kernel(mine, other, corrected, right):
    step = pl.program_id(0)

    @pl.when(step == 0)
    def _():
        right[...] = jnp.zeros_like(right)

    left = jnp.concatenate([get_factor(mine, other, step * 3 + tap) for tap in range(3)], axis=1)
    left_high, left_low = split(left)
    high, low = split(corrected[...].reshape(768, 256))
    both = lax.dot_general(jnp.concatenate([left_high, left_low], axis=0), high, NN, preferred_element_type=F32)
    rest = lax.dot_general(left_high, low, NN, preferred_element_type=F32)
    right[...] += both[0:32] + both[32:64] + rest


def blocks(*shape):
    return pl.BlockSpec((3,) + shape, lambda step: (step, 0, 0))


def right_product(mine, other, corrected):
    return pl.pallas_call(
        right_kernel,
        grid=(9,),
        in_specs=[whole(4, 28, 8, 128), whole(4, 28, 8, 128), blocks(256, 256)],
        out_specs=whole(32, 256),
        out_shape=jax.ShapeDtypeStruct((32, 256), F32),
        compiler_params=pltpu.CompilerParams(vmem_limit_bytes=LATE_LIMIT),
        name="right_product",
    )(mine, other, in_vmem(corrected))


def eliminate(first, work, made):
    places = lax.broadcasted_iota(jnp.int32, (32, 1), 0)
    for step in range(first, first + 16):
        scale = 1.0 / jnp.sqrt(work[step : step + 1, step : step + 1])
        work_row = work[step : step + 1, :] * scale
        made_row = made[step : step + 1, :] * scale
        column = work[:, step : step + 1] * scale
        later = jnp.where(places > step, column, 0.0)
        here = places == step
        work = jnp.where(here, work_row, work - later * work_row)
        made = jnp.where(here, made_row, made - later * made_row)
    return work, made


def first_half_kernel(mine, other, work, made):
    gram = jnp.zeros((32, 32), F32)
    for step in range(9):
        left = jnp.concatenate([get_factor(mine, other, step * 3 + tap) for tap in range(3)], axis=1)
        gram += lax.dot_general(left, left, NT, precision=lax.Precision.HIGHEST, preferred_element_type=F32)
    row = lax.broadcasted_iota(jnp.int32, (32, 32), 0)
    column = lax.broadcasted_iota(jnp.int32, (32, 32), 1)
    work[...], made[...] = eliminate(0, gram, jnp.where(row == column, 1.0, 0.0).astype(F32))


def second_half_kernel(work, made, inverse):
    inverse[...] = eliminate(16, work[...], made[...])[1]


SQUARE = jax.ShapeDtypeStruct((32, 32), F32)


def half_inverse(mine, other):
    return pl.pallas_call(first_half_kernel, out_shape=[SQUARE, SQUARE], compiler_params=SMALL, name="half_inverse")(
        mine, other
    )


def whole_inverse(work, made, tie=None):
    def kernel(work, made, *refs):
        second_half_kernel(work, made, refs[-1])

    more = () if tie is None else (tie,)
    vmem = pl.BlockSpec(memory_space=pltpu.VMEM)
    return pl.pallas_call(
        kernel,
        in_specs=[vmem, vmem] + [pl.BlockSpec(memory_space=pl.ANY)] * len(more),
        out_specs=vmem,
        out_shape=SQUARE,
        compiler_params=SMALL,
        name="whole_inverse",
    )(work, made, *more)


def error_kernel(mine, other, corrected, right, inverse, new_error, q_rows, basis):
    step = pl.program_id(0)

    @pl.when(step == 0)
    def _():
        rows = lax.dot_general(
            inverse[...], right[...], NN, precision=lax.Precision.HIGHEST, preferred_element_type=F32
        ) * (1.0 / 256.0)
        q_rows[...] = rows
        back = lax.dot_general(
            inverse[...].T, rows, NN, precision=lax.Precision.HIGHEST, preferred_element_type=F32
        )
        high, low = split(back)
        basis[0:32, :] = high
        basis[32:64, :] = high
        basis[64:96, :] = low
        basis[96:128, :] = jnp.zeros((32, 256), BF16)

    high, low = split(jnp.concatenate([get_factor(mine, other, step * 3 + tap) for tap in range(3)], axis=1))
    left = jnp.concatenate([high, low, high, jnp.zeros((32, 768), BF16)], axis=0)
    product = lax.dot_general(left, basis[...], TN, preferred_element_type=F32)
    new_error[...] = (corrected[...] - product.reshape(3, 256, 256)).astype(BF16)


def remaining_error(mine, other, corrected, right, inverse):
    return pl.pallas_call(
        error_kernel,
        grid=(9,),
        in_specs=[whole(4, 28, 8, 128), whole(4, 28, 8, 128), blocks(256, 256), whole(32, 256), whole(32, 32)],
        out_specs=[blocks(256, 256), whole(32, 256)],
        out_shape=[jax.ShapeDtypeStruct((27, 256, 256), BF16), jax.ShapeDtypeStruct((32, 256), F32)],
        scratch_shapes=[pltpu.VMEM((128, 256), BF16)],
        compiler_params=pltpu.CompilerParams(vmem_limit_bytes=LATE_LIMIT),
        name="remaining_error",
    )(mine, other, in_vmem(corrected), right, inverse)


CORRECTED = pltpu.VMEM((3, 3, 3, 256, 256), F32)
GRAD_LIMIT = 32 * MIB
INPUT_LIMIT = 24 * MIB
LATE_LIMIT = 24 * MIB
SMALL = pltpu.CompilerParams(vmem_limit_bytes=12 * MIB)


def in_vmem(value):
    return pltpu.with_memory_space_constraint(value, pltpu.VMEM)


def in_hbm(value):
    return pltpu.with_memory_space_constraint(value, pltpu.HBM)


def shifted(value, by):
    devices = lax.axis_size("space")
    return lax.ppermute(value, "space", [(i, i + by) for i in range(devices) if 0 <= i + by < devices])


def partners(core=0, x=0, y=0, z=0):
    def place(at_core, at_x, at_y, at_z):
        return (at_y % 2 * 2 + at_core) * 64 + (at_x * 8 + at_z) * 2 + at_y // 2

    return [
        (place(c, i, j, l), place(c ^ core, i ^ x, j ^ y, l ^ z))
        for c in range(2)
        for i in range(4)
        for j in range(4)
        for l in range(8)
    ]


def swapped(value, **bits):
    return lax.ppermute(value, ("dp", "space"), partners(**bits))


def added(values):
    return (values[0] + values[1]) + (values[2] + values[3])


def summed_among(value, steps):
    return added([value] + [swapped(value, **bits) for bits in steps])


ALONG_X = [dict(x=1), dict(x=2), dict(x=3)]
ALONG_Y = [dict(y=1), dict(y=2), dict(y=3)]
ALONG_Z = [dict(z=2), dict(z=4), dict(z=6)]
CORE_AND_Z = [dict(core=1), dict(z=1), dict(core=1, z=1)]


def body(inputs, cotangent, occupancy, neighbours, weight, error_in, q_start):
    field, gradient, occupied, slots = inputs[0], cotangent[0], occupancy[0], neighbours[0]
    mask = occupied.reshape(2, EDGE, PLANE).transpose(1, 0, 2).reshape(EDGE, 2 * PLANE).astype(F32)
    weight = weight.reshape(3, 3, 3, 256, 256)
    up, down = brick_faces(field, gradient, mask)
    lower, upper = shifted(up, 1), shifted(down, -1)
    fixed = (slots, in_hbm(field), in_hbm(gradient), mask, q_start.T, in_hbm(error_in.reshape(3, 3, 3, 256, 256)))
    corrected, mine, other = local_gradient((0,), *fixed)
    corrected, mine, other = local_gradient((-1, 1), *fixed, lower, upper, in_vmem(corrected), mine, other)
    corrected = corrected.reshape(27, 256, 256)

    part = mine + swapped(other, core=1)
    arrived = [swapped(part[k], x=k) for k in (1, 2, 3)]
    total = input_gradient(0, False, slots, gradient, mask, weight, tie=part)
    part, total = lax.optimization_barrier((added([part[0]] + arrived), total))
    part = part.reshape(4, 7, 8, 128)
    part = added([part[0]] + [swapped(part[k], y=k) for k in (1, 2, 3)])
    arrived = [swapped(part, **bits) for bits in ALONG_Z]
    total = input_gradient(-1, False, slots, gradient, mask, weight, upper, total, tie=part)
    part, total = lax.optimization_barrier((added([part] + arrived), total))
    part = part + swapped(part, z=1)
    part = jnp.concatenate([part] + [swapped(part, **bits) for bits in ALONG_Y], axis=0)
    arrived = [swapped(part, **bits) for bits in ALONG_X]
    input_grad = input_gradient(1, True, slots, gradient, mask, weight, lower, total, tie=part)
    mine, input_grad = lax.optimization_barrier((jnp.stack([part] + arrived, axis=0), input_grad))
    other = swapped(mine, core=1)

    right = right_product(mine, other, corrected)
    arrived = [swapped(right, **bits) for bits in CORE_AND_Z]
    halves = half_inverse(mine, other)
    right, *halves = lax.optimization_barrier((added([right] + arrived), *halves))
    arrived = [swapped(right, **bits) for bits in ALONG_X]
    inverse = whole_inverse(*halves, tie=right)
    right, inverse = lax.optimization_barrier((added([right] + arrived), inverse))
    right = summed_among(summed_among(right, ALONG_Y), ALONG_Z)
    new_error, q_rows = remaining_error(mine, other, corrected, right, inverse)
    return (input_grad[None], q_rows.T, new_error.reshape(1, 1, 6912, 256))


def solution(mesh):
    in_specs = (
        P("dp", "space", None, None),
        P("dp", "space", None, None),
        P("dp", "space", None),
        P("dp", "space", None),
        P(),
        P("dp", "space", None, None),
        P(),
    )
    out_specs = (P("dp", "space", None, None), P(), P("dp", "space", None, None))
    return jax.shard_map(body, mesh=mesh, in_specs=in_specs, out_specs=out_specs, check_vma=False)
```

```python
import functools

import jax
import jax.numpy as jnp
from jax import lax
from jax.experimental import pallas as pl
from jax.experimental.pallas import tpu as pltpu
from jax.sharding import PartitionSpec as P

EDGE = 8
PLANE = EDGE * EDGE
F32 = jnp.float32
BF16 = jnp.bfloat16
NT = (((1,), (1,)), ((), ()))
NN = (((1,), (0,)), ((), ()))
TN = (((0,), (0,)), ((), ()))
STEPS = (-1, 0, 1)
MIB = 1024 * 1024


def split(value):
    high = value.astype(BF16)
    low = (value - high.astype(F32)).astype(BF16)
    return high, low


def source_rows(slots, step_x, step_y, step_z, along):
    shape = (128, 1) if along == 0 else (1, 128)
    place = lax.broadcasted_iota(jnp.int32, shape, along)
    brick = place // PLANE
    y = (place // EDGE) % EDGE + step_y
    z = place % EDGE + step_z
    wrapped_y = y % EDGE
    wrapped_z = z % EDGE
    rows = jnp.full(shape, -1, jnp.int32)
    for side_y in sorted({0, step_y}):
        in_y = (y < 0) if side_y < 0 else (y >= EDGE) if side_y > 0 else (y >= 0) & (y < EDGE)
        for side_z in sorted({0, step_z}):
            in_z = (z < 0) if side_z < 0 else (z >= EDGE) if side_z > 0 else (z >= 0) & (z < EDGE)
            if side_z == 0:
                offset = wrapped_y * EDGE + wrapped_z
                first, stride = 0, PLANE
            else:
                offset = wrapped_y
                first, stride = (128 if side_z < 0 else 144), EDGE
            for which in (0, 1):
                slot = slots[which, (step_x + 1) * 9 + (side_y + 1) * 3 + side_z + 1]
                base = jnp.where(slot < 0, -4096, slot * stride + first)
                rows = jnp.where(in_y & in_z & (brick == which), base + offset, rows)
    return rows


def one_hot(rows, along, depth):
    shape = (128, depth) if along == 0 else (depth, 128)
    places = lax.broadcasted_iota(jnp.int32, shape, 1 - along)
    return jnp.where(places == rows, 1.0, 0.0).astype(BF16)


def voxel_mask(occupancy):
    padded = jnp.concatenate([occupancy[...].astype(F32), jnp.zeros((6, 512), F32)], axis=0)
    return padded.T


def own_plane(field, mask, plane):
    rows = slice(plane * PLANE, (plane + 1) * PLANE)
    return jnp.concatenate([field[b, rows, :] * mask[rows, b : b + 1] for b in (0, 1)], axis=0)


def with_faces(own, lower, upper, plane):
    rest = jnp.zeros((96, own.shape[1]), BF16)
    return jnp.concatenate([own, lower[0, plane], upper[0, plane], rest], axis=0)


def coordinates():
    dp, space = lax.axis_index("dp"), lax.axis_index("space")
    return dp % 2, space // 16, (space % 2) * 2 + dp // 2, (space // 2) % 8


def place_of(tap, y):
    return ((tap // 7) ^ y) * 7 + tap % 7


def put_factor(mine, other, tap, value):
    core, x, y, _ = coordinates()
    place = place_of(tap, y)
    halves = value[:, :128], value[:, 128:]
    kept = jnp.where(core == 0, halves[0], halves[1])
    sent = jnp.where(core == 0, halves[1], halves[0])
    for block in range(4):
        rows = slice(block * 8, block * 8 + 8)
        mine[block ^ x, place] = kept[rows]
        other[block ^ x, place] = sent[rows]


def get_factor(mine, other, tap):
    core, x, y, _ = coordinates()
    place = place_of(tap, y)
    own = jnp.concatenate([mine[block ^ x, place] for block in range(4)], axis=0)
    rest = jnp.concatenate([other[block ^ x, place] for block in range(4)], axis=0)
    both = jnp.concatenate([jnp.where(core == 0, own, rest), jnp.where(core == 0, rest, own)], axis=1)
    return both * (1.0 / 256.0)


def whole(*shape):
    return pl.BlockSpec(shape, lambda *step: (0,) * len(shape))


def faces_kernel(field, cotangent, occupancy, up, down):
    mask = voxel_mask(occupancy).astype(BF16)
    row = lax.broadcasted_iota(jnp.int32, (32, 128), 0)
    place = lax.broadcasted_iota(jnp.int32, (32, 128), 1)
    wanted = jnp.where(row < 16, row * EDGE + EDGE - 1, (row - 16) * EDGE)
    picks = jnp.where(place == wanted, 1.0, 0.0).astype(BF16)
    for which, source in enumerate((field, cotangent)):
        for plane in range(EDGE):
            found = lax.dot_general(picks, own_plane(source, mask, plane), NN, preferred_element_type=F32)
            up[which, plane] = found[:16].astype(BF16)
            down[which, plane] = found[16:].astype(BF16)


def brick_faces(field, cotangent, occupancy):
    shape = jax.ShapeDtypeStruct((2, EDGE, 16, 256), BF16)
    return pl.pallas_call(faces_kernel, out_shape=[shape, shape], compiler_params=SMALL, name="brick_faces")(
        in_hbm(field), in_hbm(cotangent), occupancy
    )


def gradient_kernel(sides, width, *refs):
    faces = sides != (0,)
    slots, field, cotangent, occupancy, start, error = refs[:6]
    refs = refs[6:]
    if faces:
        lower, upper, _, mine_before, other_before = refs[:5]
        refs = refs[5:]
    corrected, mine, other, views, sources, own, start_parts = refs
    step = pl.program_id(0)
    depth = 256 if faces else 128
    shares = 3 // width
    side = step // shares * 2 - 1 if faces else 0

    @pl.when(step == 0)
    def _():
        mask = voxel_mask(occupancy).astype(BF16)
        high, low = split(start[...].T)
        none = jnp.zeros((256, 32), BF16)
        start_parts[0:256, :] = jnp.concatenate([high, low, none, none], axis=1)
        start_parts[256:512, :] = jnp.concatenate([high, none, none, none], axis=1)
        start_parts[512:768, :] = jnp.concatenate([none, none, high, low], axis=1)
        start_parts[768:1024, :] = jnp.concatenate([none, none, high, none], axis=1)
        for plane in range(EDGE):
            own[plane * 128 : (plane + 1) * 128, :] = own_plane(cotangent, mask, plane)
            source = own_plane(field, mask, plane)
            if faces:
                source = with_faces(source, lower, upper, plane)
            sources[plane * 256 : (plane + 1) * 256, :] = source.T
        if faces:
            mine[...] = mine_before[...]
            other[...] = other_before[...]
        else:
            put_factor(mine, other, 27, jnp.zeros((32, 256), F32))

    def gather(groups):
        for first in range(0, len(groups), 2):
            pair = groups[first : first + 2]
            for step_x, left, where in (
                (-1, sources[7 * 256 : 8 * 256, :], 0),
                (0, sources[...], 1),
                (1, sources[0:256, :], 9),
            ):
                picks = jnp.concatenate(
                    [one_hot(source_rows(slots, step_x, y, z, 1), 1, depth) for y, z in pair], axis=1
                )
                found = lax.dot_general(left, picks, NN, preferred_element_type=F32).astype(BF16)
                for member in range(len(pair)):
                    for block in range(left.shape[0] // 256):
                        views[first + member, :, (where + block) * 128 : (where + block + 1) * 128] = found[
                            block * 256 : (block + 1) * 256, member * 128 : (member + 1) * 128
                        ]

    for index in range(len(sides) * shares):
        chosen = STEPS[index % shares * width : index % shares * width + width]

        @pl.when(step == index)
        def _():
            gather([(y, sides[index // shares]) for y in chosen])

    parts = []
    for member in range(width):
        columns = jnp.concatenate([views[member, :, k * 128 : k * 128 + 1024] for k in range(3)], axis=0)
        total = lax.dot_general(columns, own[...], NN, preferred_element_type=F32)
        total = total + error[:, member, 0].astype(F32).reshape(768, 256)
        corrected[0, :, member] = total.reshape(3, 256, 256)
        high, low = split(total)
        for tap_x in range(3):
            rows = slice(tap_x * 256, tap_x * 256 + 256)
            parts.append((tap_x, member, [high[rows], low[rows]]))
    for first in range(0, 3 * width, 2):
        chosen = parts[first : first + 2]
        left = jnp.concatenate([part for _, _, both in chosen for part in both], axis=1)
        made = lax.dot_general(left, start_parts[0 : left.shape[1], :], NN, preferred_element_type=F32).T
        for slot, (tap_x, member, _) in enumerate(chosen):
            step_y = step % shares * width + member
            rows = made[slot * 64 : slot * 64 + 64]
            put_factor(mine, other, tap_x * 9 + step_y * 3 + side + 1, rows[:32] + rows[32:])


def local_gradient(sides, slots, field, cotangent, occupancy, start, error, *more):
    faces = sides != (0,)
    width = FACES_WIDTH if faces else OWN_WIDTH
    shares = 3 // width

    def which(step):
        return step // shares * 2 if faces else 1

    piece = whole(4, 28, 8, 128)
    face = whole(1, EDGE, 16, 256)
    in_specs = [
        pl.BlockSpec(memory_space=pltpu.SMEM),
        whole(2, 512, 256),
        whole(2, 512, 256),
        whole(2, 512),
        whole(32, 256),
        pl.BlockSpec((3, width, 1, 256, 256), lambda step: (0, step % shares, which(step), 0, 0)),
    ]
    if faces:
        in_specs += [face, face, pl.BlockSpec(memory_space=pl.ANY), piece, piece]
    depth = 256 if faces else 128
    return pl.pallas_call(
        functools.partial(gradient_kernel, sides, width),
        grid=(len(sides) * shares,),
        in_specs=in_specs,
        out_specs=[
            pl.BlockSpec((1, 3, width, 256, 256), lambda step: (which(step), 0, step % shares, 0, 0)),
            piece,
            piece,
        ],
        out_shape=[
            CORRECTED,
            jax.ShapeDtypeStruct((4, 28, 8, 128), F32),
            jax.ShapeDtypeStruct((4, 28, 8, 128), F32),
        ],
        input_output_aliases={8: 0} if faces else {},
        scratch_shapes=[
            pltpu.VMEM((width, 256, 1280), BF16),
            pltpu.VMEM((2048, depth), BF16),
            pltpu.VMEM((1024, 256), BF16),
            pltpu.VMEM((1024, 128), BF16),
        ],
        compiler_params=pltpu.CompilerParams(vmem_limit_bytes=GRAD_LIMIT),
        cost_estimate=pl.CostEstimate(
            flops=len(sides) * 2 * 10**9, bytes_accessed=len(sides) * 4 * 10**6, transcendentals=0
        ),
        name="gradient_with_faces" if faces else "gradient_own",
    )(slots, field, cotangent, occupancy, start, error, *more)


def input_kernel(side, last, *refs):
    slots, cotangent, occupancy, weight = refs[:4]
    refs = refs[4:]
    if side:
        face, total_before = refs[:2]
        refs = refs[2:]
    result, views, total = refs[-3:]
    step = pl.program_id(0)

    @pl.when(step == 0)
    def _():
        mask = voxel_mask(occupancy).astype(BF16)
        sources = [own_plane(cotangent, mask, plane) for plane in range(EDGE)]
        if side:
            sources = [with_faces(own, face, face, plane) for plane, own in enumerate(sources)]
        for index, y in enumerate(STEPS):
            picks = [one_hot(source_rows(slots, x, y, -side, 0), 0, 256 if side else 128) for x in STEPS]
            for plane in range(-1, EDGE + 1):
                which = 0 if plane < 0 else 2 if plane >= EDGE else 1
                found = lax.dot_general(picks[which], sources[plane % EDGE], NN, preferred_element_type=F32)
                views[index, (plane + 1) * 128 : (plane + 2) * 128, :] = found.astype(BF16)
        total[...] = total_before[...] if side else jnp.zeros_like(total)

    columns = jnp.concatenate(
        [views[2 - step, (2 - tap_x) * 128 : (2 - tap_x) * 128 + 1024, :] for tap_x in range(3)], axis=1
    )
    weights = jnp.concatenate([weight[tap_x, 0, 0] for tap_x in range(3)], axis=1)
    total[...] += lax.dot_general(columns, weights, NT, preferred_element_type=F32)

    @pl.when(step == 2)
    def _():
        if not last:
            result[...] = total[...]
            return
        mask = voxel_mask(occupancy)
        for plane in range(EDGE):
            for brick in (0, 1):
                first = (2 * plane + brick) * PLANE
                rows = slice(plane * PLANE, (plane + 1) * PLANE)
                kept = total[first : first + PLANE, :] * mask[rows, brick : brick + 1]
                result[brick, rows, :] = kept.astype(BF16)


def input_gradient(side, last, slots, cotangent, occupancy, weight, *more, tie=None):
    in_specs = [
        pl.BlockSpec(memory_space=pltpu.SMEM),
        whole(2, 512, 256),
        whole(2, 512),
        pl.BlockSpec((3, 1, 1, 256, 256), lambda step: (0, step, side + 1, 0, 0)),
    ]
    if side:
        in_specs += [pl.BlockSpec((1, EDGE, 16, 256), lambda step: (1, 0, 0, 0)), whole(1024, 256)]
    if tie is not None:
        in_specs += [pl.BlockSpec(memory_space=pl.ANY)]
        more += (tie,)
    if last:
        shape, spec = jax.ShapeDtypeStruct((2, 512, 256), BF16), whole(2, 512, 256)
    else:
        shape, spec = jax.ShapeDtypeStruct((1024, 256), F32), whole(1024, 256)
    return pl.pallas_call(
        functools.partial(input_kernel, side, last),
        grid=(3,),
        in_specs=in_specs,
        out_specs=spec,
        out_shape=shape,
        scratch_shapes=[pltpu.VMEM((3, 1280, 256), BF16), pltpu.VMEM((1024, 256), F32)],
        compiler_params=pltpu.CompilerParams(vmem_limit_bytes=INPUT_LIMIT),
        cost_estimate=pl.CostEstimate(flops=2 * 10**9, bytes_accessed=4 * 10**6, transcendentals=0),
        name=("input_own", "input_above", "input_below")[side],
    )(slots, cotangent, occupancy, weight, *more)


def taps_left(mine, other, step_x, step_y):
    first = step_x * 9 + step_y * 3
    return jnp.concatenate([get_factor(mine, other, first + k) for k in range(3)], axis=1)


def right_kernel(mine, other, corrected, right):
    step = pl.program_id(0)

    @pl.when(step == 0)
    def _():
        right[...] = jnp.zeros_like(right)

    total = jnp.zeros((32, 256), F32)
    for step_y in range(3):
        left_high, left_low = split(taps_left(mine, other, step, step_y))
        high, low = split(corrected[:, 0, step_y].reshape(768, 256))
        both = lax.dot_general(
            jnp.concatenate([left_high, left_low], axis=0), high, NN, preferred_element_type=F32
        )
        total += both[0:32] + both[32:64]
        total += lax.dot_general(left_high, low, NN, preferred_element_type=F32)
    right[...] += total


def along_x(*shape):
    return pl.BlockSpec((3, 1, 3) + shape, lambda step: (0, step, 0, 0, 0))


def right_product(mine, other, corrected):
    return pl.pallas_call(
        right_kernel,
        grid=(3,),
        in_specs=[whole(4, 28, 8, 128), whole(4, 28, 8, 128), along_x(256, 256)],
        out_specs=whole(32, 256),
        out_shape=jax.ShapeDtypeStruct((32, 256), F32),
        compiler_params=pltpu.CompilerParams(vmem_limit_bytes=LATE_LIMIT),
        name="right_product",
    )(mine, other, in_vmem(corrected))


def eliminate(first, work, made):
    places = lax.broadcasted_iota(jnp.int32, (32, 1), 0)
    for step in range(first, first + 16):
        scale = 1.0 / jnp.sqrt(work[step : step + 1, step : step + 1])
        work_row = work[step : step + 1, :] * scale
        made_row = made[step : step + 1, :] * scale
        column = work[:, step : step + 1] * scale
        later = jnp.where(places > step, column, 0.0)
        here = places == step
        work = jnp.where(here, work_row, work - later * work_row)
        made = jnp.where(here, made_row, made - later * made_row)
    return work, made


def first_half_kernel(mine, other, work, made):
    gram = jnp.zeros((32, 32), F32)
    for step in range(9):
        left = jnp.concatenate([get_factor(mine, other, step * 3 + tap) for tap in range(3)], axis=1)
        gram += lax.dot_general(left, left, NT, precision=lax.Precision.HIGHEST, preferred_element_type=F32)
    row = lax.broadcasted_iota(jnp.int32, (32, 32), 0)
    column = lax.broadcasted_iota(jnp.int32, (32, 32), 1)
    work[...], made[...] = eliminate(0, gram, jnp.where(row == column, 1.0, 0.0).astype(F32))


def second_half_kernel(work, made, inverse):
    inverse[...] = eliminate(16, work[...], made[...])[1]


SQUARE = jax.ShapeDtypeStruct((32, 32), F32)


def half_inverse(mine, other):
    return pl.pallas_call(first_half_kernel, out_shape=[SQUARE, SQUARE], compiler_params=SMALL, name="half_inverse")(
        mine, other
    )


def whole_inverse(work, made, tie=None):
    def kernel(work, made, *refs):
        second_half_kernel(work, made, refs[-1])

    more = () if tie is None else (tie,)
    vmem = pl.BlockSpec(memory_space=pltpu.VMEM)
    return pl.pallas_call(
        kernel,
        in_specs=[vmem, vmem] + [pl.BlockSpec(memory_space=pl.ANY)] * len(more),
        out_specs=vmem,
        out_shape=SQUARE,
        compiler_params=SMALL,
        name="whole_inverse",
    )(work, made, *more)


def error_kernel(mine, other, corrected, right, inverse, new_error, q_rows, basis):
    step = pl.program_id(0)

    @pl.when(step == 0)
    def _():
        rows = lax.dot_general(
            inverse[...], right[...], NN, precision=lax.Precision.HIGHEST, preferred_element_type=F32
        ) * (1.0 / 256.0)
        q_rows[...] = rows
        back = lax.dot_general(
            inverse[...].T, rows, NN, precision=lax.Precision.HIGHEST, preferred_element_type=F32
        )
        high, low = split(back)
        basis[0:32, :] = high
        basis[32:64, :] = high
        basis[64:96, :] = low
        basis[96:128, :] = jnp.zeros((32, 256), BF16)

    for step_y in range(3):
        high, low = split(taps_left(mine, other, step, step_y))
        left = jnp.concatenate([high, low, high, jnp.zeros((32, 768), BF16)], axis=0)
        product = lax.dot_general(left, basis[...], TN, preferred_element_type=F32)
        rest = corrected[:, 0, step_y] - product.reshape(3, 256, 256)
        new_error[0, step_y] = rest.astype(BF16)


def remaining_error(mine, other, corrected, right, inverse):
    return pl.pallas_call(
        error_kernel,
        grid=(3,),
        in_specs=[
            whole(4, 28, 8, 128),
            whole(4, 28, 8, 128),
            along_x(256, 256),
            whole(32, 256),
            whole(32, 32),
        ],
        out_specs=[pl.BlockSpec((1, 3, 3, 256, 256), lambda step: (step, 0, 0, 0, 0)), whole(32, 256)],
        out_shape=[jax.ShapeDtypeStruct((3, 3, 3, 256, 256), BF16), jax.ShapeDtypeStruct((32, 256), F32)],
        scratch_shapes=[pltpu.VMEM((128, 256), BF16)],
        compiler_params=pltpu.CompilerParams(vmem_limit_bytes=LATE_LIMIT),
        name="remaining_error",
    )(mine, other, in_vmem(corrected), right, inverse)


CORRECTED = pltpu.VMEM((3, 3, 3, 256, 256), F32)
GRAD_LIMIT = 32 * MIB
OWN_WIDTH = 3
FACES_WIDTH = 3
INPUT_LIMIT = 24 * MIB
LATE_LIMIT = 24 * MIB
SMALL = pltpu.CompilerParams(vmem_limit_bytes=12 * MIB)


def in_vmem(value):
    return pltpu.with_memory_space_constraint(value, pltpu.VMEM)


def in_hbm(value):
    return pltpu.with_memory_space_constraint(value, pltpu.HBM)


def shifted(value, by):
    devices = lax.axis_size("space")
    return lax.ppermute(value, "space", [(i, i + by) for i in range(devices) if 0 <= i + by < devices])


def partners(core=0, x=0, y=0, z=0):
    def place(at_core, at_x, at_y, at_z):
        return (at_y % 2 * 2 + at_core) * 64 + (at_x * 8 + at_z) * 2 + at_y // 2

    return [
        (place(c, i, j, l), place(c ^ core, i ^ x, j ^ y, l ^ z))
        for c in range(2)
        for i in range(4)
        for j in range(4)
        for l in range(8)
    ]


def swapped(value, **bits):
    return lax.ppermute(value, ("dp", "space"), partners(**bits))


def added(values):
    return (values[0] + values[1]) + (values[2] + values[3])


def summed_among(value, steps):
    return added([value] + [swapped(value, **bits) for bits in steps])


ALONG_X = [dict(x=1), dict(x=2), dict(x=3)]
ALONG_Y = [dict(y=1), dict(y=2), dict(y=3)]
ALONG_Z = [dict(z=1), dict(z=2), dict(z=3)]
CORE_AND_Z = [dict(core=1), dict(z=6), dict(core=1, z=6)]


def body(inputs, cotangent, occupancy, neighbours, weight, error_in, q_start):
    field, gradient = inputs[0], cotangent[0]
    occupied, slots = in_hbm(occupancy[0]), in_hbm(neighbours[0])
    weight = weight.reshape(3, 3, 3, 256, 256)
    up, down = brick_faces(field, gradient, occupied)
    lower, upper = shifted(up, 1), shifted(down, -1)
    fixed = (slots, in_hbm(field), in_hbm(gradient), occupied, in_hbm(q_start.T), in_hbm(error_in.reshape(3, 3, 3, 256, 256)))
    corrected, mine, other = local_gradient((0,), *fixed)
    corrected, mine, other = local_gradient((-1, 1), *fixed, lower, upper, in_vmem(corrected), mine, other)

    part = mine + swapped(other, core=1)
    arrived = [swapped(part[k], x=k) for k in (1, 2, 3)]
    total = input_gradient(0, False, slots, gradient, occupied, weight, tie=part)
    part, total = lax.optimization_barrier((added([part[0]] + arrived), total))
    part = part.reshape(4, 7, 8, 128)
    part = added([part[0]] + [swapped(part[k], y=k) for k in (1, 2, 3)])
    arrived = [swapped(part, **bits) for bits in ALONG_Z]
    total = input_gradient(-1, False, slots, gradient, occupied, weight, upper, total, tie=part)
    part, total = lax.optimization_barrier((added([part] + arrived), total))
    part = part + swapped(part, z=6)
    part = jnp.concatenate([part] + [swapped(part, **bits) for bits in ALONG_Y], axis=0)
    arrived = [swapped(part, **bits) for bits in ALONG_X]
    input_grad = input_gradient(1, True, slots, gradient, occupied, weight, lower, total, tie=part)
    mine, input_grad = lax.optimization_barrier((jnp.stack([part] + arrived, axis=0), input_grad))
    other = swapped(mine, core=1)

    right = right_product(mine, other, corrected)
    arrived = [swapped(right, **bits) for bits in CORE_AND_Z]
    halves = half_inverse(mine, other)
    right, *halves = lax.optimization_barrier((added([right] + arrived), *halves))
    arrived = [swapped(right, **bits) for bits in ALONG_X]
    inverse = whole_inverse(*halves, tie=right)
    right, inverse = lax.optimization_barrier((added([right] + arrived), inverse))
    right = summed_among(summed_among(right, ALONG_Y), ALONG_Z)
    new_error, q_rows = remaining_error(mine, other, corrected, right, inverse)
    return (input_grad[None], q_rows.T, new_error.reshape(1, 1, 6912, 256))


def solution(mesh):
    in_specs = (
        P("dp", "space", None, None),
        P("dp", "space", None, None),
        P("dp", "space", None),
        P("dp", "space", None),
        P(),
        P("dp", "space", None, None),
        P(),
    )
    out_specs = (P("dp", "space", None, None), P(), P("dp", "space", None, None))
    return jax.shard_map(body, mesh=mesh, in_specs=in_specs, out_specs=out_specs, check_vma=False)
```

```python
import functools

import jax
import jax.numpy as jnp
from jax import lax
from jax.experimental import pallas as pl
from jax.experimental.pallas import tpu as pltpu
from jax.sharding import PartitionSpec as P

EDGE = 8
PLANE = EDGE * EDGE
F32 = jnp.float32
BF16 = jnp.bfloat16
NT = (((1,), (1,)), ((), ()))
NN = (((1,), (0,)), ((), ()))
TN = (((0,), (0,)), ((), ()))
STEPS = (-1, 0, 1)
MIB = 1024 * 1024


def split(value):
    high = value.astype(BF16)
    low = (value - high.astype(F32)).astype(BF16)
    return high, low


def source_rows(slots, step_x, step_y, step_z, along):
    shape = (128, 1) if along == 0 else (1, 128)
    place = lax.broadcasted_iota(jnp.int32, shape, along)
    brick = place // PLANE
    y = (place // EDGE) % EDGE + step_y
    z = place % EDGE + step_z
    wrapped_y = y % EDGE
    wrapped_z = z % EDGE
    rows = jnp.full(shape, -1, jnp.int32)
    for side_y in sorted({0, step_y}):
        in_y = (y < 0) if side_y < 0 else (y >= EDGE) if side_y > 0 else (y >= 0) & (y < EDGE)
        for side_z in sorted({0, step_z}):
            in_z = (z < 0) if side_z < 0 else (z >= EDGE) if side_z > 0 else (z >= 0) & (z < EDGE)
            if side_z == 0:
                offset = wrapped_y * EDGE + wrapped_z
                first, stride = 0, PLANE
            else:
                offset = wrapped_y
                first, stride = (128 if side_z < 0 else 144), EDGE
            for which in (0, 1):
                slot = slots[which, (step_x + 1) * 9 + (side_y + 1) * 3 + side_z + 1]
                base = jnp.where(slot < 0, -4096, slot * stride + first)
                rows = jnp.where(in_y & in_z & (brick == which), base + offset, rows)
    return rows


def one_hot(rows, along, depth):
    shape = (128, depth) if along == 0 else (depth, 128)
    places = lax.broadcasted_iota(jnp.int32, shape, 1 - along)
    return jnp.where(places == rows, 1.0, 0.0).astype(BF16)


def voxel_mask(occupancy):
    padded = jnp.concatenate([occupancy[...].astype(F32), jnp.zeros((6, 512), F32)], axis=0)
    return padded.T


def own_plane(field, mask, plane):
    rows = slice(plane * PLANE, (plane + 1) * PLANE)
    return jnp.concatenate([field[b, rows, :] * mask[rows, b : b + 1] for b in (0, 1)], axis=0)


def with_faces(own, lower, upper, plane):
    rest = jnp.zeros((96, own.shape[1]), BF16)
    return jnp.concatenate([own, lower[0, plane], upper[0, plane], rest], axis=0)


def coordinates():
    dp, space = lax.axis_index("dp"), lax.axis_index("space")
    return dp % 2, space // 16, (space % 2) * 2 + dp // 2, (space // 2) % 8


def place_of(tap, y):
    return ((tap // 7) ^ y) * 7 + tap % 7


def put_factor(mine, other, tap, value):
    core, x, y, _ = coordinates()
    place = place_of(tap, y)
    halves = value[:, :128], value[:, 128:]
    kept = jnp.where(core == 0, halves[0], halves[1])
    sent = jnp.where(core == 0, halves[1], halves[0])
    for block in range(4):
        rows = slice(block * 8, block * 8 + 8)
        mine[block ^ x, place] = kept[rows]
        other[block ^ x, place] = sent[rows]


def get_factor(mine, other, tap):
    core, x, y, _ = coordinates()
    place = place_of(tap, y)
    own = jnp.concatenate([mine[block ^ x, place] for block in range(4)], axis=0)
    rest = jnp.concatenate([other[block ^ x, place] for block in range(4)], axis=0)
    both = jnp.concatenate([jnp.where(core == 0, own, rest), jnp.where(core == 0, rest, own)], axis=1)
    return both * (1.0 / 256.0)


def whole(*shape):
    return pl.BlockSpec(shape, lambda *step: (0,) * len(shape))


def faces_kernel(field, cotangent, occupancy, up, down):
    mask = voxel_mask(occupancy).astype(BF16)
    row = lax.broadcasted_iota(jnp.int32, (32, 128), 0)
    place = lax.broadcasted_iota(jnp.int32, (32, 128), 1)
    wanted = jnp.where(row < 16, row * EDGE + EDGE - 1, (row - 16) * EDGE)
    picks = jnp.where(place == wanted, 1.0, 0.0).astype(BF16)
    for which, source in enumerate((field, cotangent)):
        for plane in range(EDGE):
            found = lax.dot_general(picks, own_plane(source, mask, plane), NN, preferred_element_type=F32)
            up[which, plane] = found[:16].astype(BF16)
            down[which, plane] = found[16:].astype(BF16)


def brick_faces(field, cotangent, occupancy):
    shape = jax.ShapeDtypeStruct((2, EDGE, 16, 256), BF16)
    return pl.pallas_call(faces_kernel, out_shape=[shape, shape], compiler_params=SMALL, name="brick_faces")(
        in_hbm(field), in_hbm(cotangent), occupancy
    )


def gradient_kernel(sides, width, *refs):
    faces = sides != (0,)
    slots, field, cotangent, occupancy, start, error = refs[:6]
    refs = refs[6:]
    if faces:
        lower, upper, _, _, mine_before, other_before = refs[:6]
        refs = refs[6:]
    kept, sent, mine, other, views, sources, own, start_parts = refs
    core = coordinates()[0]
    step = pl.program_id(0)
    depth = 256 if faces else 128
    shares = 3 // width
    side = step // shares * 2 - 1 if faces else 0

    @pl.when(step == 0)
    def _():
        mask = voxel_mask(occupancy).astype(BF16)
        high, low = split(start[...].T)
        none = jnp.zeros((256, 32), BF16)
        start_parts[0:256, :] = jnp.concatenate([high, low, none, none], axis=1)
        start_parts[256:512, :] = jnp.concatenate([high, none, none, none], axis=1)
        start_parts[512:768, :] = jnp.concatenate([none, none, high, low], axis=1)
        start_parts[768:1024, :] = jnp.concatenate([none, none, high, none], axis=1)
        for plane in range(EDGE):
            own[plane * 128 : (plane + 1) * 128, :] = own_plane(cotangent, mask, plane)
            source = own_plane(field, mask, plane)
            if faces:
                source = with_faces(source, lower, upper, plane)
            sources[plane * 256 : (plane + 1) * 256, :] = source.T
        if faces:
            mine[...] = mine_before[...]
            other[...] = other_before[...]
        else:
            put_factor(mine, other, 27, jnp.zeros((32, 256), F32))

    def gather(groups):
        for first in range(0, len(groups), 2):
            pair = groups[first : first + 2]
            for step_x, left, where in (
                (-1, sources[7 * 256 : 8 * 256, :], 0),
                (0, sources[...], 1),
                (1, sources[0:256, :], 9),
            ):
                picks = jnp.concatenate(
                    [one_hot(source_rows(slots, step_x, y, z, 1), 1, depth) for y, z in pair], axis=1
                )
                found = lax.dot_general(left, picks, NN, preferred_element_type=F32).astype(BF16)
                for member in range(len(pair)):
                    for block in range(left.shape[0] // 256):
                        views[first + member, :, (where + block) * 128 : (where + block + 1) * 128] = found[
                            block * 256 : (block + 1) * 256, member * 128 : (member + 1) * 128
                        ]

    for index in range(len(sides) * shares):
        chosen = STEPS[index % shares * width : index % shares * width + width]

        @pl.when(step == index)
        def _():
            gather([(y, sides[index // shares]) for y in chosen])

    parts = []
    for member in range(width):
        columns = jnp.concatenate([views[member, :, k * 128 : k * 128 + 1024] for k in range(3)], axis=0)
        total = lax.dot_general(columns, own[...], NN, preferred_element_type=F32)
        total = total + error[:, member, 0].astype(F32).reshape(768, 256)
        halves = total.reshape(3, 2, 128, 256)
        kept[0, :, member] = jnp.where(core == 0, halves[:, 0], halves[:, 1])
        sent[0, :, member] = jnp.where(core == 0, halves[:, 1], halves[:, 0])
        high, low = split(total)
        for tap_x in range(3):
            rows = slice(tap_x * 256, tap_x * 256 + 256)
            parts.append((tap_x, member, [high[rows], low[rows]]))
    for first in range(0, 3 * width, 2):
        chosen = parts[first : first + 2]
        left = jnp.concatenate([part for _, _, both in chosen for part in both], axis=1)
        made = lax.dot_general(left, start_parts[0 : left.shape[1], :], NN, preferred_element_type=F32).T
        for slot, (tap_x, member, _) in enumerate(chosen):
            step_y = step % shares * width + member
            rows = made[slot * 64 : slot * 64 + 64]
            put_factor(mine, other, tap_x * 9 + step_y * 3 + side + 1, rows[:32] + rows[32:])


def local_gradient(sides, slots, field, cotangent, occupancy, start, error, *more):
    faces = sides != (0,)
    width = FACES_WIDTH if faces else OWN_WIDTH
    shares = 3 // width

    def which(step):
        return step // shares * 2 if faces else 1

    piece = whole(4, 28, 8, 128)
    face = whole(1, EDGE, 16, 256)
    anywhere = pl.BlockSpec(memory_space=pl.ANY)
    half = pl.BlockSpec((1, 3, width, 128, 256), lambda step: (which(step), 0, step % shares, 0, 0))
    in_specs = [
        pl.BlockSpec(memory_space=pltpu.SMEM),
        whole(2, 512, 256),
        whole(2, 512, 256),
        whole(2, 512),
        whole(32, 256),
        pl.BlockSpec((3, width, 1, 256, 256), lambda step: (0, step % shares, which(step), 0, 0)),
    ]
    if faces:
        in_specs += [face, face, anywhere, anywhere, piece, piece]
    depth = 256 if faces else 128
    return pl.pallas_call(
        functools.partial(gradient_kernel, sides, width),
        grid=(len(sides) * shares,),
        in_specs=in_specs,
        out_specs=[half, half, piece, piece],
        out_shape=[
            HALF,
            HALF,
            jax.ShapeDtypeStruct((4, 28, 8, 128), F32),
            jax.ShapeDtypeStruct((4, 28, 8, 128), F32),
        ],
        input_output_aliases={8: 0, 9: 1} if faces else {},
        scratch_shapes=[
            pltpu.VMEM((width, 256, 1280), BF16),
            pltpu.VMEM((2048, depth), BF16),
            pltpu.VMEM((1024, 256), BF16),
            pltpu.VMEM((1024, 128), BF16),
        ],
        compiler_params=pltpu.CompilerParams(vmem_limit_bytes=GRAD_LIMIT),
        cost_estimate=pl.CostEstimate(
            flops=len(sides) * 2 * 10**9, bytes_accessed=len(sides) * 4 * 10**6, transcendentals=0
        ),
        name="gradient_with_faces" if faces else "gradient_own",
    )(slots, field, cotangent, occupancy, start, error, *more)


def input_kernel(side, last, *refs):
    slots, cotangent, occupancy, weight = refs[:4]
    refs = refs[4:]
    if side:
        face, total_before = refs[:2]
        refs = refs[2:]
    result, views, total = refs[-3:]
    step = pl.program_id(0)

    @pl.when(step == 0)
    def _():
        mask = voxel_mask(occupancy).astype(BF16)
        sources = [own_plane(cotangent, mask, plane) for plane in range(EDGE)]
        if side:
            sources = [with_faces(own, face, face, plane) for plane, own in enumerate(sources)]
        for index, y in enumerate(STEPS):
            picks = [one_hot(source_rows(slots, x, y, -side, 0), 0, 256 if side else 128) for x in STEPS]
            for plane in range(-1, EDGE + 1):
                which = 0 if plane < 0 else 2 if plane >= EDGE else 1
                found = lax.dot_general(picks[which], sources[plane % EDGE], NN, preferred_element_type=F32)
                views[index, (plane + 1) * 128 : (plane + 2) * 128, :] = found.astype(BF16)
        total[...] = total_before[...] if side else jnp.zeros_like(total)

    columns = jnp.concatenate(
        [views[2 - step, (2 - tap_x) * 128 : (2 - tap_x) * 128 + 1024, :] for tap_x in range(3)], axis=1
    )
    weights = jnp.concatenate([weight[tap_x, 0, 0] for tap_x in range(3)], axis=1)
    total[...] += lax.dot_general(columns, weights, NT, preferred_element_type=F32)

    @pl.when(step == 2)
    def _():
        if not last:
            result[...] = total[...]
            return
        mask = voxel_mask(occupancy)
        for plane in range(EDGE):
            for brick in (0, 1):
                first = (2 * plane + brick) * PLANE
                rows = slice(plane * PLANE, (plane + 1) * PLANE)
                kept = total[first : first + PLANE, :] * mask[rows, brick : brick + 1]
                result[brick, rows, :] = kept.astype(BF16)


def input_gradient(side, last, slots, cotangent, occupancy, weight, *more, tie=None):
    in_specs = [
        pl.BlockSpec(memory_space=pltpu.SMEM),
        whole(2, 512, 256),
        whole(2, 512),
        pl.BlockSpec((3, 1, 1, 256, 256), lambda step: (0, step, side + 1, 0, 0)),
    ]
    if side:
        in_specs += [pl.BlockSpec((1, EDGE, 16, 256), lambda step: (1, 0, 0, 0)), whole(1024, 256)]
    if tie is not None:
        in_specs += [pl.BlockSpec(memory_space=pl.ANY)]
        more += (tie,)
    if last:
        shape, spec = jax.ShapeDtypeStruct((2, 512, 256), BF16), whole(2, 512, 256)
    else:
        shape, spec = jax.ShapeDtypeStruct((1024, 256), F32), whole(1024, 256)
    return pl.pallas_call(
        functools.partial(input_kernel, side, last),
        grid=(3,),
        in_specs=in_specs,
        out_specs=spec,
        out_shape=shape,
        scratch_shapes=[pltpu.VMEM((3, 1280, 256), BF16), pltpu.VMEM((1024, 256), F32)],
        compiler_params=pltpu.CompilerParams(vmem_limit_bytes=INPUT_LIMIT),
        cost_estimate=pl.CostEstimate(flops=2 * 10**9, bytes_accessed=4 * 10**6, transcendentals=0),
        name=("input_own", "input_above", "input_below")[side],
    )(slots, cotangent, occupancy, weight, *more)


def taps_left(mine, other, step_x, step_y):
    first = step_x * 9 + step_y * 3
    return jnp.concatenate([get_factor(mine, other, first + k) for k in range(3)], axis=1)


def right_kernel(mine, kept, partner, right):
    step = pl.program_id(0)
    _, x, y, _ = coordinates()

    @pl.when(step == 0)
    def _():
        right[...] = jnp.zeros_like(right)

    total = jnp.zeros((32, 256), F32)
    for step_y in range(3):
        columns = []
        for step_z in range(3):
            place = place_of(step * 9 + step_y * 3 + step_z, y)
            columns.append(jnp.concatenate([mine[block ^ x, place] for block in range(4)], axis=0))
        left_high, left_low = split(jnp.concatenate(columns, axis=1) * (1.0 / 256.0))
        high, low = split((kept[:, 0, step_y] + partner[:, 0, step_y]).reshape(384, 256))
        both = lax.dot_general(
            jnp.concatenate([left_high, left_low], axis=0), high, NN, preferred_element_type=F32
        )
        total += both[0:32] + both[32:64]
        total += lax.dot_general(left_high, low, NN, preferred_element_type=F32)
    right[...] += total


def along_x(*shape):
    return pl.BlockSpec((3, 1, 3) + shape, lambda step: (0, step, 0, 0, 0))


def right_product(mine, kept, partner):
    return pl.pallas_call(
        right_kernel,
        grid=(3,),
        in_specs=[whole(4, 28, 8, 128), along_x(128, 256), along_x(128, 256)],
        out_specs=whole(32, 256),
        out_shape=jax.ShapeDtypeStruct((32, 256), F32),
        compiler_params=pltpu.CompilerParams(vmem_limit_bytes=LATE_LIMIT),
        name="right_product",
    )(mine, in_vmem(kept), in_vmem(partner))


def eliminate(first, work, made):
    places = lax.broadcasted_iota(jnp.int32, (32, 1), 0)
    for step in range(first, first + 16):
        scale = 1.0 / jnp.sqrt(work[step : step + 1, step : step + 1])
        work_row = work[step : step + 1, :] * scale
        made_row = made[step : step + 1, :] * scale
        column = work[:, step : step + 1] * scale
        later = jnp.where(places > step, column, 0.0)
        here = places == step
        work = jnp.where(here, work_row, work - later * work_row)
        made = jnp.where(here, made_row, made - later * made_row)
    return work, made


def first_half_kernel(mine, other, work, made):
    gram = jnp.zeros((32, 32), F32)
    for step in range(9):
        left = jnp.concatenate([get_factor(mine, other, step * 3 + tap) for tap in range(3)], axis=1)
        gram += lax.dot_general(left, left, NT, precision=lax.Precision.HIGHEST, preferred_element_type=F32)
    row = lax.broadcasted_iota(jnp.int32, (32, 32), 0)
    column = lax.broadcasted_iota(jnp.int32, (32, 32), 1)
    work[...], made[...] = eliminate(0, gram, jnp.where(row == column, 1.0, 0.0).astype(F32))


def second_half_kernel(work, made, inverse):
    inverse[...] = eliminate(16, work[...], made[...])[1]


SQUARE = jax.ShapeDtypeStruct((32, 32), F32)


def half_inverse(mine, other):
    return pl.pallas_call(first_half_kernel, out_shape=[SQUARE, SQUARE], compiler_params=SMALL, name="half_inverse")(
        mine, other
    )


def whole_inverse(work, made, tie=None):
    def kernel(work, made, *refs):
        second_half_kernel(work, made, refs[-1])

    more = () if tie is None else (tie,)
    vmem = pl.BlockSpec(memory_space=pltpu.VMEM)
    return pl.pallas_call(
        kernel,
        in_specs=[vmem, vmem] + [pl.BlockSpec(memory_space=pl.ANY)] * len(more),
        out_specs=vmem,
        out_shape=SQUARE,
        compiler_params=SMALL,
        name="whole_inverse",
    )(work, made, *more)


def error_kernel(mine, other, kept, sent, right, inverse, new_error, q_rows, basis):
    step = pl.program_id(0)

    @pl.when(step == 0)
    def _():
        rows = lax.dot_general(
            inverse[...], right[...], NN, precision=lax.Precision.HIGHEST, preferred_element_type=F32
        ) * (1.0 / 256.0)
        q_rows[...] = rows
        back = lax.dot_general(
            inverse[...].T, rows, NN, precision=lax.Precision.HIGHEST, preferred_element_type=F32
        )
        high, low = split(back)
        basis[0:32, :] = high
        basis[32:64, :] = high
        basis[64:96, :] = low
        basis[96:128, :] = jnp.zeros((32, 256), BF16)

    core = coordinates()[0]
    for step_y in range(3):
        high, low = split(taps_left(mine, other, step, step_y))
        left = jnp.concatenate([high, low, high, jnp.zeros((32, 768), BF16)], axis=0)
        product = lax.dot_general(left, basis[...], TN, preferred_element_type=F32)
        product = product.reshape(3, 2, 128, 256)
        own, rest = kept[:, 0, step_y], sent[:, 0, step_y]
        halves = jnp.where(core == 0, own, rest), jnp.where(core == 0, rest, own)
        for half in (0, 1):
            rows = slice(half * 128, half * 128 + 128)
            new_error[0, step_y, :, rows, :] = (halves[half] - product[:, half]).astype(BF16)


def remaining_error(mine, other, kept, sent, right, inverse):
    return pl.pallas_call(
        error_kernel,
        grid=(3,),
        in_specs=[
            whole(4, 28, 8, 128),
            whole(4, 28, 8, 128),
            along_x(128, 256),
            along_x(128, 256),
            whole(32, 256),
            whole(32, 32),
        ],
        out_specs=[pl.BlockSpec((1, 3, 3, 256, 256), lambda step: (step, 0, 0, 0, 0)), whole(32, 256)],
        out_shape=[jax.ShapeDtypeStruct((3, 3, 3, 256, 256), BF16), jax.ShapeDtypeStruct((32, 256), F32)],
        scratch_shapes=[pltpu.VMEM((128, 256), BF16)],
        compiler_params=pltpu.CompilerParams(vmem_limit_bytes=LATE_LIMIT),
        name="remaining_error",
    )(mine, other, in_vmem(kept), in_vmem(sent), right, inverse)


HALF = pltpu.VMEM((3, 3, 3, 128, 256), F32)
GRAD_LIMIT = 32 * MIB
OWN_WIDTH = 3
FACES_WIDTH = 3
INPUT_LIMIT = 24 * MIB
LATE_LIMIT = 24 * MIB
SMALL = pltpu.CompilerParams(vmem_limit_bytes=12 * MIB)


def in_vmem(value):
    return pltpu.with_memory_space_constraint(value, pltpu.VMEM)


def in_hbm(value):
    return pltpu.with_memory_space_constraint(value, pltpu.HBM)


def shifted(value, by):
    devices = lax.axis_size("space")
    return lax.ppermute(value, "space", [(i, i + by) for i in range(devices) if 0 <= i + by < devices])


def partners(core=0, x=0, y=0, z=0):
    def place(at_core, at_x, at_y, at_z):
        return (at_y % 2 * 2 + at_core) * 64 + (at_x * 8 + at_z) * 2 + at_y // 2

    return [
        (place(c, i, j, l), place(c ^ core, i ^ x, j ^ y, l ^ z))
        for c in range(2)
        for i in range(4)
        for j in range(4)
        for l in range(8)
    ]


def swapped(value, **bits):
    return lax.ppermute(value, ("dp", "space"), partners(**bits))


def added(values):
    return (values[0] + values[1]) + (values[2] + values[3])


def summed_among(value, steps):
    return added([value] + [swapped(value, **bits) for bits in steps])


ALONG_X = [dict(x=1), dict(x=2), dict(x=3)]
ALONG_Y = [dict(y=1), dict(y=2), dict(y=3)]
ALONG_Z = [dict(z=1), dict(z=2), dict(z=3)]
CORE_AND_Z = [dict(core=1), dict(z=6), dict(core=1, z=6)]


def body(inputs, cotangent, occupancy, neighbours, weight, error_in, q_start):
    field, gradient = inputs[0], cotangent[0]
    occupied, slots = in_hbm(occupancy[0]), in_hbm(neighbours[0])
    weight = weight.reshape(3, 3, 3, 256, 256)
    up, down = brick_faces(field, gradient, occupied)
    lower, upper = shifted(up, 1), shifted(down, -1)
    fixed = (slots, in_hbm(field), in_hbm(gradient), occupied, in_hbm(q_start.T), in_hbm(error_in.reshape(3, 3, 3, 256, 256)))
    kept, sent, mine, other = local_gradient((0,), *fixed)
    kept, sent, mine, other = local_gradient(
        (-1, 1), *fixed, lower, upper, in_vmem(kept), in_vmem(sent), mine, other
    )

    part = mine + swapped(other, core=1)
    part, travelling = lax.optimization_barrier((part, sent))
    arrived = [swapped(part[k], x=k) for k in (1, 2, 3)]
    partner = swapped(travelling, core=1)
    total = input_gradient(0, False, slots, gradient, occupied, weight, tie=part)
    part, total = lax.optimization_barrier((added([part[0]] + arrived), total))
    part = part.reshape(4, 7, 8, 128)
    part = added([part[0]] + [swapped(part[k], y=k) for k in (1, 2, 3)])
    part = summed_among(part, ALONG_Z)
    arrived = swapped(part, z=6)
    total = input_gradient(-1, False, slots, gradient, occupied, weight, upper, total, tie=part)
    part, total = lax.optimization_barrier((part + arrived, total))
    part = jnp.concatenate([part] + [swapped(part, **bits) for bits in ALONG_Y], axis=0)
    arrived = [swapped(part, **bits) for bits in ALONG_X]
    input_grad = input_gradient(1, True, slots, gradient, occupied, weight, lower, total, tie=part)
    mine, partner, input_grad = lax.optimization_barrier(
        (jnp.stack([part] + arrived, axis=0), partner, input_grad)
    )

    right = right_product(mine, kept, partner)
    right, mine = lax.optimization_barrier((summed_among(right, CORE_AND_Z), mine))
    arrived = [swapped(right, **bits) for bits in ALONG_X]
    other = swapped(mine, core=1)
    right, other = lax.optimization_barrier((added([right] + arrived), other))
    arrived = [swapped(right, **bits) for bits in ALONG_Y]
    halves = half_inverse(mine, other)
    right, *halves = lax.optimization_barrier((added([right] + arrived), *halves))
    arrived = [swapped(right, **bits) for bits in ALONG_Z]
    inverse = whole_inverse(*halves, tie=right)
    right = added([right] + arrived)
    new_error, q_rows = remaining_error(mine, other, kept, sent, right, inverse)
    return (input_grad[None], q_rows.T, new_error.reshape(1, 1, 6912, 256))


def solution(mesh):
    in_specs = (
        P("dp", "space", None, None),
        P("dp", "space", None, None),
        P("dp", "space", None),
        P("dp", "space", None),
        P(),
        P("dp", "space", None, None),
        P(),
    )
    out_specs = (P("dp", "space", None, None), P(), P("dp", "space", None, None))
    return jax.shard_map(body, mesh=mesh, in_specs=in_specs, out_specs=out_specs, check_vma=False)
```

```python
import functools

import jax
import jax.numpy as jnp
from jax import lax
from jax.experimental import pallas as pl
from jax.experimental.pallas import tpu as pltpu
from jax.sharding import PartitionSpec as P

EDGE = 8
PLANE = EDGE * EDGE
F32 = jnp.float32
BF16 = jnp.bfloat16
NT = (((1,), (1,)), ((), ()))
NN = (((1,), (0,)), ((), ()))
TN = (((0,), (0,)), ((), ()))
STEPS = (-1, 0, 1)
MIB = 1024 * 1024


def split(value):
    high = value.astype(BF16)
    low = (value - high.astype(F32)).astype(BF16)
    return high, low


def source_rows(slots, step_x, step_y, step_z, along):
    shape = (128, 1) if along == 0 else (1, 128)
    place = lax.broadcasted_iota(jnp.int32, shape, along)
    brick = place // PLANE
    y = (place // EDGE) % EDGE + step_y
    z = place % EDGE + step_z
    wrapped_y = y % EDGE
    wrapped_z = z % EDGE
    rows = jnp.full(shape, -1, jnp.int32)
    for side_y in sorted({0, step_y}):
        in_y = (y < 0) if side_y < 0 else (y >= EDGE) if side_y > 0 else (y >= 0) & (y < EDGE)
        for side_z in sorted({0, step_z}):
            in_z = (z < 0) if side_z < 0 else (z >= EDGE) if side_z > 0 else (z >= 0) & (z < EDGE)
            if side_z == 0:
                offset = wrapped_y * EDGE + wrapped_z
                first, stride = 0, PLANE
            else:
                offset = wrapped_y
                first, stride = (128 if side_z < 0 else 144), EDGE
            for which in (0, 1):
                slot = slots[which, (step_x + 1) * 9 + (side_y + 1) * 3 + side_z + 1]
                base = jnp.where(slot < 0, -4096, slot * stride + first)
                rows = jnp.where(in_y & in_z & (brick == which), base + offset, rows)
    return rows


def one_hot(rows, along, depth):
    shape = (128, depth) if along == 0 else (depth, 128)
    places = lax.broadcasted_iota(jnp.int32, shape, 1 - along)
    return jnp.where(places == rows, 1.0, 0.0).astype(BF16)


def voxel_mask(occupancy):
    padded = jnp.concatenate([occupancy[...].astype(F32), jnp.zeros((6, 512), F32)], axis=0)
    return padded.T


def own_plane(field, mask, plane):
    rows = slice(plane * PLANE, (plane + 1) * PLANE)
    return jnp.concatenate([field[b, rows, :] * mask[rows, b : b + 1] for b in (0, 1)], axis=0)


def with_faces(own, lower, upper, plane):
    rest = jnp.zeros((96, own.shape[1]), BF16)
    return jnp.concatenate([own, lower[0, plane], upper[0, plane], rest], axis=0)


def coordinates():
    dp, space = lax.axis_index("dp"), lax.axis_index("space")
    return dp % 2, space // 16, (space % 2) * 2 + dp // 2, (space // 2) % 8


def place_of(tap, y):
    return ((tap // 7) ^ y) * 7 + tap % 7


def put_factor(part, tap, value):
    _, x, y, _ = coordinates()
    place = place_of(tap, y)
    for block in range(4):
        part[block ^ x, place] = value[block * 8 : block * 8 + 8]


def get_factor(part, tap):
    _, x, y, _ = coordinates()
    place = place_of(tap, y)
    return jnp.concatenate([part[block ^ x, place] for block in range(4)], axis=0) * (1.0 / 256.0)


def taps_left(part, step_x, step_y):
    first = step_x * 9 + step_y * 3
    return jnp.concatenate([get_factor(part, first + k) for k in range(3)], axis=1)


def on_core(own, given):
    return jnp.where(coordinates()[0] == 0, given, own)


def whole(*shape):
    return pl.BlockSpec(shape, lambda *step: (0,) * len(shape))


FACTOR_SPEC = whole(4, 28, 8, 256)


def faces_kernel(field, cotangent, occupancy, up, down):
    mask = voxel_mask(occupancy).astype(BF16)
    row = lax.broadcasted_iota(jnp.int32, (32, 128), 0)
    place = lax.broadcasted_iota(jnp.int32, (32, 128), 1)
    wanted = jnp.where(row < 16, row * EDGE + EDGE - 1, (row - 16) * EDGE)
    picks = jnp.where(place == wanted, 1.0, 0.0).astype(BF16)
    for which, source in enumerate((field, cotangent)):
        for plane in range(EDGE):
            found = lax.dot_general(picks, own_plane(source, mask, plane), NN, preferred_element_type=F32)
            up[which, plane] = found[:16].astype(BF16)
            down[which, plane] = found[16:].astype(BF16)


def brick_faces(field, cotangent, occupancy):
    shape = jax.ShapeDtypeStruct((2, EDGE, 16, 256), BF16)
    return pl.pallas_call(faces_kernel, out_shape=[shape, shape], compiler_params=SMALL, name="brick_faces")(
        in_hbm(field), in_hbm(cotangent), occupancy
    )


def gradient_kernel(sides, width, *refs):
    faces = sides != (0,)
    slots, field, cotangent, occupancy, start, error = refs[:6]
    refs = refs[6:]
    if faces:
        lower, upper, _, before = refs[:4]
        refs = refs[4:]
    corrected, factor, views, sources, own, start_parts = refs
    step = pl.program_id(0)
    depth = 256 if faces else 128
    shares = 3 // width
    side = step // shares * 2 - 1 if faces else 0

    @pl.when(step == 0)
    def _():
        mask = voxel_mask(occupancy).astype(BF16)
        high, low = split(start[...].T)
        none = jnp.zeros((256, 32), BF16)
        start_parts[0:256, :] = jnp.concatenate([high, low, none, none], axis=1)
        start_parts[256:512, :] = jnp.concatenate([high, none, none, none], axis=1)
        start_parts[512:768, :] = jnp.concatenate([none, none, high, low], axis=1)
        start_parts[768:1024, :] = jnp.concatenate([none, none, high, none], axis=1)
        for plane in range(EDGE):
            own[plane * 128 : (plane + 1) * 128, :] = own_plane(cotangent, mask, plane)
            source = own_plane(field, mask, plane)
            if faces:
                source = with_faces(source, lower, upper, plane)
            sources[plane * 256 : (plane + 1) * 256, :] = source.T
        if faces:
            factor[...] = before[...]
        else:
            put_factor(factor, 27, jnp.zeros((32, 256), F32))

    def gather(groups):
        for first in range(0, len(groups), 2):
            pair = groups[first : first + 2]
            for step_x, left, where in (
                (-1, sources[7 * 256 : 8 * 256, :], 0),
                (0, sources[...], 1),
                (1, sources[0:256, :], 9),
            ):
                picks = jnp.concatenate(
                    [one_hot(source_rows(slots, step_x, y, z, 1), 1, depth) for y, z in pair], axis=1
                )
                found = lax.dot_general(left, picks, NN, preferred_element_type=F32).astype(BF16)
                for member in range(len(pair)):
                    for block in range(left.shape[0] // 256):
                        views[first + member, :, (where + block) * 128 : (where + block + 1) * 128] = found[
                            block * 256 : (block + 1) * 256, member * 128 : (member + 1) * 128
                        ]

    for index in range(len(sides) * shares):
        chosen = STEPS[index % shares * width : index % shares * width + width]

        @pl.when(step == index)
        def _():
            gather([(y, sides[index // shares]) for y in chosen])

    parts = []
    for member in range(width):
        columns = jnp.concatenate([views[member, :, k * 128 : k * 128 + 1024] for k in range(3)], axis=0)
        total = lax.dot_general(columns, own[...], NN, preferred_element_type=F32)
        total = total + error[:, member, 0].astype(F32).reshape(768, 256)
        corrected[0, :, member] = total.reshape(3, 256, 256)
        high, low = split(total)
        for tap_x in range(3):
            rows = slice(tap_x * 256, tap_x * 256 + 256)
            parts.append((tap_x, member, [high[rows], low[rows]]))
    for first in range(0, 3 * width, 2):
        chosen = parts[first : first + 2]
        left = jnp.concatenate([part for _, _, both in chosen for part in both], axis=1)
        made = lax.dot_general(left, start_parts[0 : left.shape[1], :], NN, preferred_element_type=F32).T
        for slot, (tap_x, member, _) in enumerate(chosen):
            step_y = step % shares * width + member
            rows = made[slot * 64 : slot * 64 + 64]
            put_factor(factor, tap_x * 9 + step_y * 3 + side + 1, rows[:32] + rows[32:])


def local_gradient(sides, slots, field, cotangent, occupancy, start, error, *more):
    faces = sides != (0,)
    width = FACES_WIDTH if faces else OWN_WIDTH
    shares = 3 // width

    def which(step):
        return step // shares * 2 if faces else 1

    face = whole(1, EDGE, 16, 256)
    in_specs = [
        pl.BlockSpec(memory_space=pltpu.SMEM),
        whole(2, 512, 256),
        whole(2, 512, 256),
        whole(2, 512),
        whole(32, 256),
        pl.BlockSpec((3, width, 1, 256, 256), lambda step: (0, step % shares, which(step), 0, 0)),
    ]
    if faces:
        in_specs += [face, face, pl.BlockSpec(memory_space=pl.ANY), FACTOR_SPEC]
    depth = 256 if faces else 128
    return pl.pallas_call(
        functools.partial(gradient_kernel, sides, width),
        grid=(len(sides) * shares,),
        in_specs=in_specs,
        out_specs=[
            pl.BlockSpec((1, 3, width, 256, 256), lambda step: (which(step), 0, step % shares, 0, 0)),
            FACTOR_SPEC,
        ],
        out_shape=[CORRECTED, jax.ShapeDtypeStruct((4, 28, 8, 256), F32)],
        input_output_aliases={8: 0} if faces else {},
        scratch_shapes=[
            pltpu.VMEM((width, 256, 1280), BF16),
            pltpu.VMEM((2048, depth), BF16),
            pltpu.VMEM((1024, 256), BF16),
            pltpu.VMEM((1024, 128), BF16),
        ],
        compiler_params=pltpu.CompilerParams(vmem_limit_bytes=GRAD_LIMIT),
        cost_estimate=pl.CostEstimate(
            flops=len(sides) * 2 * 10**9, bytes_accessed=len(sides) * 4 * 10**6, transcendentals=0
        ),
        name="gradient_with_faces" if faces else "gradient_own",
    )(slots, field, cotangent, occupancy, start, error, *more)


def input_kernel(side, last, *refs):
    slots, cotangent, occupancy, weight = refs[:4]
    refs = refs[4:]
    if side:
        face, total_before = refs[:2]
        refs = refs[2:]
    result, views, total = refs[-3:]
    step = pl.program_id(0)

    @pl.when(step == 0)
    def _():
        mask = voxel_mask(occupancy).astype(BF16)
        sources = [own_plane(cotangent, mask, plane) for plane in range(EDGE)]
        if side:
            sources = [with_faces(own, face, face, plane) for plane, own in enumerate(sources)]
        for index, y in enumerate(STEPS):
            picks = [one_hot(source_rows(slots, x, y, -side, 0), 0, 256 if side else 128) for x in STEPS]
            for plane in range(-1, EDGE + 1):
                which = 0 if plane < 0 else 2 if plane >= EDGE else 1
                found = lax.dot_general(picks[which], sources[plane % EDGE], NN, preferred_element_type=F32)
                views[index, (plane + 1) * 128 : (plane + 2) * 128, :] = found.astype(BF16)
        total[...] = total_before[...] if side else jnp.zeros_like(total)

    columns = jnp.concatenate(
        [views[2 - step, (2 - tap_x) * 128 : (2 - tap_x) * 128 + 1024, :] for tap_x in range(3)], axis=1
    )
    weights = jnp.concatenate([weight[tap_x, 0, 0] for tap_x in range(3)], axis=1)
    total[...] += lax.dot_general(columns, weights, NT, preferred_element_type=F32)

    @pl.when(step == 2)
    def _():
        if not last:
            result[...] = total[...]
            return
        mask = voxel_mask(occupancy)
        for plane in range(EDGE):
            for brick in (0, 1):
                first = (2 * plane + brick) * PLANE
                rows = slice(plane * PLANE, (plane + 1) * PLANE)
                kept = total[first : first + PLANE, :] * mask[rows, brick : brick + 1]
                result[brick, rows, :] = kept.astype(BF16)


def input_gradient(side, last, slots, cotangent, occupancy, weight, *more, tie=None):
    in_specs = [
        pl.BlockSpec(memory_space=pltpu.SMEM),
        whole(2, 512, 256),
        whole(2, 512),
        pl.BlockSpec((3, 1, 1, 256, 256), lambda step: (0, step, side + 1, 0, 0)),
    ]
    if side:
        in_specs += [pl.BlockSpec((1, EDGE, 16, 256), lambda step: (1, 0, 0, 0)), whole(1024, 256)]
    if tie is not None:
        in_specs += [pl.BlockSpec(memory_space=pl.ANY)]
        more += (tie,)
    if last:
        shape, spec = jax.ShapeDtypeStruct((2, 512, 256), BF16), whole(2, 512, 256)
    else:
        shape, spec = jax.ShapeDtypeStruct((1024, 256), F32), whole(1024, 256)
    return pl.pallas_call(
        functools.partial(input_kernel, side, last),
        grid=(3,),
        in_specs=in_specs,
        out_specs=spec,
        out_shape=shape,
        scratch_shapes=[pltpu.VMEM((3, 1280, 256), BF16), pltpu.VMEM((1024, 256), F32)],
        compiler_params=pltpu.CompilerParams(vmem_limit_bytes=INPUT_LIMIT),
        cost_estimate=pl.CostEstimate(flops=2 * 10**9, bytes_accessed=4 * 10**6, transcendentals=0),
        name=("input_own", "input_above", "input_below")[side],
    )(slots, cotangent, occupancy, weight, *more)


def right_kernel(part, corrected, partner, right):
    step = pl.program_id(0)

    @pl.when(step == 0)
    def _():
        right[...] = jnp.zeros_like(right)

    total = jnp.zeros((32, 256), F32)
    for step_y in range(3):
        left_high, left_low = split(taps_left(part, step, step_y))
        high, low = split((corrected[:, 0, step_y] + partner[:, 0, step_y]).reshape(768, 256))
        both = lax.dot_general(
            jnp.concatenate([left_high, left_low], axis=0), high, NN, preferred_element_type=F32
        )
        total += both[0:32] + both[32:64]
        total += lax.dot_general(left_high, low, NN, preferred_element_type=F32)
    right[...] += total


def along_x(*shape):
    return pl.BlockSpec((3, 1, 3) + shape, lambda step: (0, step, 0, 0, 0))


def right_product(part, corrected, partner):
    return pl.pallas_call(
        right_kernel,
        grid=(3,),
        in_specs=[FACTOR_SPEC, along_x(256, 256), along_x(256, 256)],
        out_specs=whole(32, 256),
        out_shape=jax.ShapeDtypeStruct((32, 256), F32),
        compiler_params=pltpu.CompilerParams(vmem_limit_bytes=LATE_LIMIT),
        name="right_product",
    )(part, in_vmem(corrected), in_vmem(partner))


def eliminate(first, work, made):
    places = lax.broadcasted_iota(jnp.int32, (32, 1), 0)
    for step in range(first, first + 16):
        scale = 1.0 / jnp.sqrt(work[step : step + 1, step : step + 1])
        work_row = work[step : step + 1, :] * scale
        made_row = made[step : step + 1, :] * scale
        column = work[:, step : step + 1] * scale
        later = jnp.where(places > step, column, 0.0)
        here = places == step
        work = jnp.where(here, work_row, work - later * work_row)
        made = jnp.where(here, made_row, made - later * made_row)
    return work, made


def first_half_kernel(part, given, work, made):
    gram = jnp.zeros((32, 32), F32)
    for step in range(9):
        left = on_core(taps_left(part, step // 3, step % 3), taps_left(given, step // 3, step % 3))
        gram += lax.dot_general(left, left, NT, precision=lax.Precision.HIGHEST, preferred_element_type=F32)
    row = lax.broadcasted_iota(jnp.int32, (32, 32), 0)
    column = lax.broadcasted_iota(jnp.int32, (32, 32), 1)
    work[...], made[...] = eliminate(0, gram, jnp.where(row == column, 1.0, 0.0).astype(F32))


def second_half_kernel(work, made, inverse):
    inverse[...] = eliminate(16, work[...], made[...])[1]


SQUARE = jax.ShapeDtypeStruct((32, 32), F32)


def half_inverse(part, given):
    return pl.pallas_call(first_half_kernel, out_shape=[SQUARE, SQUARE], compiler_params=SMALL, name="half_inverse")(
        part, given
    )


def whole_inverse(work, made, tie=None):
    def kernel(work, made, *refs):
        second_half_kernel(work, made, refs[-1])

    more = () if tie is None else (tie,)
    vmem = pl.BlockSpec(memory_space=pltpu.VMEM)
    return pl.pallas_call(
        kernel,
        in_specs=[vmem, vmem] + [pl.BlockSpec(memory_space=pl.ANY)] * len(more),
        out_specs=vmem,
        out_shape=SQUARE,
        compiler_params=SMALL,
        name="whole_inverse",
    )(work, made, *more)


def error_kernel(part, given, corrected, right, right_given, inverse, new_error, q_rows, basis):
    step = pl.program_id(0)

    @pl.when(step == 0)
    def _():
        rows = lax.dot_general(
            inverse[...], on_core(right[...], right_given[...]), NN, precision=lax.Precision.HIGHEST, preferred_element_type=F32
        ) * (1.0 / 256.0)
        q_rows[...] = rows
        back = lax.dot_general(
            inverse[...].T, rows, NN, precision=lax.Precision.HIGHEST, preferred_element_type=F32
        )
        high, low = split(back)
        basis[0:32, :] = high
        basis[32:64, :] = high
        basis[64:96, :] = low
        basis[96:128, :] = jnp.zeros((32, 256), BF16)

    for step_y in range(3):
        high, low = split(on_core(taps_left(part, step, step_y), taps_left(given, step, step_y)))
        left = jnp.concatenate([high, low, high, jnp.zeros((32, 768), BF16)], axis=0)
        product = lax.dot_general(left, basis[...], TN, preferred_element_type=F32)
        rest = corrected[:, 0, step_y] - product.reshape(3, 256, 256)
        new_error[0, step_y] = rest.astype(BF16)


def remaining_error(part, given, corrected, right, right_given, inverse):
    return pl.pallas_call(
        error_kernel,
        grid=(3,),
        in_specs=[
            FACTOR_SPEC,
            FACTOR_SPEC,
            along_x(256, 256),
            whole(32, 256),
            whole(32, 256),
            whole(32, 32),
        ],
        out_specs=[pl.BlockSpec((1, 3, 3, 256, 256), lambda step: (step, 0, 0, 0, 0)), whole(32, 256)],
        out_shape=[jax.ShapeDtypeStruct((3, 3, 3, 256, 256), BF16), jax.ShapeDtypeStruct((32, 256), F32)],
        scratch_shapes=[pltpu.VMEM((128, 256), BF16)],
        compiler_params=pltpu.CompilerParams(vmem_limit_bytes=LATE_LIMIT),
        name="remaining_error",
    )(part, given, in_vmem(corrected), right, right_given, inverse)


CORRECTED = pltpu.VMEM((3, 3, 3, 256, 256), F32)
GRAD_LIMIT = 32 * MIB
OWN_WIDTH = 3
FACES_WIDTH = 3
INPUT_LIMIT = 24 * MIB
LATE_LIMIT = 24 * MIB
SMALL = pltpu.CompilerParams(vmem_limit_bytes=12 * MIB)


def in_vmem(value):
    return pltpu.with_memory_space_constraint(value, pltpu.VMEM)


def in_hbm(value):
    return pltpu.with_memory_space_constraint(value, pltpu.HBM)


def shifted(value, by):
    devices = lax.axis_size("space")
    return lax.ppermute(value, "space", [(i, i + by) for i in range(devices) if 0 <= i + by < devices])


def place(core, x, y, z):
    return (y % 2 * 2 + core) * 64 + (x * 8 + z) * 2 + y // 2


def swapped(value, x=0, y=0, z=0):
    chips = [(i, j, k) for i in range(4) for j in range(4) for k in range(8)]
    pairs = [(place(1, i, j, k), place(1, i ^ x, j ^ y, k ^ z)) for i, j, k in chips]
    return lax.ppermute(value, ("dp", "space"), pairs)


def handed(value, to):
    chips = [(i, j, k) for i in range(4) for j in range(4) for k in range(8)]
    pairs = [(place(1 - to, *chip), place(to, *chip)) for chip in chips]
    return lax.ppermute(value, ("dp", "space"), pairs)


def added(values):
    return (values[0] + values[1]) + (values[2] + values[3])


def summed_among(value, steps):
    return added([value] + [swapped(value, **bits) for bits in steps])


ALONG_X = [dict(x=1), dict(x=2), dict(x=3)]
ALONG_Y = [dict(y=1), dict(y=2), dict(y=3)]
ALONG_Z = [dict(z=1), dict(z=2), dict(z=3)]


def body(inputs, cotangent, occupancy, neighbours, weight, error_in, q_start):
    field, gradient = inputs[0], cotangent[0]
    occupied, slots = in_hbm(occupancy[0]), in_hbm(neighbours[0])
    weight = weight.reshape(3, 3, 3, 256, 256)
    up, down = brick_faces(field, gradient, occupied)
    lower, upper = shifted(up, 1), shifted(down, -1)
    fixed = (slots, in_hbm(field), in_hbm(gradient), occupied, in_hbm(q_start.T), in_hbm(error_in.reshape(3, 3, 3, 256, 256)))
    corrected, factor = local_gradient((0,), *fixed)
    corrected, factor = local_gradient((-1, 1), *fixed, lower, upper, in_vmem(corrected), factor)

    part = factor + handed(factor, to=1)
    part, travelling = lax.optimization_barrier((part, corrected))
    arrived = [swapped(part[k], x=k) for k in (1, 2, 3)]
    partner = handed(travelling, to=1)
    total = input_gradient(0, False, slots, gradient, occupied, weight, tie=part)
    part, total = lax.optimization_barrier((added([part[0]] + arrived), total))
    part = part.reshape(4, 7, 8, 256)
    part = added([part[0]] + [swapped(part[k], y=k) for k in (1, 2, 3)])
    part = summed_among(part, ALONG_Z)
    arrived = swapped(part, z=6)
    total = input_gradient(-1, False, slots, gradient, occupied, weight, upper, total, tie=part)
    part, total = lax.optimization_barrier((part + arrived, total))
    part = jnp.concatenate([part] + [swapped(part, **bits) for bits in ALONG_Y], axis=0)
    arrived = [swapped(part, **bits) for bits in ALONG_X]
    input_grad = input_gradient(1, True, slots, gradient, occupied, weight, lower, total, tie=part)
    part, partner, input_grad = lax.optimization_barrier(
        (jnp.stack([part] + arrived, axis=0), partner, input_grad)
    )

    right = right_product(part, corrected, partner)
    right, part = lax.optimization_barrier((summed_among(right, ALONG_X), part))
    arrived = [swapped(right, **bits) for bits in ALONG_Y]
    given = handed(part, to=0)
    right, given = lax.optimization_barrier((added([right] + arrived), given))
    arrived = [swapped(right, **bits) for bits in ALONG_Z]
    halves = half_inverse(part, given)
    right, *halves = lax.optimization_barrier((added([right] + arrived), *halves))
    arrived = swapped(right, z=6)
    inverse = whole_inverse(*halves, tie=right)
    right, inverse = lax.optimization_barrier((right + arrived, inverse))
    right_given = handed(right, to=0)
    new_error, q_rows = remaining_error(part, given, corrected, right, right_given, inverse)
    return (input_grad[None], q_rows.T, new_error.reshape(1, 1, 6912, 256))


def solution(mesh):
    in_specs = (
        P("dp", "space", None, None),
        P("dp", "space", None, None),
        P("dp", "space", None),
        P("dp", "space", None),
        P(),
        P("dp", "space", None, None),
        P(),
    )
    out_specs = (P("dp", "space", None, None), P(), P("dp", "space", None, None))
    return jax.shard_map(body, mesh=mesh, in_specs=in_specs, out_specs=out_specs, check_vma=False)
```

```python
import functools

import jax
import jax.numpy as jnp
from jax import lax
from jax.experimental import pallas as pl
from jax.experimental.pallas import tpu as pltpu
from jax.sharding import PartitionSpec as P

EDGE = 8
PLANE = EDGE * EDGE
F32 = jnp.float32
BF16 = jnp.bfloat16
NT = (((1,), (1,)), ((), ()))
NN = (((1,), (0,)), ((), ()))
TN = (((0,), (0,)), ((), ()))
STEPS = (-1, 0, 1)
MIB = 1024 * 1024


def split(value):
    high = value.astype(BF16)
    low = (value - high.astype(F32)).astype(BF16)
    return high, low


def source_rows(slots, step_x, step_y, step_z, along):
    shape = (128, 1) if along == 0 else (1, 128)
    place = lax.broadcasted_iota(jnp.int32, shape, along)
    brick = place // PLANE
    y = (place // EDGE) % EDGE + step_y
    z = place % EDGE + step_z
    wrapped_y = y % EDGE
    wrapped_z = z % EDGE
    rows = jnp.full(shape, -1, jnp.int32)
    for side_y in sorted({0, step_y}):
        in_y = (y < 0) if side_y < 0 else (y >= EDGE) if side_y > 0 else (y >= 0) & (y < EDGE)
        for side_z in sorted({0, step_z}):
            in_z = (z < 0) if side_z < 0 else (z >= EDGE) if side_z > 0 else (z >= 0) & (z < EDGE)
            if side_z == 0:
                offset = wrapped_y * EDGE + wrapped_z
                first, stride = 0, PLANE
            else:
                offset = wrapped_y
                first, stride = (128 if side_z < 0 else 144), EDGE
            for which in (0, 1):
                slot = slots[which, (step_x + 1) * 9 + (side_y + 1) * 3 + side_z + 1]
                if side_z:
                    end = 0 if side_z < 0 else lax.axis_size("space") - 1
                    slot = jnp.where(lax.axis_index("space") == end, -1, slot)
                base = jnp.where(slot < 0, -4096, slot * stride + first)
                rows = jnp.where(in_y & in_z & (brick == which), base + offset, rows)
    return rows


def one_hot(rows, along, depth):
    shape = (128, depth) if along == 0 else (depth, 128)
    places = lax.broadcasted_iota(jnp.int32, shape, 1 - along)
    return jnp.where(places == rows, 1.0, 0.0).astype(BF16)


def voxel_mask(occupancy):
    padded = jnp.concatenate([occupancy[...].astype(F32), jnp.zeros((6, 512), F32)], axis=0)
    return padded.T


def own_plane(field, mask, plane):
    rows = slice(plane * PLANE, (plane + 1) * PLANE)
    return jnp.concatenate([field[b, rows, :] * mask[rows, b : b + 1] for b in (0, 1)], axis=0)


def with_faces(own, lower, upper, plane):
    rest = jnp.zeros((96, own.shape[1]), BF16)
    return jnp.concatenate([own, lower[0, plane], upper[0, plane], rest], axis=0)


def coordinates():
    dp, space = lax.axis_index("dp"), lax.axis_index("space")
    return dp % 2, space // 16, (space % 2) * 2 + dp // 2, (space // 2) % 8


def place_of(tap, y):
    return ((tap // 7) ^ y) * 7 + tap % 7


def put_factor(part, tap, value):
    _, x, y, _ = coordinates()
    place = place_of(tap, y)
    for block in range(4):
        part[block ^ x, place] = value[block * 8 : block * 8 + 8]


def get_factor(part, tap):
    _, x, y, _ = coordinates()
    place = place_of(tap, y)
    return jnp.concatenate([part[block ^ x, place] for block in range(4)], axis=0) * (1.0 / 256.0)


def taps_left(part, step_x, step_y):
    first = step_x * 9 + step_y * 3
    return jnp.concatenate([get_factor(part, first + k) for k in range(3)], axis=1)


def on_core(own, given):
    return jnp.where(coordinates()[0] == 0, given, own)


def whole(*shape):
    return pl.BlockSpec(shape, lambda *step: (0,) * len(shape))


FACTOR_SPEC = whole(4, 28, 8, 256)


def faces_kernel(field, cotangent, occupancy, up, down):
    mask = voxel_mask(occupancy).astype(BF16)
    row = lax.broadcasted_iota(jnp.int32, (32, 128), 0)
    place = lax.broadcasted_iota(jnp.int32, (32, 128), 1)
    wanted = jnp.where(row < 16, row * EDGE + EDGE - 1, (row - 16) * EDGE)
    picks = jnp.where(place == wanted, 1.0, 0.0).astype(BF16)
    for which, source in enumerate((field, cotangent)):
        for plane in range(EDGE):
            found = lax.dot_general(picks, own_plane(source, mask, plane), NN, preferred_element_type=F32)
            up[which, plane] = found[:16].astype(BF16)
            down[which, plane] = found[16:].astype(BF16)


def brick_faces(field, cotangent, occupancy):
    shape = jax.ShapeDtypeStruct((2, EDGE, 16, 256), BF16)
    return pl.pallas_call(faces_kernel, out_shape=[shape, shape], compiler_params=SMALL, name="brick_faces")(
        in_hbm(field), in_hbm(cotangent), occupancy
    )


def gradient_kernel(sides, width, *refs):
    faces = sides != (0,)
    slots, field, cotangent, occupancy, start, error = refs[:6]
    refs = refs[6:]
    if faces:
        lower, upper, _, before = refs[:4]
        refs = refs[4:]
    corrected, factor, views, sources, own, start_parts = refs
    step = pl.program_id(0)
    depth = 256 if faces else 128
    shares = 3 // width
    side = step // shares * 2 - 1 if faces else 0

    @pl.when(step == 0)
    def _():
        mask = voxel_mask(occupancy).astype(BF16)
        high, low = split(start[...].T)
        none = jnp.zeros((256, 32), BF16)
        start_parts[0:256, :] = jnp.concatenate([high, low, none, none], axis=1)
        start_parts[256:512, :] = jnp.concatenate([high, none, none, none], axis=1)
        start_parts[512:768, :] = jnp.concatenate([none, none, high, low], axis=1)
        start_parts[768:1024, :] = jnp.concatenate([none, none, high, none], axis=1)
        for plane in range(EDGE):
            own[plane * 128 : (plane + 1) * 128, :] = own_plane(cotangent, mask, plane)
            source = own_plane(field, mask, plane)
            if faces:
                source = with_faces(source, lower, upper, plane)
            sources[plane * 256 : (plane + 1) * 256, :] = source.T
        if faces:
            factor[...] = before[...]
        else:
            put_factor(factor, 27, jnp.zeros((32, 256), F32))

    def gather(groups):
        for first in range(0, len(groups), 2):
            pair = groups[first : first + 2]
            for step_x, left, where in (
                (-1, sources[7 * 256 : 8 * 256, :], 0),
                (0, sources[...], 1),
                (1, sources[0:256, :], 9),
            ):
                picks = jnp.concatenate(
                    [one_hot(source_rows(slots, step_x, y, z, 1), 1, depth) for y, z in pair], axis=1
                )
                found = lax.dot_general(left, picks, NN, preferred_element_type=F32).astype(BF16)
                for member in range(len(pair)):
                    for block in range(left.shape[0] // 256):
                        views[first + member, :, (where + block) * 128 : (where + block + 1) * 128] = found[
                            block * 256 : (block + 1) * 256, member * 128 : (member + 1) * 128
                        ]

    for index in range(len(sides) * shares):
        chosen = STEPS[index % shares * width : index % shares * width + width]

        @pl.when(step == index)
        def _():
            gather([(y, sides[index // shares]) for y in chosen])

    parts = []
    for member in range(width):
        columns = jnp.concatenate([views[member, :, k * 128 : k * 128 + 1024] for k in range(3)], axis=0)
        total = lax.dot_general(columns, own[...], NN, preferred_element_type=F32)
        total = total + error[:, member, 0].astype(F32).reshape(768, 256)
        corrected[0, :, member] = total.reshape(3, 256, 256)
        high, low = split(total)
        for tap_x in range(3):
            rows = slice(tap_x * 256, tap_x * 256 + 256)
            parts.append((tap_x, member, [high[rows], low[rows]]))
    for first in range(0, 3 * width, 2):
        chosen = parts[first : first + 2]
        left = jnp.concatenate([part for _, _, both in chosen for part in both], axis=1)
        made = lax.dot_general(left, start_parts[0 : left.shape[1], :], NN, preferred_element_type=F32).T
        for slot, (tap_x, member, _) in enumerate(chosen):
            step_y = step % shares * width + member
            rows = made[slot * 64 : slot * 64 + 64]
            put_factor(factor, tap_x * 9 + step_y * 3 + side + 1, rows[:32] + rows[32:])


def local_gradient(sides, slots, field, cotangent, occupancy, start, error, *more):
    faces = sides != (0,)
    width = FACES_WIDTH if faces else OWN_WIDTH
    shares = 3 // width

    def which(step):
        return step // shares * 2 if faces else 1

    face = whole(1, EDGE, 16, 256)
    in_specs = [
        pl.BlockSpec(memory_space=pltpu.SMEM),
        whole(2, 512, 256),
        whole(2, 512, 256),
        whole(2, 512),
        whole(32, 256),
        pl.BlockSpec((3, width, 1, 256, 256), lambda step: (0, step % shares, which(step), 0, 0)),
    ]
    if faces:
        in_specs += [face, face, pl.BlockSpec(memory_space=pl.ANY), FACTOR_SPEC]
    depth = 256 if faces else 128
    return pl.pallas_call(
        functools.partial(gradient_kernel, sides, width),
        grid=(len(sides) * shares,),
        in_specs=in_specs,
        out_specs=[
            pl.BlockSpec((1, 3, width, 256, 256), lambda step: (which(step), 0, step % shares, 0, 0)),
            FACTOR_SPEC,
        ],
        out_shape=[CORRECTED, jax.ShapeDtypeStruct((4, 28, 8, 256), F32)],
        input_output_aliases={8: 0} if faces else {},
        scratch_shapes=[
            pltpu.VMEM((width, 256, 1280), BF16),
            pltpu.VMEM((2048, depth), BF16),
            pltpu.VMEM((1024, 256), BF16),
            pltpu.VMEM((1024, 128), BF16),
        ],
        compiler_params=pltpu.CompilerParams(vmem_limit_bytes=GRAD_LIMIT),
        cost_estimate=pl.CostEstimate(
            flops=len(sides) * 2 * 10**9, bytes_accessed=len(sides) * 4 * 10**6, transcendentals=0
        ),
        name="gradient_with_faces" if faces else "gradient_own",
    )(slots, field, cotangent, occupancy, start, error, *more)


def input_kernel(side, last, *refs):
    slots, cotangent, occupancy, weight = refs[:4]
    refs = refs[4:]
    if side:
        face, total_before = refs[:2]
        refs = refs[2:]
    result, views, total = refs[-3:]
    step = pl.program_id(0)

    @pl.when(step == 0)
    def _():
        mask = voxel_mask(occupancy).astype(BF16)
        sources = [own_plane(cotangent, mask, plane) for plane in range(EDGE)]
        if side:
            sources = [with_faces(own, face, face, plane) for plane, own in enumerate(sources)]
        for index, y in enumerate(STEPS):
            picks = [one_hot(source_rows(slots, x, y, -side, 0), 0, 256 if side else 128) for x in STEPS]
            for plane in range(-1, EDGE + 1):
                which = 0 if plane < 0 else 2 if plane >= EDGE else 1
                found = lax.dot_general(picks[which], sources[plane % EDGE], NN, preferred_element_type=F32)
                views[index, (plane + 1) * 128 : (plane + 2) * 128, :] = found.astype(BF16)
        total[...] = total_before[...] if side else jnp.zeros_like(total)

    columns = jnp.concatenate(
        [views[2 - step, (2 - tap_x) * 128 : (2 - tap_x) * 128 + 1024, :] for tap_x in range(3)], axis=1
    )
    weights = jnp.concatenate([weight[tap_x, 0, 0] for tap_x in range(3)], axis=1)
    total[...] += lax.dot_general(columns, weights, NT, preferred_element_type=F32)

    @pl.when(step == 2)
    def _():
        if not last:
            result[...] = total[...]
            return
        mask = voxel_mask(occupancy)
        for plane in range(EDGE):
            for brick in (0, 1):
                first = (2 * plane + brick) * PLANE
                rows = slice(plane * PLANE, (plane + 1) * PLANE)
                kept = total[first : first + PLANE, :] * mask[rows, brick : brick + 1]
                result[brick, rows, :] = kept.astype(BF16)


def input_gradient(side, last, slots, cotangent, occupancy, weight, *more, tie=None):
    in_specs = [
        pl.BlockSpec(memory_space=pltpu.SMEM),
        whole(2, 512, 256),
        whole(2, 512),
        pl.BlockSpec((3, 1, 1, 256, 256), lambda step: (0, step, side + 1, 0, 0)),
    ]
    if side:
        in_specs += [pl.BlockSpec((1, EDGE, 16, 256), lambda step: (1, 0, 0, 0)), whole(1024, 256)]
    if tie is not None:
        in_specs += [pl.BlockSpec(memory_space=pl.ANY)]
        more += (tie,)
    if last:
        shape, spec = jax.ShapeDtypeStruct((2, 512, 256), BF16), whole(2, 512, 256)
    else:
        shape, spec = jax.ShapeDtypeStruct((1024, 256), F32), whole(1024, 256)
    return pl.pallas_call(
        functools.partial(input_kernel, side, last),
        grid=(3,),
        in_specs=in_specs,
        out_specs=spec,
        out_shape=shape,
        scratch_shapes=[pltpu.VMEM((3, 1280, 256), BF16), pltpu.VMEM((1024, 256), F32)],
        compiler_params=pltpu.CompilerParams(vmem_limit_bytes=INPUT_LIMIT),
        cost_estimate=pl.CostEstimate(flops=2 * 10**9, bytes_accessed=4 * 10**6, transcendentals=0),
        name=("input_own", "input_above", "input_below")[side],
    )(slots, cotangent, occupancy, weight, *more)


def right_kernel(part, corrected, partner, right):
    step = pl.program_id(0)

    @pl.when(step == 0)
    def _():
        right[...] = jnp.zeros_like(right)

    total = jnp.zeros((32, 256), F32)
    for step_y in range(3):
        left_high, left_low = split(taps_left(part, step, step_y))
        high, low = split((corrected[:, 0, step_y] + partner[:, 0, step_y]).reshape(768, 256))
        both = lax.dot_general(
            jnp.concatenate([left_high, left_low], axis=0), high, NN, preferred_element_type=F32
        )
        total += both[0:32] + both[32:64]
        total += lax.dot_general(left_high, low, NN, preferred_element_type=F32)
    right[...] += total


def along_x(*shape):
    return pl.BlockSpec((3, 1, 3) + shape, lambda step: (0, step, 0, 0, 0))


def right_product(part, corrected, partner):
    return pl.pallas_call(
        right_kernel,
        grid=(3,),
        in_specs=[FACTOR_SPEC, along_x(256, 256), along_x(256, 256)],
        out_specs=whole(32, 256),
        out_shape=jax.ShapeDtypeStruct((32, 256), F32),
        compiler_params=pltpu.CompilerParams(vmem_limit_bytes=LATE_LIMIT),
        name="right_product",
    )(part, in_vmem(corrected), in_vmem(partner))


def eliminate(first, work, made):
    places = lax.broadcasted_iota(jnp.int32, (32, 1), 0)
    for step in range(first, first + 16):
        scale = 1.0 / jnp.sqrt(work[step : step + 1, step : step + 1])
        work_row = work[step : step + 1, :] * scale
        made_row = made[step : step + 1, :] * scale
        column = work[:, step : step + 1] * scale
        later = jnp.where(places > step, column, 0.0)
        here = places == step
        work = jnp.where(here, work_row, work - later * work_row)
        made = jnp.where(here, made_row, made - later * made_row)
    return work, made


def first_half_kernel(part, given, work, made):
    gram = jnp.zeros((32, 32), F32)
    for step in range(9):
        left = on_core(taps_left(part, step // 3, step % 3), taps_left(given, step // 3, step % 3))
        gram += lax.dot_general(left, left, NT, precision=lax.Precision.HIGHEST, preferred_element_type=F32)
    row = lax.broadcasted_iota(jnp.int32, (32, 32), 0)
    column = lax.broadcasted_iota(jnp.int32, (32, 32), 1)
    work[...], made[...] = eliminate(0, gram, jnp.where(row == column, 1.0, 0.0).astype(F32))


def second_half_kernel(work, made, inverse):
    inverse[...] = eliminate(16, work[...], made[...])[1]


SQUARE = jax.ShapeDtypeStruct((32, 32), F32)


def half_inverse(part, given):
    return pl.pallas_call(first_half_kernel, out_shape=[SQUARE, SQUARE], compiler_params=SMALL, name="half_inverse")(
        part, given
    )


def whole_inverse(work, made, tie=None):
    def kernel(work, made, *refs):
        second_half_kernel(work, made, refs[-1])

    more = () if tie is None else (tie,)
    vmem = pl.BlockSpec(memory_space=pltpu.VMEM)
    return pl.pallas_call(
        kernel,
        in_specs=[vmem, vmem] + [pl.BlockSpec(memory_space=pl.ANY)] * len(more),
        out_specs=vmem,
        out_shape=SQUARE,
        compiler_params=SMALL,
        name="whole_inverse",
    )(work, made, *more)


def error_kernel(part, given, corrected, right, right_given, inverse, new_error, q_rows, basis):
    step = pl.program_id(0)

    @pl.when(step == 0)
    def _():
        rows = lax.dot_general(
            inverse[...], on_core(right[...], right_given[...]), NN, precision=lax.Precision.HIGHEST, preferred_element_type=F32
        ) * (1.0 / 256.0)
        q_rows[...] = rows
        back = lax.dot_general(
            inverse[...].T, rows, NN, precision=lax.Precision.HIGHEST, preferred_element_type=F32
        )
        high, low = split(back)
        basis[0:32, :] = high
        basis[32:64, :] = high
        basis[64:96, :] = low
        basis[96:128, :] = jnp.zeros((32, 256), BF16)

    for step_y in range(3):
        high, low = split(on_core(taps_left(part, step, step_y), taps_left(given, step, step_y)))
        left = jnp.concatenate([high, low, high, jnp.zeros((32, 768), BF16)], axis=0)
        product = lax.dot_general(left, basis[...], TN, preferred_element_type=F32)
        rest = corrected[:, 0, step_y] - product.reshape(3, 256, 256)
        new_error[0, step_y] = rest.astype(BF16)


def remaining_error(part, given, corrected, right, right_given, inverse):
    return pl.pallas_call(
        error_kernel,
        grid=(3,),
        in_specs=[
            FACTOR_SPEC,
            FACTOR_SPEC,
            along_x(256, 256),
            whole(32, 256),
            whole(32, 256),
            whole(32, 32),
        ],
        out_specs=[pl.BlockSpec((1, 3, 3, 256, 256), lambda step: (step, 0, 0, 0, 0)), whole(32, 256)],
        out_shape=[jax.ShapeDtypeStruct((3, 3, 3, 256, 256), BF16), jax.ShapeDtypeStruct((32, 256), F32)],
        scratch_shapes=[pltpu.VMEM((128, 256), BF16)],
        compiler_params=pltpu.CompilerParams(vmem_limit_bytes=LATE_LIMIT),
        name="remaining_error",
    )(part, given, in_vmem(corrected), right, right_given, inverse)


CORRECTED = pltpu.VMEM((3, 3, 3, 256, 256), F32)
GRAD_LIMIT = 32 * MIB
OWN_WIDTH = 3
FACES_WIDTH = 3
INPUT_LIMIT = 24 * MIB
LATE_LIMIT = 24 * MIB
SMALL = pltpu.CompilerParams(vmem_limit_bytes=12 * MIB)


def in_vmem(value):
    return pltpu.with_memory_space_constraint(value, pltpu.VMEM)


def in_hbm(value):
    return pltpu.with_memory_space_constraint(value, pltpu.HBM)


def shifted(value, by):
    devices = lax.axis_size("space")
    return lax.ppermute(value, "space", [(i, (i + by) % devices) for i in range(devices)])


def place(core, x, y, z):
    return (y % 2 * 2 + core) * 64 + (x * 8 + z) * 2 + y // 2


CHIPS = [(x, y, z) for x in range(4) for y in range(4) for z in range(8)]


def swapped(value, x=0, y=0, z=0):
    pairs = [(place(1, i, j, k), place(1, i ^ x, j ^ y, k ^ z)) for i, j, k in CHIPS]
    pairs += [(place(0, *chip), place(0, *chip)) for chip in CHIPS]
    return lax.ppermute(value, ("dp", "space"), pairs)


def handed(value):
    pairs = [(place(core, *chip), place(1 - core, *chip)) for chip in CHIPS for core in (0, 1)]
    return lax.ppermute(value, ("dp", "space"), pairs)


def added(values):
    return (values[0] + values[1]) + (values[2] + values[3])


def summed_among(value, steps):
    return added([value] + [swapped(value, **bits) for bits in steps])


ALONG_X = [dict(x=1), dict(x=2), dict(x=3)]
ALONG_Y = [dict(y=1), dict(y=2), dict(y=3)]
ALONG_Z = [dict(z=1), dict(z=2), dict(z=3)]


def body(inputs, cotangent, occupancy, neighbours, weight, error_in, q_start):
    field, gradient = inputs[0], cotangent[0]
    occupied, slots = in_hbm(occupancy[0]), in_hbm(neighbours[0])
    weight = weight.reshape(3, 3, 3, 256, 256)
    up, down = brick_faces(field, gradient, occupied)
    lower, upper = shifted(up, 1), shifted(down, -1)
    fixed = (slots, in_hbm(field), in_hbm(gradient), occupied, in_hbm(q_start.T), in_hbm(error_in.reshape(3, 3, 3, 256, 256)))
    corrected, factor = local_gradient((0,), *fixed)
    corrected, factor = local_gradient((-1, 1), *fixed, lower, upper, in_vmem(corrected), factor)

    part = factor + handed(factor)
    part, travelling = lax.optimization_barrier((part, corrected))
    arrived = [swapped(part[k], x=k) for k in (1, 2, 3)]
    partner = handed(travelling)
    total = input_gradient(0, False, slots, gradient, occupied, weight, tie=part)
    part, total = lax.optimization_barrier((added([part[0]] + arrived), total))
    part = part.reshape(4, 7, 8, 256)
    part = added([part[0]] + [swapped(part[k], y=k) for k in (1, 2, 3)])
    part = summed_among(part, ALONG_Z)
    arrived = swapped(part, z=6)
    total = input_gradient(-1, False, slots, gradient, occupied, weight, upper, total, tie=part)
    part, total = lax.optimization_barrier((part + arrived, total))
    part = jnp.concatenate([part] + [swapped(part, **bits) for bits in ALONG_Y], axis=0)
    arrived = [swapped(part, **bits) for bits in ALONG_X]
    input_grad = input_gradient(1, True, slots, gradient, occupied, weight, lower, total, tie=part)
    part, partner, input_grad = lax.optimization_barrier(
        (jnp.stack([part] + arrived, axis=0), partner, input_grad)
    )

    right = right_product(part, corrected, partner)
    right, part = lax.optimization_barrier((summed_among(right, ALONG_X), part))
    arrived = [swapped(right, **bits) for bits in ALONG_Y]
    given = handed(part)
    right, given = lax.optimization_barrier((added([right] + arrived), given))
    arrived = [swapped(right, **bits) for bits in ALONG_Z]
    halves = half_inverse(part, given)
    right, *halves = lax.optimization_barrier((added([right] + arrived), *halves))
    arrived = swapped(right, z=6)
    inverse = whole_inverse(*halves, tie=right)
    right, inverse = lax.optimization_barrier((right + arrived, inverse))
    right_given = handed(right)
    new_error, q_rows = remaining_error(part, given, corrected, right, right_given, inverse)
    return (input_grad[None], q_rows.T, new_error.reshape(1, 1, 6912, 256))


def solution(mesh):
    in_specs = (
        P("dp", "space", None, None),
        P("dp", "space", None, None),
        P("dp", "space", None),
        P("dp", "space", None),
        P(),
        P("dp", "space", None, None),
        P(),
    )
    out_specs = (P("dp", "space", None, None), P(), P("dp", "space", None, None))
    return jax.shard_map(body, mesh=mesh, in_specs=in_specs, out_specs=out_specs, check_vma=False)
```

```python
import functools

import jax
import jax.numpy as jnp
from jax import lax
from jax.experimental import pallas as pl
from jax.experimental.pallas import tpu as pltpu
from jax.sharding import PartitionSpec as P

EDGE = 8
PLANE = EDGE * EDGE
F32 = jnp.float32
BF16 = jnp.bfloat16
NT = (((1,), (1,)), ((), ()))
NN = (((1,), (0,)), ((), ()))
TN = (((0,), (0,)), ((), ()))
STEPS = (-1, 0, 1)
MIB = 1024 * 1024


def split(value):
    high = value.astype(BF16)
    low = (value - high.astype(F32)).astype(BF16)
    return high, low


def source_rows(slots, step_x, step_y, step_z, along):
    shape = (128, 1) if along == 0 else (1, 128)
    place = lax.broadcasted_iota(jnp.int32, shape, along)
    brick = place // PLANE
    y = (place // EDGE) % EDGE + step_y
    z = place % EDGE + step_z
    wrapped_y = y % EDGE
    wrapped_z = z % EDGE
    rows = jnp.full(shape, -1, jnp.int32)
    for side_y in sorted({0, step_y}):
        in_y = (y < 0) if side_y < 0 else (y >= EDGE) if side_y > 0 else (y >= 0) & (y < EDGE)
        for side_z in sorted({0, step_z}):
            in_z = (z < 0) if side_z < 0 else (z >= EDGE) if side_z > 0 else (z >= 0) & (z < EDGE)
            if side_z == 0:
                offset = wrapped_y * EDGE + wrapped_z
                first, stride = 0, PLANE
            else:
                offset = wrapped_y
                first, stride = (128 if side_z < 0 else 144), EDGE
            for which in (0, 1):
                slot = slots[which, (step_x + 1) * 9 + (side_y + 1) * 3 + side_z + 1]
                if side_z:
                    end = 0 if side_z < 0 else lax.axis_size("space") - 1
                    slot = jnp.where(lax.axis_index("space") == end, -1, slot)
                base = jnp.where(slot < 0, -4096, slot * stride + first)
                rows = jnp.where(in_y & in_z & (brick == which), base + offset, rows)
    return rows


def one_hot(rows, along, depth):
    shape = (128, depth) if along == 0 else (depth, 128)
    places = lax.broadcasted_iota(jnp.int32, shape, 1 - along)
    return jnp.where(places == rows, 1.0, 0.0).astype(BF16)


def voxel_mask(occupancy):
    padded = jnp.concatenate([occupancy[...].astype(F32), jnp.zeros((6, 512), F32)], axis=0)
    return padded.T


def own_plane(field, mask, plane):
    rows = slice(plane * PLANE, (plane + 1) * PLANE)
    return jnp.concatenate([field[b, rows, :] * mask[rows, b : b + 1] for b in (0, 1)], axis=0)


def with_faces(own, lower, upper, plane):
    rest = jnp.zeros((96, own.shape[1]), BF16)
    return jnp.concatenate([own, lower[0, plane], upper[0, plane], rest], axis=0)


def coordinates():
    dp, space = lax.axis_index("dp"), lax.axis_index("space")
    return dp % 2, space // 16, (space % 2) * 2 + dp // 2, (space // 2) % 8


def place_of(tap, y):
    return ((tap // 7) ^ y) * 7 + tap % 7


def put_factor(mine, other, tap, value):
    core, x, y, _ = coordinates()
    place = place_of(tap, y)
    halves = value[:, :128], value[:, 128:]
    kept = jnp.where(core == 0, halves[0], halves[1])
    sent = jnp.where(core == 0, halves[1], halves[0])
    for block in range(4):
        rows = slice(block * 8, block * 8 + 8)
        mine[block ^ x, place] = kept[rows]
        other[block ^ x, place] = sent[rows]


def get_factor(mine, other, tap):
    core, x, y, _ = coordinates()
    place = place_of(tap, y)
    own = jnp.concatenate([mine[block ^ x, place] for block in range(4)], axis=0)
    rest = jnp.concatenate([other[block ^ x, place] for block in range(4)], axis=0)
    both = jnp.concatenate([jnp.where(core == 0, own, rest), jnp.where(core == 0, rest, own)], axis=1)
    return both * (1.0 / 256.0)


def whole(*shape):
    return pl.BlockSpec(shape, lambda *step: (0,) * len(shape))


def faces_kernel(field, cotangent, occupancy, up, down):
    mask = voxel_mask(occupancy).astype(BF16)
    row = lax.broadcasted_iota(jnp.int32, (32, 128), 0)
    place = lax.broadcasted_iota(jnp.int32, (32, 128), 1)
    wanted = jnp.where(row < 16, row * EDGE + EDGE - 1, (row - 16) * EDGE)
    picks = jnp.where(place == wanted, 1.0, 0.0).astype(BF16)
    for which, source in enumerate((field, cotangent)):
        for plane in range(EDGE):
            found = lax.dot_general(picks, own_plane(source, mask, plane), NN, preferred_element_type=F32)
            up[which, plane] = found[:16].astype(BF16)
            down[which, plane] = found[16:].astype(BF16)


def brick_faces(field, cotangent, occupancy):
    shape = jax.ShapeDtypeStruct((2, EDGE, 16, 256), BF16)
    return pl.pallas_call(faces_kernel, out_shape=[shape, shape], compiler_params=SMALL, name="brick_faces")(
        in_hbm(field), in_hbm(cotangent), occupancy
    )


def gradient_kernel(sides, width, *refs):
    faces = sides != (0,)
    slots, field, cotangent, occupancy, start, error = refs[:6]
    refs = refs[6:]
    if faces:
        lower, upper, _, _, mine_before, other_before = refs[:6]
        refs = refs[6:]
    kept, sent, mine, other, views, sources, own, start_parts = refs
    core = coordinates()[0]
    step = pl.program_id(0)
    depth = 256 if faces else 128
    shares = 3 // width
    side = step // shares * 2 - 1 if faces else 0

    @pl.when(step == 0)
    def _():
        mask = voxel_mask(occupancy).astype(BF16)
        high, low = split(start[...].T)
        none = jnp.zeros((256, 32), BF16)
        start_parts[0:256, :] = jnp.concatenate([high, low, none, none], axis=1)
        start_parts[256:512, :] = jnp.concatenate([high, none, none, none], axis=1)
        start_parts[512:768, :] = jnp.concatenate([none, none, high, low], axis=1)
        start_parts[768:1024, :] = jnp.concatenate([none, none, high, none], axis=1)
        for plane in range(EDGE):
            own[plane * 128 : (plane + 1) * 128, :] = own_plane(cotangent, mask, plane)
            source = own_plane(field, mask, plane)
            if faces:
                source = with_faces(source, lower, upper, plane)
            sources[plane * 256 : (plane + 1) * 256, :] = source.T
        if faces:
            mine[...] = mine_before[...]
            other[...] = other_before[...]
        else:
            put_factor(mine, other, 27, jnp.zeros((32, 256), F32))

    def gather(groups):
        for first in range(0, len(groups), 2):
            pair = groups[first : first + 2]
            for step_x, left, where in (
                (-1, sources[7 * 256 : 8 * 256, :], 0),
                (0, sources[...], 1),
                (1, sources[0:256, :], 9),
            ):
                picks = jnp.concatenate(
                    [one_hot(source_rows(slots, step_x, y, z, 1), 1, depth) for y, z in pair], axis=1
                )
                found = lax.dot_general(left, picks, NN, preferred_element_type=F32).astype(BF16)
                for member in range(len(pair)):
                    for block in range(left.shape[0] // 256):
                        views[first + member, :, (where + block) * 128 : (where + block + 1) * 128] = found[
                            block * 256 : (block + 1) * 256, member * 128 : (member + 1) * 128
                        ]

    for index in range(len(sides) * shares):
        chosen = STEPS[index % shares * width : index % shares * width + width]

        @pl.when(step == index)
        def _():
            gather([(y, sides[index // shares]) for y in chosen])

    parts = []
    for member in range(width):
        columns = jnp.concatenate([views[member, :, k * 128 : k * 128 + 1024] for k in range(3)], axis=0)
        total = lax.dot_general(columns, own[...], NN, preferred_element_type=F32)
        total = total + error[:, member, 0].astype(F32).reshape(768, 256)
        halves = total.reshape(3, 2, 128, 256)
        kept[0, :, member] = jnp.where(core == 0, halves[:, 0], halves[:, 1])
        sent[0, :, member] = jnp.where(core == 0, halves[:, 1], halves[:, 0])
        high, low = split(total)
        for tap_x in range(3):
            rows = slice(tap_x * 256, tap_x * 256 + 256)
            parts.append((tap_x, member, [high[rows], low[rows]]))
    for first in range(0, 3 * width, 2):
        chosen = parts[first : first + 2]
        left = jnp.concatenate([part for _, _, both in chosen for part in both], axis=1)
        made = lax.dot_general(left, start_parts[0 : left.shape[1], :], NN, preferred_element_type=F32).T
        for slot, (tap_x, member, _) in enumerate(chosen):
            step_y = step % shares * width + member
            rows = made[slot * 64 : slot * 64 + 64]
            put_factor(mine, other, tap_x * 9 + step_y * 3 + side + 1, rows[:32] + rows[32:])


def local_gradient(sides, slots, field, cotangent, occupancy, start, error, *more):
    faces = sides != (0,)
    width = FACES_WIDTH if faces else OWN_WIDTH
    shares = 3 // width

    def which(step):
        return step // shares * 2 if faces else 1

    piece = whole(4, 28, 8, 128)
    face = whole(1, EDGE, 16, 256)
    anywhere = pl.BlockSpec(memory_space=pl.ANY)
    half = pl.BlockSpec((1, 3, width, 128, 256), lambda step: (which(step), 0, step % shares, 0, 0))
    in_specs = [
        pl.BlockSpec(memory_space=pltpu.SMEM),
        whole(2, 512, 256),
        whole(2, 512, 256),
        whole(2, 512),
        whole(32, 256),
        pl.BlockSpec((3, width, 1, 256, 256), lambda step: (0, step % shares, which(step), 0, 0)),
    ]
    if faces:
        in_specs += [face, face, anywhere, anywhere, piece, piece]
    depth = 256 if faces else 128
    return pl.pallas_call(
        functools.partial(gradient_kernel, sides, width),
        grid=(len(sides) * shares,),
        in_specs=in_specs,
        out_specs=[half, half, piece, piece],
        out_shape=[
            HALF,
            HALF,
            jax.ShapeDtypeStruct((4, 28, 8, 128), F32),
            jax.ShapeDtypeStruct((4, 28, 8, 128), F32),
        ],
        input_output_aliases={8: 0, 9: 1} if faces else {},
        scratch_shapes=[
            pltpu.VMEM((width, 256, 1280), BF16),
            pltpu.VMEM((2048, depth), BF16),
            pltpu.VMEM((1024, 256), BF16),
            pltpu.VMEM((1024, 128), BF16),
        ],
        compiler_params=pltpu.CompilerParams(vmem_limit_bytes=GRAD_LIMIT),
        cost_estimate=pl.CostEstimate(
            flops=len(sides) * 2 * 10**9, bytes_accessed=len(sides) * 4 * 10**6, transcendentals=0
        ),
        name="gradient_with_faces" if faces else "gradient_own",
    )(slots, field, cotangent, occupancy, start, error, *more)


def input_kernel(side, last, *refs):
    slots, cotangent, occupancy, weight = refs[:4]
    refs = refs[4:]
    if side:
        face, total_before = refs[:2]
        refs = refs[2:]
    result, views, total = refs[-3:]
    step = pl.program_id(0)

    @pl.when(step == 0)
    def _():
        mask = voxel_mask(occupancy).astype(BF16)
        sources = [own_plane(cotangent, mask, plane) for plane in range(EDGE)]
        if side:
            sources = [with_faces(own, face, face, plane) for plane, own in enumerate(sources)]
        for index, y in enumerate(STEPS):
            picks = [one_hot(source_rows(slots, x, y, -side, 0), 0, 256 if side else 128) for x in STEPS]
            for plane in range(-1, EDGE + 1):
                which = 0 if plane < 0 else 2 if plane >= EDGE else 1
                found = lax.dot_general(picks[which], sources[plane % EDGE], NN, preferred_element_type=F32)
                views[index, (plane + 1) * 128 : (plane + 2) * 128, :] = found.astype(BF16)
        total[...] = total_before[...] if side else jnp.zeros_like(total)

    columns = jnp.concatenate(
        [views[2 - step, (2 - tap_x) * 128 : (2 - tap_x) * 128 + 1024, :] for tap_x in range(3)], axis=1
    )
    weights = jnp.concatenate([weight[tap_x, 0, 0] for tap_x in range(3)], axis=1)
    total[...] += lax.dot_general(columns, weights, NT, preferred_element_type=F32)

    @pl.when(step == 2)
    def _():
        if not last:
            result[...] = total[...]
            return
        mask = voxel_mask(occupancy)
        for plane in range(EDGE):
            for brick in (0, 1):
                first = (2 * plane + brick) * PLANE
                rows = slice(plane * PLANE, (plane + 1) * PLANE)
                kept = total[first : first + PLANE, :] * mask[rows, brick : brick + 1]
                result[brick, rows, :] = kept.astype(BF16)


def input_gradient(side, last, slots, cotangent, occupancy, weight, *more, tie=None):
    in_specs = [
        pl.BlockSpec(memory_space=pltpu.SMEM),
        whole(2, 512, 256),
        whole(2, 512),
        pl.BlockSpec((3, 1, 1, 256, 256), lambda step: (0, step, side + 1, 0, 0)),
    ]
    if side:
        in_specs += [pl.BlockSpec((1, EDGE, 16, 256), lambda step: (1, 0, 0, 0)), whole(1024, 256)]
    if tie is not None:
        in_specs += [pl.BlockSpec(memory_space=pl.ANY)]
        more += (tie,)
    if last:
        shape, spec = jax.ShapeDtypeStruct((2, 512, 256), BF16), whole(2, 512, 256)
    else:
        shape, spec = jax.ShapeDtypeStruct((1024, 256), F32), whole(1024, 256)
    return pl.pallas_call(
        functools.partial(input_kernel, side, last),
        grid=(3,),
        in_specs=in_specs,
        out_specs=spec,
        out_shape=shape,
        scratch_shapes=[pltpu.VMEM((3, 1280, 256), BF16), pltpu.VMEM((1024, 256), F32)],
        compiler_params=pltpu.CompilerParams(vmem_limit_bytes=INPUT_LIMIT),
        cost_estimate=pl.CostEstimate(flops=2 * 10**9, bytes_accessed=4 * 10**6, transcendentals=0),
        name=("input_own", "input_above", "input_below")[side],
    )(slots, cotangent, occupancy, weight, *more)


def taps_left(mine, other, step_x, step_y):
    first = step_x * 9 + step_y * 3
    return jnp.concatenate([get_factor(mine, other, first + k) for k in range(3)], axis=1)


def right_kernel(mine, kept, partner, right):
    step = pl.program_id(0)
    _, x, y, _ = coordinates()

    @pl.when(step == 0)
    def _():
        right[...] = jnp.zeros_like(right)

    total = jnp.zeros((32, 256), F32)
    for step_y in range(3):
        columns = []
        for step_z in range(3):
            place = place_of(step * 9 + step_y * 3 + step_z, y)
            columns.append(jnp.concatenate([mine[block ^ x, place] for block in range(4)], axis=0))
        left_high, left_low = split(jnp.concatenate(columns, axis=1) * (1.0 / 256.0))
        high, low = split((kept[:, 0, step_y] + partner[:, 0, step_y]).reshape(384, 256))
        both = lax.dot_general(
            jnp.concatenate([left_high, left_low], axis=0), high, NN, preferred_element_type=F32
        )
        total += both[0:32] + both[32:64]
        total += lax.dot_general(left_high, low, NN, preferred_element_type=F32)
    right[...] += total


def along_x(*shape):
    return pl.BlockSpec((3, 1, 3) + shape, lambda step: (0, step, 0, 0, 0))


def right_product(mine, kept, partner):
    return pl.pallas_call(
        right_kernel,
        grid=(3,),
        in_specs=[whole(4, 28, 8, 128), along_x(128, 256), along_x(128, 256)],
        out_specs=whole(32, 256),
        out_shape=jax.ShapeDtypeStruct((32, 256), F32),
        compiler_params=pltpu.CompilerParams(vmem_limit_bytes=LATE_LIMIT),
        name="right_product",
    )(mine, in_vmem(kept), in_vmem(partner))


def eliminate(first, work, made):
    places = lax.broadcasted_iota(jnp.int32, (32, 1), 0)
    for step in range(first, first + 16):
        scale = 1.0 / jnp.sqrt(work[step : step + 1, step : step + 1])
        work_row = work[step : step + 1, :] * scale
        made_row = made[step : step + 1, :] * scale
        column = work[:, step : step + 1] * scale
        later = jnp.where(places > step, column, 0.0)
        here = places == step
        work = jnp.where(here, work_row, work - later * work_row)
        made = jnp.where(here, made_row, made - later * made_row)
    return work, made


def first_half_kernel(mine, other, work, made):
    gram = jnp.zeros((32, 32), F32)
    for step in range(9):
        left = jnp.concatenate([get_factor(mine, other, step * 3 + tap) for tap in range(3)], axis=1)
        gram += lax.dot_general(left, left, NT, precision=lax.Precision.HIGHEST, preferred_element_type=F32)
    row = lax.broadcasted_iota(jnp.int32, (32, 32), 0)
    column = lax.broadcasted_iota(jnp.int32, (32, 32), 1)
    work[...], made[...] = eliminate(0, gram, jnp.where(row == column, 1.0, 0.0).astype(F32))


def second_half_kernel(work, made, inverse):
    inverse[...] = eliminate(16, work[...], made[...])[1]


SQUARE = jax.ShapeDtypeStruct((32, 32), F32)


def half_inverse(mine, other):
    return pl.pallas_call(first_half_kernel, out_shape=[SQUARE, SQUARE], compiler_params=SMALL, name="half_inverse")(
        mine, other
    )


def whole_inverse(work, made, tie=None):
    def kernel(work, made, *refs):
        second_half_kernel(work, made, refs[-1])

    more = () if tie is None else (tie,)
    vmem = pl.BlockSpec(memory_space=pltpu.VMEM)
    return pl.pallas_call(
        kernel,
        in_specs=[vmem, vmem] + [pl.BlockSpec(memory_space=pl.ANY)] * len(more),
        out_specs=vmem,
        out_shape=SQUARE,
        compiler_params=SMALL,
        name="whole_inverse",
    )(work, made, *more)


def error_kernel(mine, other, kept, sent, right, inverse, new_error, q_rows, basis):
    step = pl.program_id(0)

    @pl.when(step == 0)
    def _():
        rows = lax.dot_general(
            inverse[...], right[...], NN, precision=lax.Precision.HIGHEST, preferred_element_type=F32
        ) * (1.0 / 256.0)
        q_rows[...] = rows
        back = lax.dot_general(
            inverse[...].T, rows, NN, precision=lax.Precision.HIGHEST, preferred_element_type=F32
        )
        high, low = split(back)
        basis[0:32, :] = high
        basis[32:64, :] = high
        basis[64:96, :] = low
        basis[96:128, :] = jnp.zeros((32, 256), BF16)

    core = coordinates()[0]
    for step_y in range(3):
        high, low = split(taps_left(mine, other, step, step_y))
        left = jnp.concatenate([high, low, high, jnp.zeros((32, 768), BF16)], axis=0)
        product = lax.dot_general(left, basis[...], TN, preferred_element_type=F32)
        product = product.reshape(3, 2, 128, 256)
        own, rest = kept[:, 0, step_y], sent[:, 0, step_y]
        halves = jnp.where(core == 0, own, rest), jnp.where(core == 0, rest, own)
        for half in (0, 1):
            rows = slice(half * 128, half * 128 + 128)
            new_error[0, step_y, :, rows, :] = (halves[half] - product[:, half]).astype(BF16)


def remaining_error(mine, other, kept, sent, right, inverse):
    return pl.pallas_call(
        error_kernel,
        grid=(3,),
        in_specs=[
            whole(4, 28, 8, 128),
            whole(4, 28, 8, 128),
            along_x(128, 256),
            along_x(128, 256),
            whole(32, 256),
            whole(32, 32),
        ],
        out_specs=[pl.BlockSpec((1, 3, 3, 256, 256), lambda step: (step, 0, 0, 0, 0)), whole(32, 256)],
        out_shape=[jax.ShapeDtypeStruct((3, 3, 3, 256, 256), BF16), jax.ShapeDtypeStruct((32, 256), F32)],
        scratch_shapes=[pltpu.VMEM((128, 256), BF16)],
        compiler_params=pltpu.CompilerParams(vmem_limit_bytes=LATE_LIMIT),
        name="remaining_error",
    )(mine, other, in_vmem(kept), in_vmem(sent), right, inverse)


HALF = pltpu.VMEM((3, 3, 3, 128, 256), F32)
GRAD_LIMIT = 32 * MIB
OWN_WIDTH = 3
FACES_WIDTH = 3
INPUT_LIMIT = 24 * MIB
LATE_LIMIT = 24 * MIB
SMALL = pltpu.CompilerParams(vmem_limit_bytes=12 * MIB)


def in_vmem(value):
    return pltpu.with_memory_space_constraint(value, pltpu.VMEM)


def in_hbm(value):
    return pltpu.with_memory_space_constraint(value, pltpu.HBM)


def shifted(value, by):
    devices = lax.axis_size("space")
    return lax.ppermute(value, "space", [(i, (i + by) % devices) for i in range(devices)])


def partners(core=0, x=0, y=0, z=0):
    def place(at_core, at_x, at_y, at_z):
        return (at_y % 2 * 2 + at_core) * 64 + (at_x * 8 + at_z) * 2 + at_y // 2

    return [
        (place(c, i, j, l), place(c ^ core, i ^ x, j ^ y, l ^ z))
        for c in range(2)
        for i in range(4)
        for j in range(4)
        for l in range(8)
    ]


def swapped(value, **bits):
    return lax.ppermute(value, ("dp", "space"), partners(**bits))


def added(values):
    return (values[0] + values[1]) + (values[2] + values[3])


def summed_among(value, steps):
    return added([value] + [swapped(value, **bits) for bits in steps])


ALONG_X = [dict(x=1), dict(x=2), dict(x=3)]
ALONG_Y = [dict(y=1), dict(y=2), dict(y=3)]
ALONG_Z = [dict(z=1), dict(z=2), dict(z=3)]
CORE_AND_Z = [dict(core=1), dict(z=6), dict(core=1, z=6)]


def body(inputs, cotangent, occupancy, neighbours, weight, error_in, q_start):
    field, gradient = inputs[0], cotangent[0]
    occupied, slots = in_hbm(occupancy[0]), in_hbm(neighbours[0])
    weight = weight.reshape(3, 3, 3, 256, 256)
    up, down = brick_faces(field, gradient, occupied)
    lower, upper = shifted(up, 1), shifted(down, -1)
    fixed = (slots, in_hbm(field), in_hbm(gradient), occupied, in_hbm(q_start.T), in_hbm(error_in.reshape(3, 3, 3, 256, 256)))
    kept, sent, mine, other = local_gradient((0,), *fixed)
    kept, sent, mine, other = local_gradient(
        (-1, 1), *fixed, lower, upper, in_vmem(kept), in_vmem(sent), mine, other
    )

    part = mine + swapped(other, core=1)
    part, travelling = lax.optimization_barrier((part, sent))
    arrived = [swapped(part[k], x=k) for k in (1, 2, 3)]
    partner = swapped(travelling, core=1)
    total = input_gradient(0, False, slots, gradient, occupied, weight, tie=part)
    part, total = lax.optimization_barrier((added([part[0]] + arrived), total))
    part = part.reshape(4, 7, 8, 128)
    part = added([part[0]] + [swapped(part[k], y=k) for k in (1, 2, 3)])
    part = summed_among(part, ALONG_Z)
    arrived = swapped(part, z=6)
    total = input_gradient(-1, False, slots, gradient, occupied, weight, upper, total, tie=part)
    part, total = lax.optimization_barrier((part + arrived, total))
    part = jnp.concatenate([part] + [swapped(part, **bits) for bits in ALONG_Y], axis=0)
    arrived = [swapped(part, **bits) for bits in ALONG_X]
    input_grad = input_gradient(1, True, slots, gradient, occupied, weight, lower, total, tie=part)
    mine, partner, input_grad = lax.optimization_barrier(
        (jnp.stack([part] + arrived, axis=0), partner, input_grad)
    )

    right = right_product(mine, kept, partner)
    right, mine = lax.optimization_barrier((summed_among(right, CORE_AND_Z), mine))
    arrived = [swapped(right, **bits) for bits in ALONG_X]
    other = swapped(mine, core=1)
    right, other = lax.optimization_barrier((added([right] + arrived), other))
    arrived = [swapped(right, **bits) for bits in ALONG_Y]
    halves = half_inverse(mine, other)
    right, *halves = lax.optimization_barrier((added([right] + arrived), *halves))
    arrived = [swapped(right, **bits) for bits in ALONG_Z]
    inverse = whole_inverse(*halves, tie=right)
    right = added([right] + arrived)
    new_error, q_rows = remaining_error(mine, other, kept, sent, right, inverse)
    return (input_grad[None], q_rows.T, new_error.reshape(1, 1, 6912, 256))


def solution(mesh):
    in_specs = (
        P("dp", "space", None, None),
        P("dp", "space", None, None),
        P("dp", "space", None),
        P("dp", "space", None),
        P(),
        P("dp", "space", None, None),
        P(),
    )
    out_specs = (P("dp", "space", None, None), P(), P("dp", "space", None, None))
    return jax.shard_map(body, mesh=mesh, in_specs=in_specs, out_specs=out_specs, check_vma=False)
```

```python
import functools

import jax
import jax.numpy as jnp
from jax import lax
from jax.experimental import pallas as pl
from jax.experimental.pallas import tpu as pltpu
from jax.sharding import PartitionSpec as P

EDGE = 8
PLANE = EDGE * EDGE
F32 = jnp.float32
BF16 = jnp.bfloat16
NT = (((1,), (1,)), ((), ()))
NN = (((1,), (0,)), ((), ()))
TN = (((0,), (0,)), ((), ()))
STEPS = (-1, 0, 1)
MIB = 1024 * 1024


def split(value):
    high = value.astype(BF16)
    low = (value - high.astype(F32)).astype(BF16)
    return high, low


def source_rows(slots, step_x, step_y, step_z, along):
    shape = (128, 1) if along == 0 else (1, 128)
    place = lax.broadcasted_iota(jnp.int32, shape, along)
    brick = place // PLANE
    y = (place // EDGE) % EDGE + step_y
    z = place % EDGE + step_z
    wrapped_y = y % EDGE
    wrapped_z = z % EDGE
    rows = jnp.full(shape, -1, jnp.int32)
    for side_y in sorted({0, step_y}):
        in_y = (y < 0) if side_y < 0 else (y >= EDGE) if side_y > 0 else (y >= 0) & (y < EDGE)
        for side_z in sorted({0, step_z}):
            in_z = (z < 0) if side_z < 0 else (z >= EDGE) if side_z > 0 else (z >= 0) & (z < EDGE)
            if side_z == 0:
                offset = wrapped_y * EDGE + wrapped_z
                first, stride = 0, PLANE
            else:
                offset = wrapped_y
                first, stride = (128 if side_z < 0 else 144), EDGE
            for which in (0, 1):
                slot = slots[which, (step_x + 1) * 9 + (side_y + 1) * 3 + side_z + 1]
                if side_z:
                    end = 0 if side_z < 0 else lax.axis_size("space") - 1
                    slot = jnp.where(lax.axis_index("space") == end, -1, slot)
                base = jnp.where(slot < 0, -4096, slot * stride + first)
                rows = jnp.where(in_y & in_z & (brick == which), base + offset, rows)
    return rows


def one_hot(rows, along, depth):
    shape = (128, depth) if along == 0 else (depth, 128)
    places = lax.broadcasted_iota(jnp.int32, shape, 1 - along)
    return jnp.where(places == rows, 1.0, 0.0).astype(BF16)


def voxel_mask(occupancy):
    padded = jnp.concatenate([occupancy[...].astype(F32), jnp.zeros((6, 512), F32)], axis=0)
    return padded.T


def own_plane(field, mask, plane):
    rows = slice(plane * PLANE, (plane + 1) * PLANE)
    return jnp.concatenate([field[b, rows, :] * mask[rows, b : b + 1] for b in (0, 1)], axis=0)


def with_faces(own, lower, upper, plane):
    rest = jnp.zeros((96, own.shape[1]), BF16)
    return jnp.concatenate([own, lower[0, plane], upper[0, plane], rest], axis=0)


def coordinates():
    dp, space = lax.axis_index("dp"), lax.axis_index("space")
    return dp % 2, space // 16, (space % 2) * 2 + dp // 2, (space // 2) % 8


def place_of(tap, y):
    return ((tap // 7) ^ y) * 7 + tap % 7


def put_factor(mine, other, tap, value):
    core, x, y, _ = coordinates()
    place = place_of(tap, y)
    halves = value[:, :128], value[:, 128:]
    kept = jnp.where(core == 0, halves[0], halves[1])
    sent = jnp.where(core == 0, halves[1], halves[0])
    for block in range(4):
        rows = slice(block * 8, block * 8 + 8)
        mine[block ^ x, place] = kept[rows]
        other[block ^ x, place] = sent[rows]


def get_factor(mine, other, tap):
    core, x, y, _ = coordinates()
    place = place_of(tap, y)
    own = jnp.concatenate([mine[block ^ x, place] for block in range(4)], axis=0)
    rest = jnp.concatenate([other[block ^ x, place] for block in range(4)], axis=0)
    both = jnp.concatenate([jnp.where(core == 0, own, rest), jnp.where(core == 0, rest, own)], axis=1)
    return both * (1.0 / 256.0)


def whole(*shape):
    return pl.BlockSpec(shape, lambda *step: (0,) * len(shape))


def faces_kernel(field, cotangent, occupancy, up, down):
    mask = voxel_mask(occupancy).astype(BF16)
    row = lax.broadcasted_iota(jnp.int32, (32, 128), 0)
    place = lax.broadcasted_iota(jnp.int32, (32, 128), 1)
    wanted = jnp.where(row < 16, row * EDGE + EDGE - 1, (row - 16) * EDGE)
    picks = jnp.where(place == wanted, 1.0, 0.0).astype(BF16)
    for which, source in enumerate((field, cotangent)):
        for plane in range(EDGE):
            found = lax.dot_general(picks, own_plane(source, mask, plane), NN, preferred_element_type=F32)
            up[which, plane] = found[:16].astype(BF16)
            down[which, plane] = found[16:].astype(BF16)


def brick_faces(field, cotangent, occupancy):
    shape = jax.ShapeDtypeStruct((2, EDGE, 16, 256), BF16)
    return pl.pallas_call(faces_kernel, out_shape=[shape, shape], compiler_params=SMALL, name="brick_faces")(
        in_hbm(field), in_hbm(cotangent), occupancy
    )


def gradient_kernel(sides, width, *refs):
    faces = sides != (0,)
    slots, field, cotangent, occupancy, start, error = refs[:6]
    refs = refs[6:]
    if faces:
        lower, upper, _, _, mine_before, other_before = refs[:6]
        refs = refs[6:]
    kept, sent, mine, other, views, sources, own, start_parts = refs
    core = coordinates()[0]
    step = pl.program_id(0)
    depth = 256 if faces else 128
    shares = 3 // width
    side = step // shares * 2 - 1 if faces else 0

    @pl.when(step == 0)
    def _():
        mask = voxel_mask(occupancy).astype(BF16)
        high, low = split(start[...].T)
        none = jnp.zeros((256, 32), BF16)
        start_parts[0:256, :] = jnp.concatenate([high, low, none, none], axis=1)
        start_parts[256:512, :] = jnp.concatenate([high, none, none, none], axis=1)
        start_parts[512:768, :] = jnp.concatenate([none, none, high, low], axis=1)
        start_parts[768:1024, :] = jnp.concatenate([none, none, high, none], axis=1)
        for plane in range(EDGE):
            own[plane * 128 : (plane + 1) * 128, :] = own_plane(cotangent, mask, plane)
            source = own_plane(field, mask, plane)
            if faces:
                source = with_faces(source, lower, upper, plane)
            sources[plane * 256 : (plane + 1) * 256, :] = source.T
        if faces:
            mine[...] = mine_before[...]
            other[...] = other_before[...]
        else:
            put_factor(mine, other, 27, jnp.zeros((32, 256), F32))

    def gather(groups):
        for first in range(0, len(groups), 2):
            pair = groups[first : first + 2]
            for step_x, left, where in (
                (-1, sources[7 * 256 : 8 * 256, :], 0),
                (0, sources[...], 1),
                (1, sources[0:256, :], 9),
            ):
                picks = jnp.concatenate(
                    [one_hot(source_rows(slots, step_x, y, z, 1), 1, depth) for y, z in pair], axis=1
                )
                found = lax.dot_general(left, picks, NN, preferred_element_type=F32).astype(BF16)
                for member in range(len(pair)):
                    for block in range(left.shape[0] // 256):
                        views[first + member, :, (where + block) * 128 : (where + block + 1) * 128] = found[
                            block * 256 : (block + 1) * 256, member * 128 : (member + 1) * 128
                        ]

    for index in range(len(sides) * shares):
        chosen = STEPS[index % shares * width : index % shares * width + width]

        @pl.when(step == index)
        def _():
            gather([(y, sides[index // shares]) for y in chosen])

    parts = []
    for member in range(width):
        columns = jnp.concatenate([views[member, :, k * 128 : k * 128 + 1024] for k in range(3)], axis=0)
        total = lax.dot_general(columns, own[...], NN, preferred_element_type=F32)
        total = total + error[:, member, 0].astype(F32).reshape(768, 256)
        halves = total.reshape(3, 2, 128, 256)
        kept[0, :, member] = jnp.where(core == 0, halves[:, 0], halves[:, 1])
        sent[0, :, member] = jnp.where(core == 0, halves[:, 1], halves[:, 0])
        high, low = split(total)
        for tap_x in range(3):
            rows = slice(tap_x * 256, tap_x * 256 + 256)
            parts.append((tap_x, member, [high[rows], low[rows]]))
    for first in range(0, 3 * width, 2):
        chosen = parts[first : first + 2]
        left = jnp.concatenate([part for _, _, both in chosen for part in both], axis=1)
        made = lax.dot_general(left, start_parts[0 : left.shape[1], :], NN, preferred_element_type=F32).T
        for slot, (tap_x, member, _) in enumerate(chosen):
            step_y = step % shares * width + member
            rows = made[slot * 64 : slot * 64 + 64]
            put_factor(mine, other, tap_x * 9 + step_y * 3 + side + 1, rows[:32] + rows[32:])


def local_gradient(sides, slots, field, cotangent, occupancy, start, error, *more):
    faces = sides != (0,)
    width = FACES_WIDTH if faces else OWN_WIDTH
    shares = 3 // width

    def which(step):
        return step // shares * 2 if faces else 1

    piece = whole(4, 28, 8, 128)
    face = whole(1, EDGE, 16, 256)
    anywhere = pl.BlockSpec(memory_space=pl.ANY)
    half = pl.BlockSpec((1, 3, width, 128, 256), lambda step: (which(step), 0, step % shares, 0, 0))
    in_specs = [
        pl.BlockSpec(memory_space=pltpu.SMEM),
        whole(2, 512, 256),
        whole(2, 512, 256),
        whole(2, 512),
        whole(32, 256),
        pl.BlockSpec((3, width, 1, 256, 256), lambda step: (0, step % shares, which(step), 0, 0)),
    ]
    if faces:
        in_specs += [face, face, anywhere, anywhere, piece, piece]
    depth = 256 if faces else 128
    return pl.pallas_call(
        functools.partial(gradient_kernel, sides, width),
        grid=(len(sides) * shares,),
        in_specs=in_specs,
        out_specs=[half, half, piece, piece],
        out_shape=[
            HALF,
            HALF,
            jax.ShapeDtypeStruct((4, 28, 8, 128), F32),
            jax.ShapeDtypeStruct((4, 28, 8, 128), F32),
        ],
        input_output_aliases={8: 0, 9: 1} if faces else {},
        scratch_shapes=[
            pltpu.VMEM((width, 256, 1280), BF16),
            pltpu.VMEM((2048, depth), BF16),
            pltpu.VMEM((1024, 256), BF16),
            pltpu.VMEM((1024, 128), BF16),
        ],
        compiler_params=pltpu.CompilerParams(vmem_limit_bytes=GRAD_LIMIT),
        cost_estimate=pl.CostEstimate(
            flops=len(sides) * 2 * 10**9, bytes_accessed=len(sides) * 4 * 10**6, transcendentals=0
        ),
        name="gradient_with_faces" if faces else "gradient_own",
    )(slots, field, cotangent, occupancy, start, error, *more)


def input_kernel(side, last, *refs):
    slots, cotangent, occupancy, weight = refs[:4]
    refs = refs[4:]
    if side:
        face, total_before = refs[:2]
        refs = refs[2:]
    result, views, total = refs[-3:]
    step = pl.program_id(0)

    @pl.when(step == 0)
    def _():
        mask = voxel_mask(occupancy).astype(BF16)
        sources = [own_plane(cotangent, mask, plane) for plane in range(EDGE)]
        if side:
            sources = [with_faces(own, face, face, plane) for plane, own in enumerate(sources)]
        for index, y in enumerate(STEPS):
            picks = [one_hot(source_rows(slots, x, y, -side, 0), 0, 256 if side else 128) for x in STEPS]
            for plane in range(-1, EDGE + 1):
                which = 0 if plane < 0 else 2 if plane >= EDGE else 1
                found = lax.dot_general(picks[which], sources[plane % EDGE], NN, preferred_element_type=F32)
                views[index, (plane + 1) * 128 : (plane + 2) * 128, :] = found.astype(BF16)
        total[...] = total_before[...] if side else jnp.zeros_like(total)

    columns = jnp.concatenate(
        [views[2 - step, (2 - tap_x) * 128 : (2 - tap_x) * 128 + 1024, :] for tap_x in range(3)], axis=1
    )
    weights = jnp.concatenate([weight[tap_x, 0, 0] for tap_x in range(3)], axis=1)
    total[...] += lax.dot_general(columns, weights, NT, preferred_element_type=F32)

    @pl.when(step == 2)
    def _():
        if not last:
            result[...] = total[...]
            return
        mask = voxel_mask(occupancy)
        for plane in range(EDGE):
            for brick in (0, 1):
                first = (2 * plane + brick) * PLANE
                rows = slice(plane * PLANE, (plane + 1) * PLANE)
                kept = total[first : first + PLANE, :] * mask[rows, brick : brick + 1]
                result[brick, rows, :] = kept.astype(BF16)


def input_gradient(side, last, slots, cotangent, occupancy, weight, *more, tie=None):
    in_specs = [
        pl.BlockSpec(memory_space=pltpu.SMEM),
        whole(2, 512, 256),
        whole(2, 512),
        pl.BlockSpec((3, 1, 1, 256, 256), lambda step: (0, step, side + 1, 0, 0)),
    ]
    if side:
        in_specs += [pl.BlockSpec((1, EDGE, 16, 256), lambda step: (1, 0, 0, 0)), whole(1024, 256)]
    if tie is not None:
        in_specs += [pl.BlockSpec(memory_space=pl.ANY)]
        more += (tie,)
    if last:
        shape, spec = jax.ShapeDtypeStruct((2, 512, 256), BF16), whole(2, 512, 256)
    else:
        shape, spec = jax.ShapeDtypeStruct((1024, 256), F32), whole(1024, 256)
    return pl.pallas_call(
        functools.partial(input_kernel, side, last),
        grid=(3,),
        in_specs=in_specs,
        out_specs=spec,
        out_shape=shape,
        scratch_shapes=[pltpu.VMEM((3, 1280, 256), BF16), pltpu.VMEM((1024, 256), F32)],
        compiler_params=pltpu.CompilerParams(vmem_limit_bytes=INPUT_LIMIT),
        cost_estimate=pl.CostEstimate(flops=2 * 10**9, bytes_accessed=4 * 10**6, transcendentals=0),
        name=("input_own", "input_above", "input_below")[side],
    )(slots, cotangent, occupancy, weight, *more)


def taps_left(mine, other, step_x, step_y):
    first = step_x * 9 + step_y * 3
    return jnp.concatenate([get_factor(mine, other, first + k) for k in range(3)], axis=1)


def right_kernel(mine, kept, partner, right):
    step = pl.program_id(0)
    _, x, y, _ = coordinates()

    @pl.when(step == 0)
    def _():
        right[...] = jnp.zeros_like(right)

    total = jnp.zeros((32, 256), F32)
    for step_y in range(3):
        columns = []
        for step_z in range(3):
            place = place_of(step * 9 + step_y * 3 + step_z, y)
            columns.append(jnp.concatenate([mine[block ^ x, place] for block in range(4)], axis=0))
        left_high, left_low = split(jnp.concatenate(columns, axis=1) * (1.0 / 256.0))
        high, low = split((kept[:, 0, step_y] + partner[:, 0, step_y]).reshape(384, 256))
        both = lax.dot_general(
            jnp.concatenate([left_high, left_low], axis=0), high, NN, preferred_element_type=F32
        )
        total += both[0:32] + both[32:64]
        total += lax.dot_general(left_high, low, NN, preferred_element_type=F32)
    right[...] += total


def along_x(*shape):
    return pl.BlockSpec((3, 1, 3) + shape, lambda step: (0, step, 0, 0, 0))


def right_product(mine, kept, partner):
    return pl.pallas_call(
        right_kernel,
        grid=(3,),
        in_specs=[whole(4, 28, 8, 128), along_x(128, 256), along_x(128, 256)],
        out_specs=whole(32, 256),
        out_shape=jax.ShapeDtypeStruct((32, 256), F32),
        compiler_params=pltpu.CompilerParams(vmem_limit_bytes=LATE_LIMIT),
        name="right_product",
    )(mine, in_vmem(kept), in_vmem(partner))


def eliminate(first, work, made):
    places = lax.broadcasted_iota(jnp.int32, (32, 1), 0)
    for step in range(first, first + 16):
        scale = 1.0 / jnp.sqrt(work[step : step + 1, step : step + 1])
        work_row = work[step : step + 1, :] * scale
        made_row = made[step : step + 1, :] * scale
        column = work[:, step : step + 1] * scale
        later = jnp.where(places > step, column, 0.0)
        here = places == step
        work = jnp.where(here, work_row, work - later * work_row)
        made = jnp.where(here, made_row, made - later * made_row)
    return work, made


def first_half_kernel(mine, other, work, made):
    gram = jnp.zeros((32, 32), F32)
    for step in range(9):
        left = jnp.concatenate([get_factor(mine, other, step * 3 + tap) for tap in range(3)], axis=1)
        gram += lax.dot_general(left, left, NT, precision=lax.Precision.HIGHEST, preferred_element_type=F32)
    row = lax.broadcasted_iota(jnp.int32, (32, 32), 0)
    column = lax.broadcasted_iota(jnp.int32, (32, 32), 1)
    work[...], made[...] = eliminate(0, gram, jnp.where(row == column, 1.0, 0.0).astype(F32))


def second_half_kernel(work, made, inverse):
    inverse[...] = eliminate(16, work[...], made[...])[1]


SQUARE = jax.ShapeDtypeStruct((32, 32), F32)


def half_inverse(mine, other):
    return pl.pallas_call(first_half_kernel, out_shape=[SQUARE, SQUARE], compiler_params=SMALL, name="half_inverse")(
        mine, other
    )


def whole_inverse(work, made, tie=None):
    def kernel(work, made, *refs):
        second_half_kernel(work, made, refs[-1])

    more = () if tie is None else (tie,)
    vmem = pl.BlockSpec(memory_space=pltpu.VMEM)
    return pl.pallas_call(
        kernel,
        in_specs=[vmem, vmem] + [pl.BlockSpec(memory_space=pl.ANY)] * len(more),
        out_specs=vmem,
        out_shape=SQUARE,
        compiler_params=SMALL,
        name="whole_inverse",
    )(work, made, *more)


def error_kernel(mine, other, kept, sent, right, inverse, new_error, q_rows, basis):
    step = pl.program_id(0)

    @pl.when(step == 0)
    def _():
        rows = lax.dot_general(
            inverse[...], right[...], NN, precision=lax.Precision.HIGHEST, preferred_element_type=F32
        ) * (1.0 / 256.0)
        q_rows[...] = rows
        back = lax.dot_general(
            inverse[...].T, rows, NN, precision=lax.Precision.HIGHEST, preferred_element_type=F32
        )
        high, low = split(back)
        basis[0:32, :] = high
        basis[32:64, :] = high
        basis[64:96, :] = low
        basis[96:128, :] = jnp.zeros((32, 256), BF16)

    core = coordinates()[0]
    for step_y in range(3):
        high, low = split(taps_left(mine, other, step, step_y))
        left = jnp.concatenate([high, low, high, jnp.zeros((32, 768), BF16)], axis=0)
        product = lax.dot_general(left, basis[...], TN, preferred_element_type=F32)
        product = product.reshape(3, 2, 128, 256)
        own, rest = kept[:, 0, step_y], sent[:, 0, step_y]
        halves = jnp.where(core == 0, own, rest), jnp.where(core == 0, rest, own)
        for half in (0, 1):
            rows = slice(half * 128, half * 128 + 128)
            new_error[0, step_y, :, rows, :] = (halves[half] - product[:, half]).astype(BF16)


def remaining_error(mine, other, kept, sent, right, inverse):
    return pl.pallas_call(
        error_kernel,
        grid=(3,),
        in_specs=[
            whole(4, 28, 8, 128),
            whole(4, 28, 8, 128),
            along_x(128, 256),
            along_x(128, 256),
            whole(32, 256),
            whole(32, 32),
        ],
        out_specs=[pl.BlockSpec((1, 3, 3, 256, 256), lambda step: (step, 0, 0, 0, 0)), whole(32, 256)],
        out_shape=[jax.ShapeDtypeStruct((3, 3, 3, 256, 256), BF16), jax.ShapeDtypeStruct((32, 256), F32)],
        scratch_shapes=[pltpu.VMEM((128, 256), BF16)],
        compiler_params=pltpu.CompilerParams(vmem_limit_bytes=LATE_LIMIT),
        name="remaining_error",
    )(mine, other, in_vmem(kept), in_vmem(sent), right, inverse)


HALF = pltpu.VMEM((3, 3, 3, 128, 256), F32)
GRAD_LIMIT = 32 * MIB
OWN_WIDTH = 3
FACES_WIDTH = 3
INPUT_LIMIT = 24 * MIB
LATE_LIMIT = 24 * MIB
SMALL = pltpu.CompilerParams(vmem_limit_bytes=12 * MIB)


def in_vmem(value):
    return pltpu.with_memory_space_constraint(value, pltpu.VMEM)


def in_hbm(value):
    return pltpu.with_memory_space_constraint(value, pltpu.HBM)


def shifted(value, by):
    devices = lax.axis_size("space")
    return lax.ppermute(value, "space", [(i, (i + by) % devices) for i in range(devices)])


def partners(core=0, x=0, y=0, z=0):
    def place(at_core, at_x, at_y, at_z):
        return (at_y % 2 * 2 + at_core) * 64 + (at_x * 8 + at_z) * 2 + at_y // 2

    return [
        (place(c, i, j, l), place(c ^ core, i ^ x, j ^ y, l ^ z))
        for c in range(2)
        for i in range(4)
        for j in range(4)
        for l in range(8)
    ]


def swapped(value, **bits):
    return lax.ppermute(value, ("dp", "space"), partners(**bits))


def added(values):
    return (values[0] + values[1]) + (values[2] + values[3])


def summed_among(value, steps):
    return added([value] + [swapped(value, **bits) for bits in steps])


ALONG_X = [dict(x=1), dict(x=2), dict(x=3)]
ALONG_Y = [dict(y=1), dict(y=2), dict(y=3)]
ALONG_Z = [dict(z=1), dict(z=2), dict(z=3)]
CORE_AND_Z = [dict(core=1), dict(z=6), dict(core=1, z=6)]


def body(inputs, cotangent, occupancy, neighbours, weight, error_in, q_start):
    field, gradient = inputs[0], cotangent[0]
    occupied, slots = in_hbm(occupancy[0]), in_hbm(neighbours[0])
    weight = weight.reshape(3, 3, 3, 256, 256)
    up, down = brick_faces(field, gradient, occupied)
    lower, upper = shifted(up, 1), shifted(down, -1)
    fixed = (slots, in_hbm(field), in_hbm(gradient), occupied, in_hbm(q_start.T), in_hbm(error_in.reshape(3, 3, 3, 256, 256)))
    kept, sent, mine, other = local_gradient((0,), *fixed)
    kept, sent, mine, other = local_gradient(
        (-1, 1), *fixed, lower, upper, in_vmem(kept), in_vmem(sent), mine, other
    )

    part = mine + swapped(other, core=1)
    part, travelling = lax.optimization_barrier((part, sent))
    arrived = [swapped(part[k], x=k) for k in (1, 2, 3)]
    partner = swapped(travelling, core=1)
    total = input_gradient(0, False, slots, gradient, occupied, weight, tie=part)
    part, total = lax.optimization_barrier((added([part[0]] + arrived), total))
    part = part.reshape(4, 7, 8, 128)
    part = added([part[0]] + [swapped(part[k], y=k) for k in (1, 2, 3)])
    part = summed_among(part, ALONG_Z)
    arrived = swapped(part, z=6)
    total = input_gradient(-1, False, slots, gradient, occupied, weight, upper, total, tie=part)
    part, total = lax.optimization_barrier((part + arrived, total))
    part = jnp.concatenate([part] + [swapped(part, **bits) for bits in ALONG_Y], axis=0)
    arrived = [swapped(part, **bits) for bits in ALONG_X]
    input_grad = input_gradient(1, True, slots, gradient, occupied, weight, lower, total, tie=part)
    mine, partner, input_grad = lax.optimization_barrier(
        (jnp.stack([part] + arrived, axis=0), partner, input_grad)
    )

    other = swapped(mine, core=1)
    right = right_product(mine, kept, partner)
    right, other = lax.optimization_barrier((summed_among(right, CORE_AND_Z), other))
    arrived = [swapped(right, **bits) for bits in ALONG_X]
    halves = half_inverse(mine, other)
    right, *halves = lax.optimization_barrier((added([right] + arrived), *halves))
    arrived = [swapped(right, **bits) for bits in ALONG_Y]
    inverse = whole_inverse(*halves, tie=right)
    right, inverse = lax.optimization_barrier((added([right] + arrived), inverse))
    right = summed_among(right, ALONG_Z)
    new_error, q_rows = remaining_error(mine, other, kept, sent, right, inverse)
    return (input_grad[None], q_rows.T, new_error.reshape(1, 1, 6912, 256))


def solution(mesh):
    in_specs = (
        P("dp", "space", None, None),
        P("dp", "space", None, None),
        P("dp", "space", None),
        P("dp", "space", None),
        P(),
        P("dp", "space", None, None),
        P(),
    )
    out_specs = (P("dp", "space", None, None), P(), P("dp", "space", None, None))
    return jax.shard_map(body, mesh=mesh, in_specs=in_specs, out_specs=out_specs, check_vma=False)
```

```python
import functools

import jax
import jax.numpy as jnp
from jax import lax
from jax.experimental import pallas as pl
from jax.experimental.pallas import tpu as pltpu
from jax.sharding import PartitionSpec as P

EDGE = 8
PLANE = EDGE * EDGE
F32 = jnp.float32
BF16 = jnp.bfloat16
NT = (((1,), (1,)), ((), ()))
NN = (((1,), (0,)), ((), ()))
TN = (((0,), (0,)), ((), ()))
STEPS = (-1, 0, 1)
MIB = 1024 * 1024


def split(value):
    high = value.astype(BF16)
    low = (value - high.astype(F32)).astype(BF16)
    return high, low


def source_rows(slots, step_x, step_y, step_z, along):
    shape = (128, 1) if along == 0 else (1, 128)
    place = lax.broadcasted_iota(jnp.int32, shape, along)
    brick = place // PLANE
    y = (place // EDGE) % EDGE + step_y
    z = place % EDGE + step_z
    wrapped_y = y % EDGE
    wrapped_z = z % EDGE
    rows = jnp.full(shape, -1, jnp.int32)
    for side_y in sorted({0, step_y}):
        in_y = (y < 0) if side_y < 0 else (y >= EDGE) if side_y > 0 else (y >= 0) & (y < EDGE)
        for side_z in sorted({0, step_z}):
            in_z = (z < 0) if side_z < 0 else (z >= EDGE) if side_z > 0 else (z >= 0) & (z < EDGE)
            if side_z == 0:
                offset = wrapped_y * EDGE + wrapped_z
                first, stride = 0, PLANE
            else:
                offset = wrapped_y
                first, stride = (128 if side_z < 0 else 144), EDGE
            for which in (0, 1):
                slot = slots[which, (step_x + 1) * 9 + (side_y + 1) * 3 + side_z + 1]
                if side_z:
                    end = 0 if side_z < 0 else lax.axis_size("space") - 1
                    slot = jnp.where(lax.axis_index("space") == end, -1, slot)
                base = jnp.where(slot < 0, -4096, slot * stride + first)
                rows = jnp.where(in_y & in_z & (brick == which), base + offset, rows)
    return rows


def one_hot(rows, along, depth):
    shape = (128, depth) if along == 0 else (depth, 128)
    places = lax.broadcasted_iota(jnp.int32, shape, 1 - along)
    return jnp.where(places == rows, 1.0, 0.0).astype(BF16)


def voxel_mask(occupancy):
    padded = jnp.concatenate([occupancy[...].astype(F32), jnp.zeros((6, 512), F32)], axis=0)
    return padded.T


def own_plane(field, mask, plane):
    rows = slice(plane * PLANE, (plane + 1) * PLANE)
    return jnp.concatenate([field[b, rows, :] * mask[rows, b : b + 1] for b in (0, 1)], axis=0)


def with_faces(own, lower, upper, plane):
    rest = jnp.zeros((96, own.shape[1]), BF16)
    return jnp.concatenate([own, lower[0, plane], upper[0, plane], rest], axis=0)


def coordinates():
    dp, space = lax.axis_index("dp"), lax.axis_index("space")
    return dp % 2, space // 16, (space % 2) * 2 + dp // 2, (space // 2) % 8


def place_of(tap, y):
    return ((tap // 7) ^ y) * 7 + tap % 7


def put_factor(mine, other, tap, value):
    core, x, y, _ = coordinates()
    place = place_of(tap, y)
    halves = value[:, :128], value[:, 128:]
    kept = jnp.where(core == 0, halves[0], halves[1])
    sent = jnp.where(core == 0, halves[1], halves[0])
    for block in range(4):
        rows = slice(block * 8, block * 8 + 8)
        mine[block ^ x, place] = kept[rows]
        other[block ^ x, place] = sent[rows]


def get_factor(mine, other, tap):
    core, x, y, _ = coordinates()
    place = place_of(tap, y)
    own = jnp.concatenate([mine[block ^ x, place] for block in range(4)], axis=0)
    rest = jnp.concatenate([other[block ^ x, place] for block in range(4)], axis=0)
    both = jnp.concatenate([jnp.where(core == 0, own, rest), jnp.where(core == 0, rest, own)], axis=1)
    return both * (1.0 / 256.0)


def whole(*shape):
    return pl.BlockSpec(shape, lambda *step: (0,) * len(shape))


def faces_kernel(field, cotangent, occupancy, up, down):
    mask = voxel_mask(occupancy).astype(BF16)
    row = lax.broadcasted_iota(jnp.int32, (32, 128), 0)
    place = lax.broadcasted_iota(jnp.int32, (32, 128), 1)
    wanted = jnp.where(row < 16, row * EDGE + EDGE - 1, (row - 16) * EDGE)
    picks = jnp.where(place == wanted, 1.0, 0.0).astype(BF16)
    for which, source in enumerate((field, cotangent)):
        for plane in range(EDGE):
            found = lax.dot_general(picks, own_plane(source, mask, plane), NN, preferred_element_type=F32)
            up[which, plane] = found[:16].astype(BF16)
            down[which, plane] = found[16:].astype(BF16)


def brick_faces(field, cotangent, occupancy):
    shape = jax.ShapeDtypeStruct((2, EDGE, 16, 256), BF16)
    return pl.pallas_call(faces_kernel, out_shape=[shape, shape], compiler_params=SMALL, name="brick_faces")(
        in_hbm(field), in_hbm(cotangent), occupancy
    )


def gradient_kernel(sides, width, *refs):
    faces = sides != (0,)
    slots, field, cotangent, occupancy, start, error = refs[:6]
    refs = refs[6:]
    if faces:
        lower, upper, _, _, mine_before, other_before = refs[:6]
        refs = refs[6:]
    kept, sent, mine, other, views, sources, own, start_parts = refs
    core = coordinates()[0]
    step = pl.program_id(0)
    depth = 256 if faces else 128
    shares = 3 // width
    side = step // shares * 2 - 1 if faces else 0

    @pl.when(step == 0)
    def _():
        mask = voxel_mask(occupancy).astype(BF16)
        high, low = split(start[...].T)
        none = jnp.zeros((256, 32), BF16)
        start_parts[0:256, :] = jnp.concatenate([high, low, none, none], axis=1)
        start_parts[256:512, :] = jnp.concatenate([high, none, none, none], axis=1)
        start_parts[512:768, :] = jnp.concatenate([none, none, high, low], axis=1)
        start_parts[768:1024, :] = jnp.concatenate([none, none, high, none], axis=1)
        for plane in range(EDGE):
            own[plane * 128 : (plane + 1) * 128, :] = own_plane(cotangent, mask, plane)
            source = own_plane(field, mask, plane)
            if faces:
                source = with_faces(source, lower, upper, plane)
            sources[plane * 256 : (plane + 1) * 256, :] = source.T
        if faces:
            mine[...] = mine_before[...]
            other[...] = other_before[...]
        else:
            put_factor(mine, other, 27, jnp.zeros((32, 256), F32))

    def gather(groups):
        for first in range(0, len(groups), 2):
            pair = groups[first : first + 2]
            for step_x, left, where in (
                (-1, sources[7 * 256 : 8 * 256, :], 0),
                (0, sources[...], 1),
                (1, sources[0:256, :], 9),
            ):
                picks = jnp.concatenate(
                    [one_hot(source_rows(slots, step_x, y, z, 1), 1, depth) for y, z in pair], axis=1
                )
                found = lax.dot_general(left, picks, NN, preferred_element_type=F32).astype(BF16)
                for member in range(len(pair)):
                    for block in range(left.shape[0] // 256):
                        views[first + member, :, (where + block) * 128 : (where + block + 1) * 128] = found[
                            block * 256 : (block + 1) * 256, member * 128 : (member + 1) * 128
                        ]

    for index in range(len(sides) * shares):
        chosen = STEPS[index % shares * width : index % shares * width + width]

        @pl.when(step == index)
        def _():
            gather([(y, sides[index // shares]) for y in chosen])

    parts = []
    for member in range(width):
        columns = jnp.concatenate([views[member, :, k * 128 : k * 128 + 1024] for k in range(3)], axis=0)
        total = lax.dot_general(columns, own[...], NN, preferred_element_type=F32)
        total = total + error[:, member, 0].astype(F32).reshape(768, 256)
        halves = total.reshape(3, 2, 128, 256)
        kept[0, :, member] = jnp.where(core == 0, halves[:, 0], halves[:, 1])
        sent[0, :, member] = jnp.where(core == 0, halves[:, 1], halves[:, 0])
        high, low = split(total)
        for tap_x in range(3):
            rows = slice(tap_x * 256, tap_x * 256 + 256)
            parts.append((tap_x, member, [high[rows], low[rows]]))
    for first in range(0, 3 * width, 2):
        chosen = parts[first : first + 2]
        left = jnp.concatenate([part for _, _, both in chosen for part in both], axis=1)
        made = lax.dot_general(left, start_parts[0 : left.shape[1], :], NN, preferred_element_type=F32).T
        for slot, (tap_x, member, _) in enumerate(chosen):
            step_y = step % shares * width + member
            rows = made[slot * 64 : slot * 64 + 64]
            put_factor(mine, other, tap_x * 9 + step_y * 3 + side + 1, rows[:32] + rows[32:])


def local_gradient(sides, slots, field, cotangent, occupancy, start, error, *more):
    faces = sides != (0,)
    width = FACES_WIDTH if faces else OWN_WIDTH
    shares = 3 // width

    def which(step):
        return step // shares * 2 if faces else 1

    piece = whole(4, 28, 8, 128)
    face = whole(1, EDGE, 16, 256)
    anywhere = pl.BlockSpec(memory_space=pl.ANY)
    half = pl.BlockSpec((1, 3, width, 128, 256), lambda step: (which(step), 0, step % shares, 0, 0))
    in_specs = [
        pl.BlockSpec(memory_space=pltpu.SMEM),
        whole(2, 512, 256),
        whole(2, 512, 256),
        whole(2, 512),
        whole(32, 256),
        pl.BlockSpec((3, width, 1, 256, 256), lambda step: (0, step % shares, which(step), 0, 0)),
    ]
    if faces:
        in_specs += [face, face, anywhere, anywhere, piece, piece]
    depth = 256 if faces else 128
    return pl.pallas_call(
        functools.partial(gradient_kernel, sides, width),
        grid=(len(sides) * shares,),
        in_specs=in_specs,
        out_specs=[half, half, piece, piece],
        out_shape=[
            HALF,
            HALF,
            jax.ShapeDtypeStruct((4, 28, 8, 128), F32),
            jax.ShapeDtypeStruct((4, 28, 8, 128), F32),
        ],
        input_output_aliases={8: 0, 9: 1} if faces else {},
        scratch_shapes=[
            pltpu.VMEM((width, 256, 1280), BF16),
            pltpu.VMEM((2048, depth), BF16),
            pltpu.VMEM((1024, 256), BF16),
            pltpu.VMEM((1024, 128), BF16),
        ],
        compiler_params=pltpu.CompilerParams(vmem_limit_bytes=GRAD_LIMIT),
        cost_estimate=pl.CostEstimate(
            flops=len(sides) * 2 * 10**9, bytes_accessed=len(sides) * 4 * 10**6, transcendentals=0
        ),
        name="gradient_with_faces" if faces else "gradient_own",
    )(slots, field, cotangent, occupancy, start, error, *more)


def input_kernel(side, last, *refs):
    slots, cotangent, occupancy, weight = refs[:4]
    refs = refs[4:]
    if side:
        face, total_before = refs[:2]
        refs = refs[2:]
    result, views, total = refs[-3:]
    step = pl.program_id(0)

    @pl.when(step == 0)
    def _():
        mask = voxel_mask(occupancy).astype(BF16)
        sources = [own_plane(cotangent, mask, plane) for plane in range(EDGE)]
        if side:
            sources = [with_faces(own, face, face, plane) for plane, own in enumerate(sources)]
        for index, y in enumerate(STEPS):
            picks = [one_hot(source_rows(slots, x, y, -side, 0), 0, 256 if side else 128) for x in STEPS]
            for plane in range(-1, EDGE + 1):
                which = 0 if plane < 0 else 2 if plane >= EDGE else 1
                found = lax.dot_general(picks[which], sources[plane % EDGE], NN, preferred_element_type=F32)
                views[index, (plane + 1) * 128 : (plane + 2) * 128, :] = found.astype(BF16)
        total[...] = total_before[...] if side else jnp.zeros_like(total)

    columns = jnp.concatenate(
        [views[2 - step, (2 - tap_x) * 128 : (2 - tap_x) * 128 + 1024, :] for tap_x in range(3)], axis=1
    )
    weights = jnp.concatenate([weight[tap_x, 0, 0] for tap_x in range(3)], axis=1)
    total[...] += lax.dot_general(columns, weights, NT, preferred_element_type=F32)

    @pl.when(step == 2)
    def _():
        if not last:
            result[...] = total[...]
            return
        mask = voxel_mask(occupancy)
        for plane in range(EDGE):
            for brick in (0, 1):
                first = (2 * plane + brick) * PLANE
                rows = slice(plane * PLANE, (plane + 1) * PLANE)
                kept = total[first : first + PLANE, :] * mask[rows, brick : brick + 1]
                result[brick, rows, :] = kept.astype(BF16)


def input_gradient(side, last, slots, cotangent, occupancy, weight, *more, tie=None):
    in_specs = [
        pl.BlockSpec(memory_space=pltpu.SMEM),
        whole(2, 512, 256),
        whole(2, 512),
        pl.BlockSpec((3, 1, 1, 256, 256), lambda step: (0, step, side + 1, 0, 0)),
    ]
    if side:
        in_specs += [pl.BlockSpec((1, EDGE, 16, 256), lambda step: (1, 0, 0, 0)), whole(1024, 256)]
    if tie is not None:
        in_specs += [pl.BlockSpec(memory_space=pl.ANY)]
        more += (tie,)
    if last:
        shape, spec = jax.ShapeDtypeStruct((2, 512, 256), BF16), whole(2, 512, 256)
    else:
        shape, spec = jax.ShapeDtypeStruct((1024, 256), F32), whole(1024, 256)
    return pl.pallas_call(
        functools.partial(input_kernel, side, last),
        grid=(3,),
        in_specs=in_specs,
        out_specs=spec,
        out_shape=shape,
        scratch_shapes=[pltpu.VMEM((3, 1280, 256), BF16), pltpu.VMEM((1024, 256), F32)],
        compiler_params=pltpu.CompilerParams(vmem_limit_bytes=INPUT_LIMIT),
        cost_estimate=pl.CostEstimate(flops=2 * 10**9, bytes_accessed=4 * 10**6, transcendentals=0),
        name=("input_own", "input_above", "input_below")[side],
    )(slots, cotangent, occupancy, weight, *more)


def taps_left(mine, other, step_x, step_y):
    first = step_x * 9 + step_y * 3
    return jnp.concatenate([get_factor(mine, other, first + k) for k in range(3)], axis=1)


def right_kernel(mine, kept, partner, right):
    step = pl.program_id(0)
    _, x, y, _ = coordinates()

    @pl.when(step == 0)
    def _():
        right[...] = jnp.zeros_like(right)

    total = jnp.zeros((32, 256), F32)
    for step_y in range(3):
        columns = []
        for step_z in range(3):
            place = place_of(step * 9 + step_y * 3 + step_z, y)
            columns.append(jnp.concatenate([mine[block ^ x, place] for block in range(4)], axis=0))
        left_high, left_low = split(jnp.concatenate(columns, axis=1) * (1.0 / 256.0))
        high, low = split((kept[:, 0, step_y] + partner[:, 0, step_y]).reshape(384, 256))
        both = lax.dot_general(
            jnp.concatenate([left_high, left_low], axis=0), high, NN, preferred_element_type=F32
        )
        total += both[0:32] + both[32:64]
        total += lax.dot_general(left_high, low, NN, preferred_element_type=F32)
    right[...] += total


def along_x(*shape):
    return pl.BlockSpec((3, 1, 3) + shape, lambda step: (0, step, 0, 0, 0))


def right_product(mine, kept, partner):
    return pl.pallas_call(
        right_kernel,
        grid=(3,),
        in_specs=[whole(4, 28, 8, 128), along_x(128, 256), along_x(128, 256)],
        out_specs=whole(32, 256),
        out_shape=jax.ShapeDtypeStruct((32, 256), F32),
        compiler_params=pltpu.CompilerParams(vmem_limit_bytes=LATE_LIMIT),
        name="right_product",
    )(mine, in_vmem(kept), in_vmem(partner))


def eliminate(first, work, made):
    places = lax.broadcasted_iota(jnp.int32, (32, 1), 0)
    for step in range(first, first + 16):
        scale = 1.0 / jnp.sqrt(work[step : step + 1, step : step + 1])
        work_row = work[step : step + 1, :] * scale
        made_row = made[step : step + 1, :] * scale
        column = work[:, step : step + 1] * scale
        later = jnp.where(places > step, column, 0.0)
        here = places == step
        work = jnp.where(here, work_row, work - later * work_row)
        made = jnp.where(here, made_row, made - later * made_row)
    return work, made


def first_half_kernel(mine, other, work, made):
    gram = jnp.zeros((32, 32), F32)
    for step in range(9):
        left = jnp.concatenate([get_factor(mine, other, step * 3 + tap) for tap in range(3)], axis=1)
        gram += lax.dot_general(left, left, NT, precision=lax.Precision.HIGHEST, preferred_element_type=F32)
    row = lax.broadcasted_iota(jnp.int32, (32, 32), 0)
    column = lax.broadcasted_iota(jnp.int32, (32, 32), 1)
    work[...], made[...] = eliminate(0, gram, jnp.where(row == column, 1.0, 0.0).astype(F32))


def second_half_kernel(work, made, inverse):
    inverse[...] = eliminate(16, work[...], made[...])[1]


SQUARE = jax.ShapeDtypeStruct((32, 32), F32)


def half_inverse(mine, other):
    return pl.pallas_call(first_half_kernel, out_shape=[SQUARE, SQUARE], compiler_params=SMALL, name="half_inverse")(
        mine, other
    )


def whole_inverse(work, made, tie=None):
    def kernel(work, made, *refs):
        second_half_kernel(work, made, refs[-1])

    more = () if tie is None else (tie,)
    vmem = pl.BlockSpec(memory_space=pltpu.VMEM)
    return pl.pallas_call(
        kernel,
        in_specs=[vmem, vmem] + [pl.BlockSpec(memory_space=pl.ANY)] * len(more),
        out_specs=vmem,
        out_shape=SQUARE,
        compiler_params=SMALL,
        name="whole_inverse",
    )(work, made, *more)


def error_kernel(mine, other, kept, sent, right, inverse, new_error, q_rows, basis):
    step = pl.program_id(0)

    @pl.when(step == 0)
    def _():
        rows = lax.dot_general(
            inverse[...], right[...], NN, precision=lax.Precision.HIGHEST, preferred_element_type=F32
        ) * (1.0 / 256.0)
        q_rows[...] = rows
        back = lax.dot_general(
            inverse[...].T, rows, NN, precision=lax.Precision.HIGHEST, preferred_element_type=F32
        )
        high, low = split(back)
        basis[0:32, :] = high
        basis[32:64, :] = high
        basis[64:96, :] = low
        basis[96:128, :] = jnp.zeros((32, 256), BF16)

    core = coordinates()[0]
    for step_y in range(3):
        high, low = split(taps_left(mine, other, step, step_y))
        left = jnp.concatenate([high, low, high, jnp.zeros((32, 768), BF16)], axis=0)
        product = lax.dot_general(left, basis[...], TN, preferred_element_type=F32)
        product = product.reshape(3, 2, 128, 256)
        own, rest = kept[:, 0, step_y], sent[:, 0, step_y]
        halves = jnp.where(core == 0, own, rest), jnp.where(core == 0, rest, own)
        for half in (0, 1):
            rows = slice(half * 128, half * 128 + 128)
            new_error[0, step_y, :, rows, :] = (halves[half] - product[:, half]).astype(BF16)


def remaining_error(mine, other, kept, sent, right, inverse):
    return pl.pallas_call(
        error_kernel,
        grid=(3,),
        in_specs=[
            whole(4, 28, 8, 128),
            whole(4, 28, 8, 128),
            along_x(128, 256),
            along_x(128, 256),
            whole(32, 256),
            whole(32, 32),
        ],
        out_specs=[pl.BlockSpec((1, 3, 3, 256, 256), lambda step: (step, 0, 0, 0, 0)), whole(32, 256)],
        out_shape=[jax.ShapeDtypeStruct((3, 3, 3, 256, 256), BF16), jax.ShapeDtypeStruct((32, 256), F32)],
        scratch_shapes=[pltpu.VMEM((128, 256), BF16)],
        compiler_params=pltpu.CompilerParams(vmem_limit_bytes=LATE_LIMIT),
        name="remaining_error",
    )(mine, other, in_vmem(kept), in_vmem(sent), right, inverse)


HALF = pltpu.VMEM((3, 3, 3, 128, 256), F32)
GRAD_LIMIT = 32 * MIB
OWN_WIDTH = 3
FACES_WIDTH = 3
INPUT_LIMIT = 24 * MIB
LATE_LIMIT = 24 * MIB
SMALL = pltpu.CompilerParams(vmem_limit_bytes=12 * MIB)


def in_vmem(value):
    return pltpu.with_memory_space_constraint(value, pltpu.VMEM)


def in_hbm(value):
    return pltpu.with_memory_space_constraint(value, pltpu.HBM)


def shifted(value, by):
    devices = lax.axis_size("space")
    return lax.ppermute(value, "space", [(i, (i + by) % devices) for i in range(devices)])


def partners(core=0, x=0, y=0, z=0):
    def place(at_core, at_x, at_y, at_z):
        return (at_y % 2 * 2 + at_core) * 64 + (at_x * 8 + at_z) * 2 + at_y // 2

    return [
        (place(c, i, j, l), place(c ^ core, i ^ x, j ^ y, l ^ z))
        for c in range(2)
        for i in range(4)
        for j in range(4)
        for l in range(8)
    ]


def swapped(value, **bits):
    return lax.ppermute(value, ("dp", "space"), partners(**bits))


def added(values):
    return (values[0] + values[1]) + (values[2] + values[3])


def summed_among(value, steps):
    return added([value] + [swapped(value, **bits) for bits in steps])


ALONG_X = [dict(x=1), dict(x=2), dict(x=3)]
ALONG_Y = [dict(y=1), dict(y=2), dict(y=3)]
ALONG_Z = [dict(z=1), dict(z=2), dict(z=3)]
CORE_AND_Z = [dict(core=1), dict(z=6), dict(core=1, z=6)]


def body(inputs, cotangent, occupancy, neighbours, weight, error_in, q_start):
    field, gradient = inputs[0], cotangent[0]
    occupied, slots = in_hbm(occupancy[0]), in_hbm(neighbours[0])
    weight = weight.reshape(3, 3, 3, 256, 256)
    up, down = brick_faces(field, gradient, occupied)
    lower, upper = shifted(up, 1), shifted(down, -1)
    fixed = (slots, in_hbm(field), in_hbm(gradient), occupied, in_hbm(q_start.T), in_hbm(error_in.reshape(3, 3, 3, 256, 256)))
    kept, sent, mine, other = local_gradient((0,), *fixed)
    kept, sent, mine, other = local_gradient(
        (-1, 1), *fixed, lower, upper, in_vmem(kept), in_vmem(sent), mine, other
    )

    part = mine + swapped(other, core=1)
    part, travelling = lax.optimization_barrier((part, sent))
    arrived = [swapped(part[k], x=k) for k in (1, 2, 3)]
    partner = swapped(travelling, core=1)
    total = input_gradient(0, False, slots, gradient, occupied, weight, tie=part)
    part, total = lax.optimization_barrier((added([part[0]] + arrived), total))
    part = part.reshape(4, 7, 8, 128)
    part = added([part[0]] + [swapped(part[k], y=k) for k in (1, 2, 3)])
    part = summed_among(part, ALONG_Z)
    arrived = swapped(part, z=6)
    total = input_gradient(-1, False, slots, gradient, occupied, weight, upper, total, tie=part)
    part, total = lax.optimization_barrier((part + arrived, total))
    part = jnp.concatenate([part] + [swapped(part, **bits) for bits in ALONG_Y], axis=0)
    arrived = [swapped(part, **bits) for bits in ALONG_X]
    input_grad = input_gradient(1, True, slots, gradient, occupied, weight, lower, total, tie=part)
    mine, partner, input_grad = lax.optimization_barrier(
        (jnp.stack([part] + arrived, axis=0), partner, input_grad)
    )

    right = right_product(mine, kept, partner)
    right, mine = lax.optimization_barrier((summed_among(right, CORE_AND_Z), mine))
    arrived = [swapped(right, **bits) for bits in ALONG_Z]
    other = swapped(mine, core=1)
    right, other = lax.optimization_barrier((added([right] + arrived), other))
    arrived = [swapped(right, **bits) for bits in ALONG_X]
    halves = half_inverse(mine, other)
    right, *halves = lax.optimization_barrier((added([right] + arrived), *halves))
    arrived = [swapped(right, **bits) for bits in ALONG_Y]
    inverse = whole_inverse(*halves, tie=right)
    right = added([right] + arrived)
    new_error, q_rows = remaining_error(mine, other, kept, sent, right, inverse)
    return (input_grad[None], q_rows.T, new_error.reshape(1, 1, 6912, 256))


def solution(mesh):
    in_specs = (
        P("dp", "space", None, None),
        P("dp", "space", None, None),
        P("dp", "space", None),
        P("dp", "space", None),
        P(),
        P("dp", "space", None, None),
        P(),
    )
    out_specs = (P("dp", "space", None, None), P(), P("dp", "space", None, None))
    return jax.shard_map(body, mesh=mesh, in_specs=in_specs, out_specs=out_specs, check_vma=False)
```
